32 devices in a mesh: dp: 8 (over y, x, core), tensor: 4 (over z).
Axes of the slice: x: 2, y: 2, z: 4, core: 2. Of those that a mesh axis runs over, the one named last changes fastest.
Arguments:
- tokens: bfloat16 [8192, 2048], P('dp'), may hold values from -6 to 6
- cotangent: bfloat16 [8192, 2048], P('dp'), may hold values from -6 to 6
- segments: int32 [8, 1024], P('dp'), may hold values from 0 to 5, never falling along the last dimension, each value on 1 to 512 neighbouring positions
- norm_gains: bfloat16 [2, 2048], replicated, may hold values from 0.5 to 1.5
- w_qkv: bfloat16 [2048, 8, 384], P(None, 'tensor'), may hold values from -0.125 to 0.125
- qkv_down: bfloat16 [3, 8, 2048], replicated, may hold values from -0.125 to 0.125
- query_key_value_up: bfloat16 [8, 8, 384], P(None, 'tensor'), may hold values from -1 to 1
- feature_maps: bfloat16 [8, 64, 320], P('tensor'), may hold values from -0.75 to 0.75
- w_out: bfloat16 [2048, 2048], P('tensor'), may hold values from -1 to 1
- o_down: bfloat16 [8, 8, 256], P(None, 'tensor'), may hold values from -0.125 to 0.125
- o_up: bfloat16 [8, 2048], replicated, may hold values from -6 to 6
- w_gate_up: bfloat16 [2048, 2, 8192], P(None, None, 'tensor'), may hold values from -0.125 to 0.125
- w_down: bfloat16 [8192, 2048], P('tensor'), may hold values from -0.0625 to 0.0625
Outputs:
- output: bfloat16 [8192, 2048], P(('dp', 'tensor'))
- grad_input: bfloat16 [8192, 2048], P(('dp', 'tensor'))
- grad_norm_gains: float32 [2, 2048], P(None, ('dp', 'tensor'))
- grad_w_qkv: float32 [2048, 8, 384], P('dp', 'tensor')
- grad_qkv_down: float32 [3, 8, 2048], P(None, None, ('dp', 'tensor'))
- grad_qkv_up: float32 [8, 8, 384], P(None, 'tensor', 'dp')
- grad_feature_maps: float32 [8, 64, 320], P('tensor', None, 'dp')
- grad_w_out: float32 [2048, 2048], P('tensor', 'dp')
- grad_o_down: float32 [8, 8, 256], P(None, 'tensor', 'dp')
- grad_o_up: float32 [8, 2048], P(None, ('dp', 'tensor'))
- grad_w_gate_up: float32 [2048, 2, 8192], P('dp', None, 'tensor')
- grad_w_down: float32 [8192, 2048], P('tensor', 'dp')
The draws below stay inside these ranges and needn't reach their ends.
Inputs may be any that keep to these rules, and one draw needn't show every extreme that they name: `segments`: within each packed sequence the numbers never fall, so that each document is one run of positions; no document is longer than 512 positions, and some document reaches that length.
All inputs are finite; a program needn't handle non-finite values.
Results may differ from the reference program's by a relative error of at most 0.024.
Values may be sent and summed in bfloat16 or wider, within the bound.
A program may use at most 320 MiB of HBM per device.

```python
import math
import jax
import jax.numpy as jnp
import numpy as np
from jax import lax

D = 2048
HEADS = 32
KVH = 8
HEAD_SIZE = 64
FF = 8192
R = 8
WINDOW = 64
SEQ_LEN = 1024
QW = 2048
GROUP_W = 256
QKV_W = 384
FMW = 320
SEQ_TOTAL = 8
TOKENS = 8192


def shard_levels(key, extent, shards, low, largest):
    loudness = 1.0
    for dim, blocks in shards:
        draws = jax.random.uniform(jax.random.fold_in(jax.random.fold_in(key, 6), dim), (blocks,), jnp.float32, low / len(shards), largest / len(shards))
        loudness = loudness * jnp.repeat(jnp.exp(draws), extent[dim] // blocks).reshape((-1,) + (1,) * (len(extent) - 1 - dim))
    return loudness


def length_profile(count, total, bound, skew):
    loads = [(1 << 20) // math.isqrt(rank ** skew) + 1 for rank in range(2, count + 1)]
    spare, counts = total - bound - (count - 1), [1] * (count - 1)
    while spare > 0:
        free = [i for i in range(count - 1) if counts[i] < bound]
        mass, budget = sum([loads[i] for i in free]), spare
        for i in free:
            addition = min(bound - counts[i], max(1, budget * loads[i] // mass), spare)
            counts[i] = counts[i] + addition
            spare = spare - addition
    return np.array([bound] + counts)


def ragged(own_key, count, total, limit, lean):
    if count == 2:
        one = jax.random.randint(own_key, (), max(1, total - limit), min(limit, total - 1) + 1)
        return jnp.stack([one, total - one])
    tallies = jnp.asarray(length_profile(count, total, limit, lean), jnp.int32)
    pairs = (count - 1) // 2
    giver, taker = tallies[1:1 + 2 * pairs:2], tallies[2:2 + 2 * pairs:2]
    margin = jnp.minimum(giver - 1, limit - taker)
    shifted = jax.random.randint(jax.random.fold_in(own_key, 1), (pairs,), 0, 1 << 20) % (margin + 1)
    tallies = tallies.at[1:1 + 2 * pairs:2].set(giver - shifted).at[2:2 + 2 * pairs:2].set(taker + shifted)
    return tallies[jax.random.permutation(jax.random.fold_in(own_key, 2), count)]


def gaussian(own_key, extent, scale, limit, pieces=(), kind=jnp.bfloat16):
    entries = scale * jax.random.normal(own_key, extent, jnp.float32)
    if pieces:
        entries = entries * shard_levels(own_key, extent, pieces, -0.22, 0.18)
    return jnp.clip(entries, -limit, limit).astype(kind)


def setup_inputs(seed: int = 0) -> dict:
    seeds = jax.random.split(jax.random.key(seed), 14)
    return {
        "tokens": gaussian(seeds[0], (TOKENS, D), 1.0, 6.0, ((0, 8),)),
        "cotangent": gaussian(seeds[1], (TOKENS, D), 1.0, 6.0, ((0, 8),)),
        "segments": jax.vmap(lambda own: jnp.searchsorted(jnp.cumsum(ragged(own, 6, SEQ_LEN, SEQ_LEN // 2, 2)), jnp.arange(SEQ_LEN), side="right"))(jax.random.split(seeds[2], SEQ_TOTAL)).reshape((SEQ_TOTAL, SEQ_LEN)).astype(jnp.int32),
        "norm_gains": jnp.clip(1.0 + 0.1 * jax.random.normal(seeds[3], (2, D), jnp.float32), 0.5, 1.5).astype(jnp.bfloat16),
        "w_qkv": gaussian(seeds[4], (D, KVH, QKV_W), D ** -0.5, 0.125, ((1, 4),)),
        "qkv_down": gaussian(seeds[5], (3, R, D), D ** -0.5, 0.125),
        "query_key_value_up": gaussian(seeds[6], (R, KVH, QKV_W), (4 * R) ** -0.5, 1.0, ((1, 4),)),
        "feature_maps": gaussian(seeds[7], (KVH, HEAD_SIZE, FMW), HEAD_SIZE ** -0.5, 0.75, ((0, 4),)),
        "w_out": gaussian(seeds[8], (QW, D), (QW // 64) ** -0.5, 1.0, ((0, 4),)),
        "o_down": gaussian(seeds[9], (R, KVH, GROUP_W), QW ** -0.5, 0.125, ((1, 4),)),
        "o_up": gaussian(seeds[10], (R, D), 1 ** -0.5, 6.0),
        "w_gate_up": gaussian(seeds[11], (D, 2, FF), D ** -0.5, 0.125, ((2, 4),)),
        "w_down": gaussian(seeds[12], (FF, D), FF ** -0.5, 0.0625, ((0, 4),)),
    }


highest = lax.Precision.HIGHEST
epsilon = 1e-05
rope_base = 500000.0

@jax.custom_vjp
def low(v):
    return lax.optimization_barrier(v.astype(jnp.bfloat16)).astype(jnp.float32)

@jax.custom_vjp
def lowrank_backward(v):
    return v

def low_keep(v):
    return (low(v), None)

def low_pass(kept, grad):
    return (grad,)

def back_keep(v):
    return (v, None)

def back_low(kept, grad):
    return (low(grad),)
low.defvjp(low_keep, low_pass)
lowrank_backward.defvjp(back_keep, back_low)

def rotary_tables(length, head_span_width):
    half_width = head_span_width // 2
    frequency = rope_base ** (-(jnp.arange(half_width, dtype=jnp.float32) * 2.0) / head_span_width)
    angles = jnp.arange(length, dtype=jnp.float32)[:, None] * frequency[None, :]
    return (jnp.cos(angles), jnp.sin(angles))

def rotate(values, cosines, sine_values):
    half_width = values.shape[-1] // 2
    leading = values[..., :half_width]
    trailing = values[..., half_width:]
    return jnp.concatenate([leading * cosines - trailing * sine_values, trailing * cosines + leading * sine_values], axis=-1)

def hedgehog(logits):
    return jnp.concatenate([jax.nn.softmax(logits, axis=-1), jax.nn.softmax(-logits, axis=-1)], axis=-1)

def rms_norm(values, gain_row):
    inverse = lax.rsqrt(lax.optimization_barrier(jnp.mean(values * values, axis=-1, keepdims=True)) + epsilon)
    return values * inverse * gain_row

def adapter_columns(lowrank_update, up_maps_float, query_span_width, head_span_width):
    upper_key = query_span_width + head_span_width
    return jnp.concatenate([jnp.einsum('tr,rkc->tkc', lowrank_update[:, 0], up_maps_float[:, :, :query_span_width], precision=highest), jnp.einsum('tr,rkc->tkc', lowrank_update[:, 1], up_maps_float[:, :, query_span_width:upper_key], precision=highest), jnp.einsum('tr,rkc->tkc', lowrank_update[:, 2], up_maps_float[:, :, upper_key:], precision=highest)], axis=2)

def sequence_attention(sequence):
    queries, query_feat, keys_low, key_feat, values_low, segment_row = sequence
    score_scale = HEAD_SIZE ** (-0.5)
    scores = lowrank_backward(jnp.einsum('ikgd,jkd->kgij', queries, keys_low, precision=highest)) * score_scale
    linear = lowrank_backward(jnp.einsum('ikge,jke->kgij', query_feat, key_feat, precision=highest))
    positions = jnp.arange(SEQ_LEN, dtype=jnp.int32)
    distance = positions[:, None] - positions[None, :]
    same_doc = segment_row[:, None] == segment_row[None, :]
    inside = same_doc & (distance >= 0) & (distance < WINDOW)
    distant = same_doc & (distance >= WINDOW)
    weights = jnp.where(inside, jnp.exp(scores), jnp.where(distant, linear, 0.0))
    probabilities = low(weights / lax.optimization_barrier(jnp.sum(weights, axis=-1, keepdims=True)))
    return jnp.einsum('kgij,jkd->ikgd', probabilities, values_low, precision=highest)

def forward(tokens, norm_gains, w_qkv, qkv_down, query_key_value_up, feature_maps, w_out, o_down, o_up, w_gate_up, w_down, segments):
    group_size = HEADS // KVH
    query_span_width = group_size * HEAD_SIZE
    upper_key = query_span_width + HEAD_SIZE
    token_rows = tokens.shape[0]
    cosines, sine_values = rotary_tables(SEQ_LEN, HEAD_SIZE)
    cosines = jnp.tile(cosines, (SEQ_TOTAL, 1))
    sine_values = jnp.tile(sine_values, (SEQ_TOTAL, 1))
    normed_one = low(rms_norm(tokens, norm_gains[0]))
    lowrank_update = lowrank_backward(jnp.einsum('td,jrd->tjr', normed_one, qkv_down, precision=highest))
    joined_adapters = jnp.einsum('td,dkc->tkc', normed_one, w_qkv, precision=highest)
    joined_adapters = lowrank_backward(joined_adapters + adapter_columns(lowrank_update, query_key_value_up, query_span_width, HEAD_SIZE))
    queries = low(rotate(joined_adapters[:, :, :query_span_width].reshape(token_rows, KVH, group_size, HEAD_SIZE), cosines[:, None, None, :], sine_values[:, None, None, :]))
    keys_low = low(rotate(joined_adapters[:, :, query_span_width:upper_key], cosines[:, None, :], sine_values[:, None, :]))
    values_low = low(joined_adapters[:, :, upper_key:])
    query_maps = feature_maps[:, :, :query_span_width].reshape(KVH, HEAD_SIZE, group_size, HEAD_SIZE)
    key_maps = feature_maps[:, :, query_span_width:]
    query_feat = low(hedgehog(lowrank_backward(jnp.einsum('tkgd,kdge->tkge', queries, query_maps, precision=highest))))
    key_feat = low(hedgehog(lowrank_backward(jnp.einsum('tkd,kde->tke', keys_low, key_maps, precision=highest))))

    def by_sequence(array):
        return array.reshape((SEQ_TOTAL, SEQ_LEN) + array.shape[1:])
    attended = lax.map(jax.checkpoint(sequence_attention), (by_sequence(queries), by_sequence(query_feat), by_sequence(keys_low), by_sequence(key_feat), by_sequence(values_low), segments))
    attended = low(lowrank_backward(attended.reshape(token_rows, KVH * query_span_width)))
    lowrank_out = lowrank_backward(jnp.dot(attended, o_down.reshape(R, -1).T, precision=highest, preferred_element_type=jnp.float32))
    branch = jnp.dot(attended, w_out, precision=highest, preferred_element_type=jnp.float32) + jnp.dot(lowrank_out, o_up, precision=highest, preferred_element_type=jnp.float32)
    hidden = tokens + lowrank_backward(branch)
    normed_two = low(rms_norm(hidden, norm_gains[1]))
    gate_up = lowrank_backward(jnp.einsum('td,dsf->tsf', normed_two, w_gate_up, precision=highest))
    product = low(jax.nn.silu(gate_up[:, 0]) * gate_up[:, 1])
    mixed = lowrank_backward(jnp.dot(product, w_down, precision=highest, preferred_element_type=jnp.float32))
    return hidden + mixed

def reference(tokens, cotangent, segments, norm_gains, w_qkv, qkv_down, query_key_value_up, feature_maps, w_out, o_down, o_up, w_gate_up, w_down):
    params = tuple((array.astype(jnp.float32) for array in (tokens, norm_gains, w_qkv, qkv_down, query_key_value_up, feature_maps, w_out, o_down, o_up, w_gate_up, w_down)))

    def wrapped(*arrays):
        return forward(*arrays, segments)
    output, pullback = jax.vjp(wrapped, *params)
    gradients = pullback(cotangent.astype(jnp.float32))
    return (output.astype(jnp.bfloat16), gradients[0].astype(jnp.bfloat16), gradients[1], gradients[2], gradients[3], gradients[4], gradients[5], gradients[6], gradients[7], gradients[8], gradients[9], gradients[10])
```

```python
from functools import partial
import jax, jax.numpy as jnp
from jax import lax
from jax.experimental import pallas as pl
from jax.experimental.pallas import tpu as pltpu
from jax.sharding import PartitionSpec as P

HEADS = 32
KVH = 8
HEAD_SIZE = 64
WINDOW = 64
LONGEST = 512
epsilon = 1e-05
rope_base = 500000.0
F32 = jnp.float32
BF16 = jnp.bfloat16


def nn(a, b):
    return lax.dot_general(a, b, (((1,), (0,)), ((), ())), preferred_element_type=F32)


def nt(a, b):
    return lax.dot_general(a, b, (((1,), (1,)), ((), ())), preferred_element_type=F32)


def rotate_t(part, cosines, sines):
    half = part.shape[0] // 2
    a, b = part[:half], part[half:]
    return jnp.concatenate([a * cosines - b * sines, b * cosines + a * sines], axis=0)


def rotate_back_t(part, cosines, sines):
    half = part.shape[0] // 2
    a, b = part[:half], part[half:]
    return jnp.concatenate([a * cosines + b * sines, b * cosines - a * sines], axis=0)


def softmaxes_t(logits):
    up = jnp.exp(logits - jnp.max(logits, axis=0, keepdims=True))
    down = jnp.exp(jnp.min(logits, axis=0, keepdims=True) - logits)
    up = up * (1.0 / jnp.sum(up, axis=0, keepdims=True))
    down = down * (1.0 / jnp.sum(down, axis=0, keepdims=True))
    return up, down


def tile_plan(length, block):
    back = LONGEST // block
    return [(i, list(range(max(0, i - back), i + 1))) for i in range(length // block)]


def tile_masks(same, query_block, key_block, block):
    lowest = (query_block - key_block) * block - (block - 1)
    if lowest >= WINDOW:
        return None, same
    shape = (block, block)
    distance = (
        lax.broadcasted_iota(jnp.int32, shape, 1)
        - lax.broadcasted_iota(jnp.int32, shape, 0)
        + (query_block - key_block) * block
    )
    inside = same & (distance < WINDOW)
    if lowest < 0:
        inside = inside & (distance >= 0)
    return inside, same & (distance >= WINDOW)


def forward_kernel(heads, block, joined_ref, cos_ref, sin_ref, map_ref, row_ref, col_ref,
                   low_ref, att_ref, root_ref, keys, kfeat):
    length = cos_ref.shape[1]
    width = heads * HEAD_SIZE
    scale = HEAD_SIZE ** -0.5
    key_t = rotate_t(joined_ref[0, width:width + HEAD_SIZE], cos_ref[...], sin_ref[...]).astype(BF16)
    low_ref[0, width:width + HEAD_SIZE] = key_t
    value_t = joined_ref[0, width + HEAD_SIZE:].astype(BF16)
    low_ref[0, width + HEAD_SIZE:] = value_t
    up, down = softmaxes_t(nn(map_ref[0, width:], key_t))
    kfeat[...] = jnp.concatenate([up, down], axis=0).T.astype(BF16)
    keys[...] = key_t.astype(F32).T.astype(BF16)

    for i, tiles in tile_plan(length, block):
        cols = slice(i * block, (i + 1) * block)

        def one_head(h, carry, i=i, tiles=tiles, cols=cols):
            rows = pl.ds(pl.multiple_of(h * HEAD_SIZE, HEAD_SIZE), HEAD_SIZE)
            query = rotate_t(joined_ref[0, rows, cols], cos_ref[:, cols], sin_ref[:, cols]).astype(BF16)
            low_ref[0, rows, cols] = query
            up, down = softmaxes_t(nn(map_ref[0, rows], query))
            feat = jnp.concatenate([up, down], axis=0).astype(BF16)
            weights = []
            total = None
            for j in tiles:
                span = slice(j * block, (j + 1) * block)
                same = col_ref[span, :] == row_ref[:, cols]
                inside, far = tile_masks(same, i, j, block)
                linear = nn(kfeat[span, :], feat)
                w = jnp.where(far, linear, 0.0)
                if inside is not None:
                    w = jnp.where(inside, jnp.exp(nn(keys[span, :], query) * scale), w)
                part = jnp.sum(w, axis=0, keepdims=True)
                total = part if total is None else total + part
                weights.append(w)
            root = lax.rsqrt(total)
            root_ref[0, h, :, cols] = root
            att = None
            for j, w in zip(tiles, weights):
                p = (w * root * root).astype(BF16)
                piece = nn(low_ref[0, width + HEAD_SIZE:, j * block:(j + 1) * block], p)
                att = piece if att is None else att + piece
            att_ref[0, rows, cols] = att.astype(BF16)
            return carry

        lax.fori_loop(0, heads, one_head, 0)


def attention_forward(joined_t, cosines, sines, maps_t, seg_row, seg_col, heads, block=256):
    groups, width, length = joined_t.shape
    qw = heads * HEAD_SIZE
    whole = lambda shape: pl.BlockSpec(shape, lambda g: (0,) * len(shape))
    mine = lambda shape: pl.BlockSpec((1,) + shape, lambda g: (g,) + (0,) * len(shape))
    return pl.pallas_call(
        partial(forward_kernel, heads, block),
        grid=(groups,),
        out_shape=(
            jax.ShapeDtypeStruct((groups, width, length), BF16),
            jax.ShapeDtypeStruct((groups, qw, length), BF16),
            jax.ShapeDtypeStruct((groups, heads, 1, length), F32),
        ),
        in_specs=[mine((width, length)), whole(cosines.shape), whole(sines.shape),
                  mine(maps_t.shape[1:]), whole(seg_row.shape), whole(seg_col.shape)],
        out_specs=(mine((width, length)), mine((qw, length)), mine((heads, 1, length))),
        scratch_shapes=[pltpu.VMEM((length, HEAD_SIZE), BF16), pltpu.VMEM((length, 2 * HEAD_SIZE), BF16)],
        compiler_params=pltpu.CompilerParams(vmem_limit_bytes=48 * 2**20),
        name="attention_forward",
    )(joined_t, cosines, sines, maps_t, seg_row, seg_col)


def backward_kernel(heads, block, low_ref, cos_ref, sin_ref, map_ref, back_ref, row_ref, col_ref,
                    att_ref, root_ref, gatt_ref, grad_ref, gmap_ref,
                    keys, kfeat, kfeat_t, values, gkeys, gkfeat, gvalues):
    length = cos_ref.shape[1]
    width = heads * HEAD_SIZE
    scale = HEAD_SIZE ** -0.5
    key_t = low_ref[0, width:width + HEAD_SIZE]
    key_up, key_down = softmaxes_t(nn(map_ref[0, width:], key_t))
    both = jnp.concatenate([key_up, key_down], axis=0)
    kfeat_t[...] = both.astype(BF16)
    kfeat[...] = both.T.astype(BF16)
    keys[...] = key_t.astype(F32).T.astype(BF16)
    values[...] = low_ref[0, width + HEAD_SIZE:].astype(F32).T.astype(BF16)
    gkeys[...] = jnp.zeros_like(gkeys)
    gkfeat[...] = jnp.zeros_like(gkfeat)
    gvalues[...] = jnp.zeros_like(gvalues)
    gmap_ref[...] = jnp.zeros_like(gmap_ref)

    for i, tiles in tile_plan(length, block):
        cols = slice(i * block, (i + 1) * block)

        def one_head(h, carry, i=i, tiles=tiles, cols=cols):
            rows = pl.ds(pl.multiple_of(h * HEAD_SIZE, HEAD_SIZE), HEAD_SIZE)
            query = low_ref[0, rows, cols]
            gatt = gatt_ref[0, rows, cols]
            up, down = softmaxes_t(nn(map_ref[0, rows], query))
            feat = jnp.concatenate([up, down], axis=0).astype(BF16)
            root = root_ref[0, h, :, cols]
            inverse = root * root
            delta = jnp.sum(gatt.astype(F32) * att_ref[0, rows, cols].astype(F32), axis=0, keepdims=True)
            gquery = jnp.zeros((HEAD_SIZE, block), F32)
            gfeat = jnp.zeros((2 * HEAD_SIZE, block), F32)
            for j in tiles:
                span = slice(j * block, (j + 1) * block)
                same = col_ref[span, :] == row_ref[:, cols]
                inside, far = tile_masks(same, i, j, block)
                gprob = nn(values[span, :], gatt) - delta
                grad_far = jnp.where(far, gprob * root * root, 0.0).astype(BF16)
                p = jnp.where(far, nn(kfeat[span, :], feat) * root * root, 0.0)
                if inside is not None:
                    near = jnp.where(inside, jnp.exp(nn(keys[span, :], query) * scale) * root * root, 0.0)
                    p = jnp.where(inside, near, p)
                    grad_near = (near * gprob * scale).astype(BF16)
                    gquery = gquery + nn(low_ref[0, width:width + HEAD_SIZE, span], grad_near)
                    gkeys[span, :] += nt(grad_near, query)
                gvalues[span, :] += nt(p.astype(BF16), gatt)
                gfeat = gfeat + nn(kfeat_t[:, span], grad_far)
                gkfeat[span, :] += nt(grad_far, feat)
            glogits = softmaxes_back_t(up, down, gfeat)
            gquery = gquery + nn(back_ref[0, h], glogits)
            gmap_ref[0, h] += nt(query, glogits)
            grad_ref[0, rows, cols] = rotate_back_t(gquery, cos_ref[:, cols], sin_ref[:, cols]).astype(BF16)
            return carry

        lax.fori_loop(0, heads, one_head, 0)
    glogits = softmaxes_back_t(key_up, key_down, gkfeat[...].T)
    gkey_t = gkeys[...].T + nn(back_ref[0, heads], glogits)
    gmap_ref[0, heads] = nt(key_t, glogits)
    grad_ref[0, width:width + HEAD_SIZE] = rotate_back_t(gkey_t, cos_ref[...], sin_ref[...]).astype(BF16)
    grad_ref[0, width + HEAD_SIZE:] = gvalues[...].T.astype(BF16)


def softmaxes_back_t(up, down, grads):
    gup, gdown = grads[:HEAD_SIZE], grads[HEAD_SIZE:]
    return (
        up * (gup - jnp.sum(gup * up, axis=0, keepdims=True))
        - down * (gdown - jnp.sum(gdown * down, axis=0, keepdims=True))
    ).astype(BF16)


def attention_backward(low, cosines, sines, maps_t, maps, seg_row, seg_col, att, root, gatt, heads, block=256):
    groups, width, length = low.shape
    qw = heads * HEAD_SIZE
    whole = lambda shape: pl.BlockSpec(shape, lambda g: (0,) * len(shape))
    mine = lambda shape: pl.BlockSpec((1,) + shape, lambda g: (g,) + (0,) * len(shape))
    return pl.pallas_call(
        partial(backward_kernel, heads, block),
        grid=(groups,),
        out_shape=(
            jax.ShapeDtypeStruct((groups, width, length), BF16),
            jax.ShapeDtypeStruct((groups, heads + 1, HEAD_SIZE, HEAD_SIZE), F32),
        ),
        in_specs=[mine((width, length)), whole(cosines.shape), whole(sines.shape),
                  mine(maps_t.shape[1:]), mine(maps.shape[1:]), whole(seg_row.shape), whole(seg_col.shape),
                  mine((qw, length)), mine((heads, 1, length)), mine((qw, length))],
        out_specs=(mine((width, length)), mine((heads + 1, HEAD_SIZE, HEAD_SIZE))),
        scratch_shapes=[
            pltpu.VMEM((length, HEAD_SIZE), BF16), pltpu.VMEM((length, 2 * HEAD_SIZE), BF16),
            pltpu.VMEM((2 * HEAD_SIZE, length), BF16), pltpu.VMEM((length, HEAD_SIZE), BF16),
            pltpu.VMEM((length, HEAD_SIZE), F32), pltpu.VMEM((length, 2 * HEAD_SIZE), F32),
            pltpu.VMEM((length, HEAD_SIZE), F32)],
        compiler_params=pltpu.CompilerParams(vmem_limit_bytes=48 * 2**20),
        name="attention_backward",
    )(low, cosines, sines, maps_t, maps, seg_row, seg_col, att, root, gatt)


def rotary_tables_t(length, width):
    half = width // 2
    frequency = rope_base ** (-(jnp.arange(half, dtype=F32) * 2.0) / width)
    angles = frequency[:, None] * jnp.arange(length, dtype=F32)[None, :]
    return jnp.cos(angles), jnp.sin(angles)


def normalize(values, gain_row):
    inverse = lax.rsqrt(jnp.mean(values * values, axis=-1, keepdims=True) + epsilon)
    scaled = values * inverse
    return scaled, inverse, (scaled * gain_row).astype(BF16)


def ring(size, shift=1):
    return [(i, (i + shift) % size) for i in range(size)]


def flip(size, bit):
    return [(i, i ^ (1 << bit)) for i in range(size)]


def pick(array, index, axis):
    return lax.dynamic_index_in_dim(array, index, axis, keepdims=False)


def chunk_of(array, index, rows, axis):
    return lax.dynamic_slice_in_dim(array, index * rows, rows, axis)


def ring_sum(parts):
    size = len(parts)
    running = parts[1].astype(BF16)
    for step in range(2, size + 1):
        arrived = lax.ppermute(running, "tensor", ring(size)).astype(F32)
        running = arrived + parts[step % size].astype(F32)
        if step < size:
            running = running.astype(BF16)
    return running


def bits_of(size):
    return size.bit_length() - 1


def halve(current, axis, order, left=None):
    size = lax.axis_size("dp")
    mine = lax.axis_index("dp")
    remaining = sorted(order, reverse=True)
    shape = current.shape
    current = current.reshape(shape[:axis] + (2,) * len(remaining) + shape[axis + 1:])
    for place, bit in enumerate(order):
        where = axis + remaining.index(bit)
        own = (mine >> bit) & 1
        arrived = lax.ppermute(pick(current, 1 - own, where), "dp", flip(size, bit))
        current = pick(current, own, where).astype(F32) + arrived.astype(F32)
        remaining.remove(bit)
        if place < len(order) - 1:
            current = current.astype(BF16)
    return current


def scatter_dp(make, axis, stream_axis):
    size = lax.axis_size("dp")
    core = lax.axis_index("dp") & 1
    arrived = lax.ppermute(make(1 - core).astype(BF16), "dp", flip(size, 0))
    current = (make(core) + arrived.astype(F32)).astype(BF16)
    rest = list(range(1, bits_of(size)))
    half = current.shape[stream_axis] // 2
    first = halve(lax.slice_in_dim(current, 0, half, axis=stream_axis), axis, rest)
    second = halve(lax.slice_in_dim(current, half, 2 * half, axis=stream_axis), axis, rest[::-1])
    return jnp.concatenate([first, second], axis=stream_axis - (1 if stream_axis > axis else 0))


def scatter_small(blocks, over_tensor):
    size = lax.axis_size("dp")
    for bit in reversed(range(bits_of(size))):
        own = (lax.axis_index("dp") >> bit) & 1
        blocks = blocks.reshape((2, blocks.shape[0] // 2) + blocks.shape[1:])
        blocks = pick(blocks, own, 0) + lax.ppermute(pick(blocks, 1 - own, 0), "dp", flip(size, bit))
    blocks = blocks[0]
    if over_tensor:
        size = lax.axis_size("tensor")
        for bit in reversed(range(bits_of(size))):
            own = (lax.axis_index("tensor") >> bit) & 1
            blocks = blocks.reshape((2, blocks.shape[0] // 2) + blocks.shape[1:])
            blocks = pick(blocks, own, 0) + lax.ppermute(
                pick(blocks, 1 - own, 0), "tensor", flip(size, bit)
            )
        blocks = blocks[0]
    return blocks


def double(pieces, order):
    size = lax.axis_size("dp")
    mine = lax.axis_index("dp")
    n, rows, cols = pieces.shape
    done = []
    current = pieces.reshape((n, rows, cols))
    for bit in order:
        arrived = lax.ppermute(current, "dp", flip(size, bit))
        own = ((mine >> bit) & 1) == 0
        place = 1 + sum(1 for other in done if other > bit)
        low = jnp.where(own, current, arrived)
        high = jnp.where(own, arrived, current)
        current = jnp.stack([low, high], axis=place)
        done.append(bit)
    return current.reshape(n, size * rows, cols)


def gather_weight(shard):
    size = lax.axis_size("dp")
    n = lax.axis_size("tensor")
    rows = shard.shape[0] // size
    pieces = [chunk_of(shard, lax.axis_index("dp"), rows, 0)]
    for _ in range(n - 1):
        pieces.append(lax.ppermute(pieces[-1], "tensor", ring(n)))
    pieces = jnp.stack(pieces)
    half = shard.shape[1] // 2
    rest = list(range(1, bits_of(size)))
    first = double(pieces[:, :, :half], rest + [0])
    second = double(pieces[:, :, half:], rest[::-1] + [0])
    return jnp.concatenate([first, second], axis=2)


def local(
    tokens,
    cotangent,
    segments,
    norm_gains,
    w_qkv,
    qkv_down,
    query_key_value_up,
    feature_maps,
    w_out,
    o_down,
    o_up,
    w_gate_up,
    w_down,
):
    token_rows, model_width = tokens.shape
    groups = w_qkv.shape[1]
    heads = HEADS // KVH
    query_width = heads * HEAD_SIZE
    joined_width = w_qkv.shape[2]
    rank = o_up.shape[0]
    dp = lax.axis_size("dp")
    n = lax.axis_size("tensor")
    me = lax.axis_index("tensor")
    share = token_rows // n
    gains = norm_gains.astype(F32)
    cosines, sines = rotary_tables_t(token_rows, HEAD_SIZE)
    dot = partial(jnp.einsum, preferred_element_type=F32)

    up = query_key_value_up.astype(BF16)
    edges = ((0, query_width), (query_width, query_width + HEAD_SIZE), (query_width + HEAD_SIZE, joined_width))
    up_wide = jnp.stack(
        [jnp.pad(up[:, :, a:b], ((0, 0), (0, 0), (a, joined_width - b))) for a, b in edges]
    )
    w_joined = (
        jnp.transpose(w_qkv, (1, 2, 0)).astype(F32) + dot("jrkc,jrd->kcd", up_wide, qkv_down)
    ).astype(BF16).reshape(groups * joined_width, model_width)
    down_flat = o_down.reshape(rank, -1)
    w_branch = (w_out.astype(F32) + dot("rc,rd->cd", down_flat, o_up)).astype(BF16)
    down_all = lax.all_gather(down_flat, "tensor")
    all_branch = gather_weight(w_branch)
    all_joined = gather_weight(w_joined)

    _, _, normed_one = normalize(tokens.astype(F32), gains[0])
    lowrank = dot("td,jrd->tjr", normed_one, qkv_down)
    joined = dot("cd,td->ct", w_joined, normed_one).reshape(groups, joined_width, token_rows)
    maps_t = jnp.swapaxes(feature_maps, 1, 2)
    maps = jnp.stack(
        [feature_maps[:, :, i * HEAD_SIZE:(i + 1) * HEAD_SIZE] for i in range(heads + 1)], axis=1
    )
    seg_row = segments.reshape(1, token_rows)
    seg_col = segments.reshape(token_rows, 1)
    low, attended, root = attention_forward(joined, cosines, sines, maps_t, seg_row, seg_col, heads)
    attended_flat = attended.reshape(groups * query_width, token_rows)
    att_parts = [chunk_of(attended_flat, me, share, 1)]
    for s in range(1, n):
        att_parts.append(
            lax.ppermute(chunk_of(attended_flat, (me + s) % n, share, 1), "tensor", ring(n, s))
        )
    att_share = jnp.stack(att_parts)
    down_places = jnp.stack([pick(down_all, (me + n - s) % n, 0) for s in range(n)])
    lowrank_out = dot("nct,nrc->tr", att_share, down_places)
    tokens_share = chunk_of(tokens, me, share, 0).astype(F32)
    hidden = tokens_share + dot("nct,ncd->td", att_share, all_branch)
    scaled_two, inverse_two, normed_two = normalize(hidden, gains[1])

    normed, acts, grads, cots, mixed_parts, grad_parts = [normed_two], [], [], [], [], []
    for k in range(n):
        if k < n - 1:
            normed.append(lax.ppermute(normed[k], "tensor", ring(n)))
        cot = chunk_of(cotangent, (me + n - k) % n, share, 0)
        gate_up = dot("td,dsf->tsf", normed[k], w_gate_up)
        gate, upper = gate_up[:, 0], gate_up[:, 1]
        sigma = jax.nn.sigmoid(gate)
        silu = gate * sigma
        act = (silu * upper).astype(BF16)
        grad_act = dot("td,fd->tf", cot, w_down)
        grad_gate = grad_act * upper * sigma * (1.0 + gate * (1.0 - sigma))
        grad_gate_up = jnp.stack([grad_gate, grad_act * silu], axis=1).astype(BF16)
        grad_parts.append(dot("tsf,dsf->td", grad_gate_up, w_gate_up).astype(BF16))
        mixed_parts.append(dot("tf,fd->td", act, w_down).astype(BF16))
        acts.append(act)
        grads.append(grad_gate_up)
        cots.append(cot)
    grad_normed_two = ring_sum(grad_parts)
    weighted = grad_normed_two * gains[1]
    grad_hidden = chunk_of(cotangent, me, share, 0).astype(F32) + inverse_two * (
        weighted - scaled_two * jnp.mean(weighted * scaled_two, axis=-1, keepdims=True)
    )
    gain_two = jnp.sum(grad_normed_two * scaled_two, axis=0)
    grad_branch = grad_hidden.astype(BF16)

    grad_att_share = dot("ncd,td->nct", all_branch, grad_branch).astype(BF16)
    back = [grad_att_share[0]]
    for s in range(1, n):
        back.append(lax.ppermute(grad_att_share[s], "tensor", ring(n, -s)))
    order = [pick(jnp.stack(back), (j + n - me) % n, 0) for j in range(n)]
    grad_attended = jnp.concatenate(order, axis=1).reshape(groups, query_width, token_rows)
    mixed = ring_sum(mixed_parts)
    output = (hidden + mixed).astype(BF16)

    grad_joined, grad_maps = attention_backward(
        low, cosines, sines, maps_t, maps, seg_row, seg_col, attended, root, grad_attended, heads
    )
    flat_joined = grad_joined.reshape(groups * joined_width, token_rows)
    parts = [chunk_of(flat_joined, me, share, 1)]
    for s in range(1, n):
        parts.append(
            lax.ppermute(chunk_of(flat_joined, (me + s) % n, share, 1), "tensor", ring(n, s))
        )
    grad_normed_one = dot("nct,ncd->td", jnp.stack(parts), all_joined)
    scaled_one, inverse_one, _ = normalize(tokens_share, gains[0])
    weighted = grad_normed_one * gains[0]
    grad_input = (
        grad_hidden
        + inverse_one
        * (weighted - scaled_one * jnp.mean(weighted * scaled_one, axis=-1, keepdims=True))
    ).astype(BF16)
    gain_one = jnp.sum(grad_normed_one * scaled_one, axis=0)

    all_normed = jnp.concatenate(normed, axis=0)
    all_acts = jnp.concatenate(acts, axis=0)
    all_grads = jnp.concatenate(grads, axis=0)
    all_cots = jnp.concatenate(cots, axis=0)
    width = model_width // dp

    def of_core(array, core):
        return pick(array.reshape(array.shape[0], dp // 2, 2, width), core, 2)

    out_gate_up = scatter_dp(
        lambda core: dot("tbe,tsf->besf", of_core(all_normed, core), all_grads), 0, 2
    )
    out_down = scatter_dp(lambda core: dot("tf,tbe->fbe", all_acts, of_core(all_cots, core)), 1, 0)
    flat_att = att_share.reshape(-1, share)
    out_branch = scatter_dp(
        lambda core: dot("ct,tbe->cbe", flat_att, of_core(grad_branch, core)), 1, 0
    )
    branch_rows = out_branch.shape[0] // n
    out_branch = ring_sum([out_branch[s * branch_rows:(s + 1) * branch_rows] for s in range(n)])
    out_qkv = scatter_dp(
        lambda core: dot("tbe,kct->bekc", of_core(normed_one, core), grad_joined), 0, 1
    )

    lowrank_low = lowrank.astype(BF16)
    grad_up = jnp.concatenate(
        [dot("tr,kct->rkc", lowrank_low[:, j], grad_joined[:, a:b]) for j, (a, b) in enumerate(edges)],
        axis=2,
    )
    grad_maps = jnp.transpose(grad_maps, (0, 2, 1, 3)).reshape(groups, HEAD_SIZE, -1)
    small = jnp.concatenate(
        [
            jnp.moveaxis(grad_up.reshape(rank, groups, dp, -1), 2, 0).reshape(dp, -1),
            jnp.moveaxis(grad_maps.reshape(groups, HEAD_SIZE, dp, -1), 2, 0).reshape(dp, -1),
        ],
        axis=1,
    )
    small = scatter_small(small, False)
    cut = rank * groups * (joined_width // dp)
    out_up = small[:cut].reshape(rank, groups, -1)
    out_maps = small[cut:].reshape(groups, HEAD_SIZE, -1)

    grad_lowrank = dot("kct,jrkc->jrt", grad_joined, up_wide).astype(BF16)
    grad_qkv_down = dot("jrt,td->jrd", grad_lowrank, normed_one)
    grad_lowrank_out = dot("td,rd->tr", grad_branch, o_up).astype(BF16)
    grad_o_up = dot("tr,td->rd", lowrank_out.astype(BF16), grad_branch)
    grad_o_down = dot("tr,nct->nrc", grad_lowrank_out, att_share)
    grad_o_down = jnp.stack([pick(grad_o_down, (me + n - j) % n, 0) for j in range(n)])
    shared = jnp.concatenate(
        [gain_one[None], gain_two[None], grad_qkv_down.reshape(-1, model_width), grad_o_up], axis=0
    )
    lines = shared.shape[0]
    shared = jnp.transpose(shared.reshape(lines, dp, n, -1), (1, 2, 0, 3)).reshape(dp, n, -1)
    downs = grad_o_down.reshape(n, rank, groups, dp, -1)
    downs = jnp.transpose(downs, (3, 0, 1, 2, 4)).reshape(dp, n, -1)
    cut = shared.shape[2]
    packed = scatter_small(jnp.concatenate([shared, downs], axis=2), True)
    shared = packed[:cut].reshape(lines, -1)
    out_o_down = packed[cut:].reshape(rank, groups, -1)
    return (
        output,
        grad_input,
        shared[:2],
        out_qkv,
        shared[2:lines - rank].reshape(3, rank, -1),
        out_up,
        out_maps,
        out_branch,
        out_o_down,
        shared[lines - rank:],
        out_gate_up,
        out_down,
    )


def solution(mesh):
    in_specs = (
        P("dp", None),
        P("dp", None),
        P("dp", None),
        P(),
        P(None, "tensor", None),
        P(),
        P(None, "tensor", None),
        P("tensor", None, None),
        P("tensor", None),
        P(None, "tensor", None),
        P(),
        P(None, None, "tensor"),
        P("tensor", None),
    )
    out_specs = (
        P(("dp", "tensor"), None),
        P(("dp", "tensor"), None),
        P(None, ("dp", "tensor")),
        P("dp", "tensor", None),
        P(None, None, ("dp", "tensor")),
        P(None, "tensor", "dp"),
        P("tensor", None, "dp"),
        P("tensor", "dp"),
        P(None, "tensor", "dp"),
        P(None, ("dp", "tensor")),
        P("dp", None, "tensor"),
        P("tensor", "dp"),
    )
    return jax.shard_map(
        local, mesh=mesh, in_specs=in_specs, out_specs=out_specs, check_vma=False
    )
```

```python
from functools import partial
import jax, jax.numpy as jnp
from jax import lax
from jax.experimental import pallas as pl
from jax.experimental.pallas import tpu as pltpu
from jax.sharding import PartitionSpec as P

HEADS = 32
KVH = 8
HEAD_SIZE = 64
WINDOW = 64
LONGEST = 512
epsilon = 1e-05
rope_base = 500000.0
F32 = jnp.float32
BF16 = jnp.bfloat16


def nn(a, b):
    return lax.dot_general(a, b, (((1,), (0,)), ((), ())), preferred_element_type=F32)


def nt(a, b):
    return lax.dot_general(a, b, (((1,), (1,)), ((), ())), preferred_element_type=F32)


def rotate_t(part, cosines, sines):
    half = part.shape[0] // 2
    a, b = part[:half], part[half:]
    return jnp.concatenate([a * cosines - b * sines, b * cosines + a * sines], axis=0)


def rotate_back_t(part, cosines, sines):
    half = part.shape[0] // 2
    a, b = part[:half], part[half:]
    return jnp.concatenate([a * cosines + b * sines, b * cosines - a * sines], axis=0)


def softmaxes_t(logits):
    up = jnp.exp(logits - jnp.max(logits, axis=0, keepdims=True))
    down = jnp.exp(jnp.min(logits, axis=0, keepdims=True) - logits)
    up = up * (1.0 / jnp.sum(up, axis=0, keepdims=True))
    down = down * (1.0 / jnp.sum(down, axis=0, keepdims=True))
    return up, down


def tile_plan(length, block):
    back = LONGEST // block
    return [(i, list(range(max(0, i - back), i + 1))) for i in range(length // block)]


def tile_masks(same, query_block, key_block, block):
    lowest = (query_block - key_block) * block - (block - 1)
    if lowest >= WINDOW:
        return None, same
    shape = (block, block)
    distance = (
        lax.broadcasted_iota(jnp.int32, shape, 1)
        - lax.broadcasted_iota(jnp.int32, shape, 0)
        + (query_block - key_block) * block
    )
    inside = same & (distance < WINDOW)
    if lowest < 0:
        inside = inside & (distance >= 0)
    return inside, same & (distance >= WINDOW)


def forward_kernel(heads, block, joined_ref, cos_ref, sin_ref, map_ref, row_ref, col_ref,
                   low_ref, att_ref, root_ref, keys, kfeat):
    length = cos_ref.shape[1]
    width = heads * HEAD_SIZE
    scale = HEAD_SIZE ** -0.5
    key_t = rotate_t(joined_ref[0, width:width + HEAD_SIZE], cos_ref[...], sin_ref[...]).astype(BF16)
    low_ref[0, width:width + HEAD_SIZE] = key_t
    value_t = joined_ref[0, width + HEAD_SIZE:].astype(BF16)
    low_ref[0, width + HEAD_SIZE:] = value_t
    up, down = softmaxes_t(nn(map_ref[0, width:], key_t))
    kfeat[...] = jnp.concatenate([up, down], axis=0).T.astype(BF16)
    keys[...] = key_t.astype(F32).T.astype(BF16)

    for i, tiles in tile_plan(length, block):
        cols = slice(i * block, (i + 1) * block)

        def one_head(h, carry, i=i, tiles=tiles, cols=cols):
            rows = pl.ds(pl.multiple_of(h * HEAD_SIZE, HEAD_SIZE), HEAD_SIZE)
            query = rotate_t(joined_ref[0, rows, cols], cos_ref[:, cols], sin_ref[:, cols]).astype(BF16)
            low_ref[0, rows, cols] = query
            up, down = softmaxes_t(nn(map_ref[0, rows], query))
            feat = jnp.concatenate([up, down], axis=0).astype(BF16)
            weights = []
            total = None
            for j in tiles:
                span = slice(j * block, (j + 1) * block)
                same = col_ref[span, :] == row_ref[:, cols]
                inside, far = tile_masks(same, i, j, block)
                linear = nn(kfeat[span, :], feat)
                w = jnp.where(far, linear, 0.0)
                if inside is not None:
                    w = jnp.where(inside, jnp.exp(nn(keys[span, :], query) * scale), w)
                part = jnp.sum(w, axis=0, keepdims=True)
                total = part if total is None else total + part
                weights.append(w)
            root = lax.rsqrt(total)
            root_ref[0, h, :, cols] = root
            att = None
            for j, w in zip(tiles, weights):
                p = (w * root * root).astype(BF16)
                piece = nn(low_ref[0, width + HEAD_SIZE:, j * block:(j + 1) * block], p)
                att = piece if att is None else att + piece
            att_ref[0, rows, cols] = att.astype(BF16)
            return carry

        lax.fori_loop(0, heads, one_head, 0)


def attention_forward(joined_t, cosines, sines, maps_t, seg_row, seg_col, heads, block=256):
    groups, width, length = joined_t.shape
    qw = heads * HEAD_SIZE
    whole = lambda shape: pl.BlockSpec(shape, lambda g: (0,) * len(shape))
    mine = lambda shape: pl.BlockSpec((1,) + shape, lambda g: (g,) + (0,) * len(shape))
    return pl.pallas_call(
        partial(forward_kernel, heads, block),
        grid=(groups,),
        out_shape=(
            jax.ShapeDtypeStruct((groups, width, length), BF16),
            jax.ShapeDtypeStruct((groups, qw, length), BF16),
            jax.ShapeDtypeStruct((groups, heads, 1, length), F32),
        ),
        in_specs=[mine((width, length)), whole(cosines.shape), whole(sines.shape),
                  mine(maps_t.shape[1:]), whole(seg_row.shape), whole(seg_col.shape)],
        out_specs=(mine((width, length)), mine((qw, length)), mine((heads, 1, length))),
        scratch_shapes=[pltpu.VMEM((length, HEAD_SIZE), BF16), pltpu.VMEM((length, 2 * HEAD_SIZE), BF16)],
        compiler_params=pltpu.CompilerParams(vmem_limit_bytes=48 * 2**20),
        name="attention_forward",
    )(joined_t, cosines, sines, maps_t, seg_row, seg_col)


def backward_kernel(heads, block, low_ref, cos_ref, sin_ref, map_ref, back_ref, row_ref, col_ref,
                    att_ref, root_ref, gatt_ref, grad_ref, gmap_ref,
                    keys, kfeat, kfeat_t, values, gkeys, gkfeat, gvalues):
    length = cos_ref.shape[1]
    width = heads * HEAD_SIZE
    scale = HEAD_SIZE ** -0.5
    key_t = low_ref[0, width:width + HEAD_SIZE]
    key_up, key_down = softmaxes_t(nn(map_ref[0, width:], key_t))
    both = jnp.concatenate([key_up, key_down], axis=0)
    kfeat_t[...] = both.astype(BF16)
    kfeat[...] = both.T.astype(BF16)
    keys[...] = key_t.astype(F32).T.astype(BF16)
    values[...] = low_ref[0, width + HEAD_SIZE:].astype(F32).T.astype(BF16)
    gkeys[...] = jnp.zeros_like(gkeys)
    gkfeat[...] = jnp.zeros_like(gkfeat)
    gvalues[...] = jnp.zeros_like(gvalues)
    gmap_ref[...] = jnp.zeros_like(gmap_ref)

    for i, tiles in tile_plan(length, block):
        cols = slice(i * block, (i + 1) * block)

        def one_head(h, carry, i=i, tiles=tiles, cols=cols):
            rows = pl.ds(pl.multiple_of(h * HEAD_SIZE, HEAD_SIZE), HEAD_SIZE)
            query = low_ref[0, rows, cols]
            gatt = gatt_ref[0, rows, cols]
            up, down = softmaxes_t(nn(map_ref[0, rows], query))
            feat = jnp.concatenate([up, down], axis=0).astype(BF16)
            root = root_ref[0, h, :, cols]
            inverse = root * root
            delta = jnp.sum(gatt.astype(F32) * att_ref[0, rows, cols].astype(F32), axis=0, keepdims=True)
            gquery = jnp.zeros((HEAD_SIZE, block), F32)
            gfeat = jnp.zeros((2 * HEAD_SIZE, block), F32)
            for j in tiles:
                span = slice(j * block, (j + 1) * block)
                same = col_ref[span, :] == row_ref[:, cols]
                inside, far = tile_masks(same, i, j, block)
                gprob = nn(values[span, :], gatt) - delta
                grad_far = jnp.where(far, gprob * root * root, 0.0).astype(BF16)
                p = jnp.where(far, nn(kfeat[span, :], feat) * root * root, 0.0)
                if inside is not None:
                    near = jnp.where(inside, jnp.exp(nn(keys[span, :], query) * scale) * root * root, 0.0)
                    p = jnp.where(inside, near, p)
                    grad_near = (near * gprob * scale).astype(BF16)
                    gquery = gquery + nn(low_ref[0, width:width + HEAD_SIZE, span], grad_near)
                    gkeys[span, :] += nt(grad_near, query)
                gvalues[span, :] += nt(p.astype(BF16), gatt)
                gfeat = gfeat + nn(kfeat_t[:, span], grad_far)
                gkfeat[span, :] += nt(grad_far, feat)
            glogits = softmaxes_back_t(up, down, gfeat)
            gquery = gquery + nn(back_ref[0, h], glogits)
            gmap_ref[0, h] += nt(query, glogits)
            grad_ref[0, rows, cols] = rotate_back_t(gquery, cos_ref[:, cols], sin_ref[:, cols]).astype(BF16)
            return carry

        lax.fori_loop(0, heads, one_head, 0)
    glogits = softmaxes_back_t(key_up, key_down, gkfeat[...].T)
    gkey_t = gkeys[...].T + nn(back_ref[0, heads], glogits)
    gmap_ref[0, heads] = nt(key_t, glogits)
    grad_ref[0, width:width + HEAD_SIZE] = rotate_back_t(gkey_t, cos_ref[...], sin_ref[...]).astype(BF16)
    grad_ref[0, width + HEAD_SIZE:] = gvalues[...].T.astype(BF16)


def softmaxes_back_t(up, down, grads):
    gup, gdown = grads[:HEAD_SIZE], grads[HEAD_SIZE:]
    return (
        up * (gup - jnp.sum(gup * up, axis=0, keepdims=True))
        - down * (gdown - jnp.sum(gdown * down, axis=0, keepdims=True))
    ).astype(BF16)


def attention_backward(low, cosines, sines, maps_t, maps, seg_row, seg_col, att, root, gatt, heads, block=256):
    groups, width, length = low.shape
    qw = heads * HEAD_SIZE
    whole = lambda shape: pl.BlockSpec(shape, lambda g: (0,) * len(shape))
    mine = lambda shape: pl.BlockSpec((1,) + shape, lambda g: (g,) + (0,) * len(shape))
    return pl.pallas_call(
        partial(backward_kernel, heads, block),
        grid=(groups,),
        out_shape=(
            jax.ShapeDtypeStruct((groups, width, length), BF16),
            jax.ShapeDtypeStruct((groups, heads + 1, HEAD_SIZE, HEAD_SIZE), F32),
        ),
        in_specs=[mine((width, length)), whole(cosines.shape), whole(sines.shape),
                  mine(maps_t.shape[1:]), mine(maps.shape[1:]), whole(seg_row.shape), whole(seg_col.shape),
                  mine((qw, length)), mine((heads, 1, length)), mine((qw, length))],
        out_specs=(mine((width, length)), mine((heads + 1, HEAD_SIZE, HEAD_SIZE))),
        scratch_shapes=[
            pltpu.VMEM((length, HEAD_SIZE), BF16), pltpu.VMEM((length, 2 * HEAD_SIZE), BF16),
            pltpu.VMEM((2 * HEAD_SIZE, length), BF16), pltpu.VMEM((length, HEAD_SIZE), BF16),
            pltpu.VMEM((length, HEAD_SIZE), F32), pltpu.VMEM((length, 2 * HEAD_SIZE), F32),
            pltpu.VMEM((length, HEAD_SIZE), F32)],
        compiler_params=pltpu.CompilerParams(vmem_limit_bytes=48 * 2**20),
        name="attention_backward",
    )(low, cosines, sines, maps_t, maps, seg_row, seg_col, att, root, gatt)


def rotary_tables_t(length, width):
    half = width // 2
    frequency = rope_base ** (-(jnp.arange(half, dtype=F32) * 2.0) / width)
    angles = frequency[:, None] * jnp.arange(length, dtype=F32)[None, :]
    return jnp.cos(angles), jnp.sin(angles)


def normalize(values, gain_row):
    inverse = lax.rsqrt(jnp.mean(values * values, axis=-1, keepdims=True) + epsilon)
    scaled = values * inverse
    return scaled, inverse, (scaled * gain_row).astype(BF16)


def feed_kernel(
    n, dp, tile, cut,
    normed_in, cot_in, gate_up_in, down_in,
    sum_out, mixed_out, grads_out,
    gate_up, down, normed, cots, acts, grads, arriving, sending, mixed, turned,
    load_sems, weight_sems, out_sems, gather_send, gather_recv, sum_send, sum_recv, mixed_sems,
):
    share, width = normed_in.shape
    hidden = down_in.shape[0]
    block = width // dp
    piece = share // cut
    per = hidden // tile
    me = lax.axis_index("tensor")
    core = lax.rem(lax.axis_index("dp"), 2)
    place = (me, n - 1 - me)
    ends = (me < n - 1, me > 0)
    partner = (me + 1, me - 1)

    def device(way):
        return {"tensor": partner[way]}

    def rows_of(j, size=share):
        return pl.ds(pl.multiple_of(j * share, 16), size)

    barrier = pltpu.get_barrier_semaphore()
    for way in range(2):

        @pl.when(ends[way])
        def _(way=way):
            pl.semaphore_signal(barrier, inc=1, device_id=device(way), device_id_type=pl.DeviceIdType.MESH)

    own_load = pltpu.make_async_copy(normed_in, normed.at[rows_of(me)], load_sems.at[0])
    cot_load = pltpu.make_async_copy(cot_in, cots, load_sems.at[1])
    own_load.start()

    def weight_loads(f):
        span = slice(f * tile, (f + 1) * tile)
        return (
            pltpu.make_async_copy(gate_up_in.at[0, :, span], gate_up.at[0:width, span], weight_sems.at[0, f]),
            pltpu.make_async_copy(gate_up_in.at[1, :, span], gate_up.at[width:2 * width, span], weight_sems.at[1, f]),
            pltpu.make_async_copy(down_in.at[span], down.at[span], weight_sems.at[2, f]),
        )

    weights = [weight_loads(f) for f in range(per)]
    for load in weights[0]:
        load.start()
    cot_load.start()
    for loads in weights[1:]:
        for load in loads:
            load.start()
    inner = (me > 0) & (me < n - 1)

    @pl.when(inner)
    def _():
        pl.semaphore_wait(barrier, 2)

    @pl.when(jnp.logical_not(inner))
    def _():
        pl.semaphore_wait(barrier, 1)

    def gather(way, j):
        return pltpu.make_async_remote_copy(
            src_ref=normed.at[rows_of(j)], dst_ref=normed.at[rows_of(j)],
            send_sem=gather_send.at[way, j], recv_sem=gather_recv.at[way, j],
            device_id=device(way), device_id_type=pl.DeviceIdType.MESH)

    def gather_arrival(way, j):
        return pltpu.make_async_copy(normed.at[rows_of(j)], normed.at[rows_of(j)], gather_recv.at[way, j])

    def pass_on(way, j, q):
        rows = pl.ds(pl.multiple_of(j * share + q * piece, 16), piece)
        last = j == partner[way]
        slot = jnp.where(last, n, j) if way else j
        goal = pl.ds(pl.multiple_of(slot * share + q * piece, 16), piece)
        return pltpu.make_async_remote_copy(
            src_ref=sending.at[rows], dst_ref=arriving.at[goal],
            send_sem=sum_send.at[way, j * cut + q], recv_sem=sum_recv.at[way, j * cut + q],
            device_id=device(way), device_id_type=pl.DeviceIdType.MESH)

    def sum_arrival(way, j, q, slot):
        rows = pl.ds(pl.multiple_of(slot * share + q * piece, 16), piece)
        return pltpu.make_async_copy(arriving.at[rows], arriving.at[rows], sum_recv.at[way, j * cut + q])

    own_load.wait()
    for way in range(2):

        @pl.when(ends[way])
        def _(way=way):
            gather(way, me).start()

    def first_half(rows, f):
        span = pl.ds(pl.multiple_of(f * tile, tile), tile)
        upper = pl.ds(pl.multiple_of(hidden + f * tile, tile), tile)
        gate = nn(normed[rows, :], gate_up[0:width, span])
        up = nn(normed[rows, :], gate_up[width:2 * width, span])
        grad_act = nt(cots[rows, :], down[span, :])
        sigma = 1.0 / (1.0 + jnp.exp(-gate))
        silu = gate * sigma
        acts[rows, span] = (silu * up).astype(BF16)
        grads[rows, span] = (grad_act * up * (sigma + silu * (1.0 - sigma))).astype(BF16)
        grads[rows, upper] = (grad_act * silu).astype(BF16)

    def second_half(rows):
        @pl.loop(0, width // tile)
        def _(d):
            span = pl.ds(pl.multiple_of(d * tile, tile), tile)
            lower = pl.ds(pl.multiple_of(width + d * tile, tile), tile)
            sending[rows, span] = (
                nt(grads[rows, 0:hidden], gate_up[span, :]) + nt(grads[rows, hidden:], gate_up[lower, :])
            ).astype(BF16)

    both = jnp.minimum(me, n - 1 - me)
    long_side = jnp.where(me < n - 1 - me, 1, -1)

    def chunk_at(k):
        near = (k + 1) // 2 * (-1 if k % 2 else 1)
        return me + jnp.where(k <= 2 * both, near, (k - both) * long_side)

    def chunk_rows(k):
        return rows_of(chunk_at(k) if k else me)

    def put_mixed(k):
        return pltpu.make_async_copy(mixed, mixed_out.at[chunk_rows(k)], mixed_sems)

    def mix(k):
        if k:
            put_mixed(k - 1).wait()

        @pl.loop(0, width // tile)
        def _(d):
            span = pl.ds(pl.multiple_of(d * tile, tile), tile)
            mixed[:, span] = nn(acts[chunk_rows(k), :], down[:, span]).astype(BF16)

        put_mixed(k).start()

    for f in range(per):
        for load in weights[f]:
            load.wait()
        if f == 0:
            cot_load.wait()
        first_half(rows_of(me), f)
    second_half(rows_of(me))

    for k in range(1, n):
        mix(k - 1)
        for way in range(2):
            j = me - k if way == 0 else me + k
            there = (me >= k) if way == 0 else (me + k <= n - 1)

            @pl.when(there)
            def _(way=way, j=j):
                gather_arrival(way, j).wait()

                @pl.when(ends[way])
                def _():
                    gather(way, j).start()

        rows = chunk_rows(k)

        @pl.loop(0, per)
        def _(f):
            first_half(rows, f)

        second_half(rows)
        for way in range(2):

            @pl.when(place[way] == 0)
            def _(way=way):
                j = me + k if way == 0 else me - k
                for q in range(cut):
                    pass_on(way, j, q).start()

    room = 3 * block
    half = dp // 4
    items = dp // 2 * 2 * per

    def put(pair, j):
        start = pl.multiple_of((lax.rem(pair, 2) * 2 + j) * room, 16)
        return pltpu.make_async_copy(
            gate_up.at[pl.ds(start, room)], grads_out.at[2 * pair + j], out_sems.at[lax.rem(pair, 2), j])

    def weight_item(i):
        pair, f = lax.div(i, 2 * per), lax.rem(i, 2 * per)
        slot = lax.rem(pair, 2)
        other = lax.div(pair, half)

        def turn(source):
            for j in range(2):
                column = 2 * (2 * lax.rem(pair, half) + j) + lax.rem(core + 1 + other, 2)
                span = pl.ds(pl.multiple_of(column * block, block), block)
                turned[pl.ds(j * block, block), :] = source[:, span].T

        def store(row, goal, product):
            for j in range(2):
                start = pl.multiple_of((slot * 2 + j) * room + row * block, 16)
                gate_up[pl.ds(start, block), goal] = product[j * block:(j + 1) * block]

        @pl.when(f == 0)
        def _():
            @pl.when(pair >= 2)
            def _():
                for j in range(2):
                    put(pair - 2, j).wait()

            turn(normed)

        @pl.when(f == per)
        def _():
            turn(cots)

        @pl.when(f < per)
        def _():
            goal = pl.ds(pl.multiple_of(f * tile, tile), tile)
            for row in range(2):
                span = pl.ds(pl.multiple_of(row * hidden + f * tile, tile), tile)
                store(row, goal, nn(turned[...], grads[:, span]).astype(BF16))

        @pl.when(f >= per)
        def _():
            goal = pl.ds(pl.multiple_of((f - per) * tile, tile), tile)
            store(2, goal, nn(turned[...], acts[:, goal]).astype(BF16))

        @pl.when(f == 2 * per - 1)
        def _():
            for j in range(2):
                put(pair, j).start()

    first_step, last_step = cut + 1, cut * (n - 1) + n - 2
    every = -(-items // (last_step - first_step))

    def serve(step):
        for way in range(2):
            count = step - place[way]
            j_place = lax.div(count, cut) + 1
            q = lax.rem(count, cut)
            j = j_place if way == 0 else n - 1 - j_place

            @pl.when((place[way] > 0) & (j_place > place[way]) & (j_place < n))
            def _(way=way, j=j, q=q):
                sum_arrival(way, j, q, j).wait()
                rows = pl.ds(pl.multiple_of(j * share + q * piece, 16), piece)
                sending[rows, :] = (sending[rows, :].astype(F32) + arriving[rows, :].astype(F32)).astype(BF16)
                pass_on(way, j, q).start()

    @pl.loop(first_step, last_step)
    def _(step):
        serve(step)
        for j in range(every):
            item = (step - first_step) * every + j

            @pl.when(item < items)
            def _(item=item):
                weight_item(item)


    mix(n - 1)

    for way in range(2):

        @pl.when(place[way] > 0)
        def _(way=way):
            for q in range(cut):
                slot = n if way else me
                sum_arrival(way, me, q, slot).wait()
            slot = pl.ds(n * share, share) if way else rows_of(me)

            @pl.loop(0, width // tile)
            def _(d):
                span = pl.ds(pl.multiple_of(d * tile, tile), tile)
                sending[rows_of(me), span] = (
                    sending[rows_of(me), span].astype(F32) + arriving[slot, span].astype(F32)
                ).astype(BF16)

    final = pltpu.make_async_copy(sending.at[rows_of(me)], sum_out, load_sems.at[0])
    final.start()
    for pair in (dp // 2 - 2, dp // 2 - 1):
        for j in range(2):
            put(pair, j).wait()
    put_mixed(n - 1).wait()
    final.wait()
    for way in range(2):

        @pl.when(ends[way])
        def _(way=way):
            @pl.loop(0, n)
            def _(j):
                mine = (j <= me) if way == 0 else (j >= me)

                @pl.when(mine)
                def _():
                    gather(way, j).wait_send()

                @pl.when(jnp.logical_not(mine))
                def _():
                    for q in range(cut):
                        pass_on(way, j, q).wait_send()


def feed_forward(normed, cotangent, gate_up, down, n, dp, tile=512, cut=4):
    share, width = normed.shape
    hidden = down.shape[0]
    tokens = n * share
    block = width // dp
    anywhere = pl.BlockSpec(memory_space=pl.ANY)
    return pl.pallas_call(
        partial(feed_kernel, n, dp, tile, cut),
        out_shape=(
            jax.ShapeDtypeStruct((share, width), BF16),
            jax.ShapeDtypeStruct((tokens, width), BF16),
            jax.ShapeDtypeStruct((dp, 3 * block, hidden), BF16),
        ),
        in_specs=[anywhere] * 4,
        out_specs=(anywhere,) * 3,
        scratch_shapes=[
            pltpu.VMEM((2 * width, hidden), BF16),
            pltpu.VMEM((hidden, width), BF16),
            pltpu.VMEM((tokens, width), BF16),
            pltpu.VMEM((tokens, width), BF16),
            pltpu.VMEM((tokens, hidden), BF16),
            pltpu.VMEM((tokens, 2 * hidden), BF16),
            pltpu.VMEM((tokens + share, width), BF16),
            pltpu.VMEM((tokens, width), BF16),
            pltpu.VMEM((share, width), BF16),
            pltpu.VMEM((2 * block, tokens), BF16),
            pltpu.SemaphoreType.DMA((2,)),
            pltpu.SemaphoreType.DMA((3, hidden // tile)),
            pltpu.SemaphoreType.DMA((2, 2)),
            pltpu.SemaphoreType.DMA((2, n)),
            pltpu.SemaphoreType.DMA((2, n)),
            pltpu.SemaphoreType.DMA((2, n * cut)),
            pltpu.SemaphoreType.DMA((2, n * cut)),
            pltpu.SemaphoreType.DMA,
        ],
        compiler_params=pltpu.CompilerParams(
            collective_id=0, has_side_effects=True, vmem_limit_bytes=60 * 2**20),
        cost_estimate=pl.CostEstimate(
            flops=18 * tokens * width * hidden, bytes_accessed=2 * 24 * 2**20, transcendentals=tokens * hidden),
        name="feed_forward",
    )(normed, cotangent, gate_up, down)


def ring(size, shift=1):
    return [(i, (i + shift) % size) for i in range(size)]


def flip(size, bit):
    return [(i, i ^ (1 << bit)) for i in range(size)]


def pick(array, index, axis):
    return lax.dynamic_index_in_dim(array, index, axis, keepdims=False)


def chunk_of(array, index, rows, axis):
    return lax.dynamic_slice_in_dim(array, index * rows, rows, axis)


def ring_sum(parts):
    size = len(parts)
    running = parts[1].astype(BF16)
    for step in range(2, size + 1):
        arrived = lax.ppermute(running, "tensor", ring(size)).astype(F32)
        running = arrived + parts[step % size].astype(F32)
        if step < size:
            running = running.astype(BF16)
    return running


def bits_of(size):
    return size.bit_length() - 1


def halve(current, axis, order):
    size = lax.axis_size("dp")
    mine = lax.axis_index("dp")
    remaining = sorted(order, reverse=True)
    shape = current.shape
    current = current.reshape(shape[:axis] + (2,) * len(remaining) + shape[axis + 1:])
    for place, bit in enumerate(order):
        where = axis + remaining.index(bit)
        own = (mine >> bit) & 1
        arrived = lax.ppermute(pick(current, 1 - own, where), "dp", flip(size, bit))
        current = pick(current, own, where).astype(F32) + arrived.astype(F32)
        remaining.remove(bit)
        if place < len(order) - 1:
            current = current.astype(BF16)
    return current


def scatter_dp(other, own):
    size = lax.axis_size("dp")
    arrived = lax.ppermute(other.astype(BF16), "dp", flip(size, 0))
    current = (own.astype(F32) + arrived.astype(F32)).astype(BF16)
    rest = list(range(1, bits_of(size)))
    half = current.shape[1] // 2
    first = halve(current[:, :half], 0, rest)
    second = halve(current[:, half:], 0, rest[::-1])
    return jnp.concatenate([first, second], axis=0)


def scatter_small(blocks, over_tensor):
    size = lax.axis_size("dp")
    for bit in reversed(range(bits_of(size))):
        own = (lax.axis_index("dp") >> bit) & 1
        blocks = blocks.reshape((2, blocks.shape[0] // 2) + blocks.shape[1:])
        blocks = pick(blocks, own, 0) + lax.ppermute(pick(blocks, 1 - own, 0), "dp", flip(size, bit))
    blocks = blocks[0]
    if over_tensor:
        size = lax.axis_size("tensor")
        for bit in reversed(range(bits_of(size))):
            own = (lax.axis_index("tensor") >> bit) & 1
            blocks = blocks.reshape((2, blocks.shape[0] // 2) + blocks.shape[1:])
            blocks = pick(blocks, own, 0) + lax.ppermute(
                pick(blocks, 1 - own, 0), "tensor", flip(size, bit)
            )
        blocks = blocks[0]
    return blocks


def gather_weight(shard):
    piece = chunk_of(shard, lax.axis_index("dp"), shard.shape[0] // lax.axis_size("dp"), 0)
    whole = lax.all_gather(piece, ("tensor", "dp"), axis=0, tiled=True)
    return whole.reshape((lax.axis_size("tensor"),) + shard.shape)


def exchange(parts, shift):
    n = lax.axis_size("tensor")
    me = lax.axis_index("tensor")
    came = [parts(me)]
    for s in range(1, n):
        came.append(lax.ppermute(parts((me + s) % n), "tensor", ring(n, s)))
    return came


def by_place(came):
    n = len(came)
    me = lax.axis_index("tensor")
    stacked = jnp.stack(came)
    return [pick(stacked, (me + n - j) % n, 0) for j in range(n)]


def local(
    tokens,
    cotangent,
    segments,
    norm_gains,
    w_qkv,
    qkv_down,
    query_key_value_up,
    feature_maps,
    w_out,
    o_down,
    o_up,
    w_gate_up,
    w_down,
):
    token_rows, model_width = tokens.shape
    groups = w_qkv.shape[1]
    heads = HEADS // KVH
    query_width = heads * HEAD_SIZE
    joined_width = w_qkv.shape[2]
    rank = o_up.shape[0]
    dp = lax.axis_size("dp")
    n = lax.axis_size("tensor")
    me = lax.axis_index("tensor")
    share = token_rows // n
    gains = norm_gains.astype(F32)
    cosines, sines = rotary_tables_t(token_rows, HEAD_SIZE)
    dot = partial(jnp.einsum, preferred_element_type=F32)

    up = query_key_value_up.astype(BF16)
    edges = ((0, query_width), (query_width, query_width + HEAD_SIZE), (query_width + HEAD_SIZE, joined_width))
    up_wide = jnp.stack(
        [jnp.pad(up[:, :, a:b], ((0, 0), (0, 0), (a, joined_width - b))) for a, b in edges]
    )
    w_joined = (
        jnp.transpose(w_qkv, (1, 2, 0)).astype(F32) + dot("jrkc,jrd->kcd", up_wide, qkv_down)
    ).astype(BF16).reshape(groups * joined_width, model_width)
    down_flat = o_down.reshape(rank, -1)
    w_branch = (w_out.astype(F32) + dot("rc,rd->cd", down_flat, o_up)).astype(BF16)
    down_all = lax.all_gather(down_flat, "tensor")
    all_branch = gather_weight(w_branch)
    all_joined = gather_weight(w_joined)

    _, _, normed_one = normalize(tokens.astype(F32), gains[0])
    lowrank = dot("td,jrd->tjr", normed_one, qkv_down)
    joined = dot("cd,td->ct", w_joined, normed_one).reshape(groups, joined_width, token_rows)
    maps_t = jnp.swapaxes(feature_maps, 1, 2)
    maps = jnp.stack(
        [feature_maps[:, :, i * HEAD_SIZE:(i + 1) * HEAD_SIZE] for i in range(heads + 1)], axis=1
    )
    seg_row = segments.reshape(1, token_rows)
    seg_col = segments.reshape(token_rows, 1)
    low, attended, root = attention_forward(joined, cosines, sines, maps_t, seg_row, seg_col, heads)
    attended_flat = attended.reshape(groups * query_width, token_rows)
    att_came = exchange(lambda j: chunk_of(attended_flat, j, share, 1), 1)
    att_share = jnp.stack(by_place(att_came))
    lowrank_out = dot("nct,nrc->tr", att_share, down_all)
    tokens_share = chunk_of(tokens, me, share, 0).astype(F32)
    hidden = tokens_share + dot("nct,ncd->td", att_share, all_branch)
    scaled_two, inverse_two, normed_two = normalize(hidden, gains[1])

    grad_normed_two, mixed_parts, grads_feed = feed_forward(
        normed_two, cotangent, jnp.transpose(w_gate_up, (1, 0, 2)), w_down, n, dp
    )
    grad_normed_two = grad_normed_two.astype(F32)
    weighted = grad_normed_two * gains[1]
    grad_hidden = chunk_of(cotangent, me, share, 0).astype(F32) + inverse_two * (
        weighted - scaled_two * jnp.mean(weighted * scaled_two, axis=-1, keepdims=True)
    )
    gain_two = jnp.sum(grad_normed_two * scaled_two, axis=0)
    grad_branch = grad_hidden.astype(BF16)

    grad_att_share = dot("ncd,td->nct", all_branch, grad_branch).astype(BF16)
    back = by_place(exchange(lambda j: pick(grad_att_share, j, 0), 1))
    grad_attended = jnp.concatenate(back, axis=1).reshape(groups, query_width, token_rows)
    mixed = ring_sum([chunk_of(mixed_parts, (me + n - s) % n, share, 0) for s in range(n)])
    output = (hidden + mixed).astype(BF16)

    grad_joined, grad_maps = attention_backward(
        low, cosines, sines, maps_t, maps, seg_row, seg_col, attended, root, grad_attended, heads
    )
    flat_joined = grad_joined.reshape(groups * joined_width, token_rows)
    joined_share = jnp.stack(by_place(exchange(lambda j: chunk_of(flat_joined, j, share, 1), 1)))
    grad_normed_one = dot("nct,ncd->td", joined_share, all_joined)
    scaled_one, inverse_one, _ = normalize(tokens_share, gains[0])
    weighted = grad_normed_one * gains[0]
    grad_input = (
        grad_hidden
        + inverse_one
        * (weighted - scaled_one * jnp.mean(weighted * scaled_one, axis=-1, keepdims=True))
    ).astype(BF16)
    gain_one = jnp.sum(grad_normed_one * scaled_one, axis=0)

    width = model_width // dp
    core = lax.axis_index("dp") & 1

    def of_core(array, which):
        return jnp.concatenate([chunk_of(array, 2 * q + which, width, 1) for q in range(dp // 2)], axis=1)

    def blocks_of(product):
        return product.astype(BF16).reshape(dp // 2, width, -1)

    out_feed = scatter_dp(grads_feed[:dp // 2], grads_feed[dp // 2:]).reshape(3, width, -1)
    out_gate_up = jnp.transpose(out_feed[:2], (1, 0, 2))
    out_down = out_feed[2].T
    flat_att = jnp.concatenate(att_came, axis=0)
    out_branch = scatter_dp(
        *[blocks_of(dot("tb,ct->bc", of_core(grad_branch, which), flat_att)) for which in (1 - core, core)]
    )
    out_branch = ring_sum([chunk_of(out_branch, s, groups * query_width, 1) for s in range(n)]).T
    out_qkv = scatter_dp(
        *[blocks_of(dot("tb,ct->bc", of_core(normed_one, which), flat_joined)) for which in (1 - core, core)]
    ).reshape(width, groups, joined_width)

    lowrank_low = lowrank.astype(BF16)
    grad_up = jnp.concatenate(
        [dot("tr,kct->rkc", lowrank_low[:, j], grad_joined[:, a:b]) for j, (a, b) in enumerate(edges)],
        axis=2,
    )
    grad_maps = jnp.transpose(grad_maps, (0, 2, 1, 3)).reshape(groups, HEAD_SIZE, -1)
    small = jnp.concatenate(
        [
            jnp.moveaxis(grad_up.reshape(rank, groups, dp, -1), 2, 0).reshape(dp, -1),
            jnp.moveaxis(grad_maps.reshape(groups, HEAD_SIZE, dp, -1), 2, 0).reshape(dp, -1),
        ],
        axis=1,
    )
    small = scatter_small(small, False)
    cut = rank * groups * (joined_width // dp)
    out_up = small[:cut].reshape(rank, groups, -1)
    out_maps = small[cut:].reshape(groups, HEAD_SIZE, -1)

    grad_lowrank = dot("kct,jrkc->jrt", grad_joined, up_wide).astype(BF16)
    grad_qkv_down = dot("jrt,td->jrd", grad_lowrank, normed_one)
    grad_lowrank_out = dot("td,rd->tr", grad_branch, o_up).astype(BF16)
    grad_o_up = dot("tr,td->rd", lowrank_out.astype(BF16), grad_branch)
    grad_o_down = dot("tr,nct->nrc", grad_lowrank_out, att_share)
    shared = jnp.concatenate(
        [gain_one[None], gain_two[None], grad_qkv_down.reshape(-1, model_width), grad_o_up], axis=0
    )
    lines = shared.shape[0]
    shared = jnp.transpose(shared.reshape(lines, dp, n, -1), (1, 2, 0, 3)).reshape(dp, n, -1)
    downs = grad_o_down.reshape(n, rank, groups, dp, -1)
    downs = jnp.transpose(downs, (3, 0, 1, 2, 4)).reshape(dp, n, -1)
    cut = shared.shape[2]
    packed = scatter_small(jnp.concatenate([shared, downs], axis=2), True)
    shared = packed[:cut].reshape(lines, -1)
    out_o_down = packed[cut:].reshape(rank, groups, -1)
    return (
        output,
        grad_input,
        shared[:2],
        out_qkv,
        shared[2:lines - rank].reshape(3, rank, -1),
        out_up,
        out_maps,
        out_branch,
        out_o_down,
        shared[lines - rank:],
        out_gate_up,
        out_down,
    )


def solution(mesh):
    in_specs = (
        P("dp", None),
        P("dp", None),
        P("dp", None),
        P(),
        P(None, "tensor", None),
        P(),
        P(None, "tensor", None),
        P("tensor", None, None),
        P("tensor", None),
        P(None, "tensor", None),
        P(),
        P(None, None, "tensor"),
        P("tensor", None),
    )
    out_specs = (
        P(("dp", "tensor"), None),
        P(("dp", "tensor"), None),
        P(None, ("dp", "tensor")),
        P("dp", "tensor", None),
        P(None, None, ("dp", "tensor")),
        P(None, "tensor", "dp"),
        P("tensor", None, "dp"),
        P("tensor", "dp"),
        P(None, "tensor", "dp"),
        P(None, ("dp", "tensor")),
        P("dp", None, "tensor"),
        P("tensor", "dp"),
    )
    return jax.shard_map(
        local, mesh=mesh, in_specs=in_specs, out_specs=out_specs, check_vma=False
    )
```

```python
from functools import partial
import jax, jax.numpy as jnp
from jax import lax
from jax.experimental import pallas as pl
from jax.experimental.pallas import tpu as pltpu
from jax.sharding import PartitionSpec as P

HEADS = 32
KVH = 8
HEAD_SIZE = 64
WINDOW = 64
LONGEST = 512
epsilon = 1e-05
rope_base = 500000.0
F32 = jnp.float32
BF16 = jnp.bfloat16


def nn(a, b):
    return lax.dot_general(a, b, (((1,), (0,)), ((), ())), preferred_element_type=F32)


def nt(a, b):
    return lax.dot_general(a, b, (((1,), (1,)), ((), ())), preferred_element_type=F32)


def rotate_t(part, cosines, sines):
    half = part.shape[0] // 2
    a, b = part[:half], part[half:]
    return jnp.concatenate([a * cosines - b * sines, b * cosines + a * sines], axis=0)


def rotate_back_t(part, cosines, sines):
    half = part.shape[0] // 2
    a, b = part[:half], part[half:]
    return jnp.concatenate([a * cosines + b * sines, b * cosines - a * sines], axis=0)


def softmaxes_t(logits):
    up = jnp.exp(logits - jnp.max(logits, axis=0, keepdims=True))
    down = jnp.exp(jnp.min(logits, axis=0, keepdims=True) - logits)
    up = up * (1.0 / jnp.sum(up, axis=0, keepdims=True))
    down = down * (1.0 / jnp.sum(down, axis=0, keepdims=True))
    return up, down


def tile_plan(length, block):
    back = LONGEST // block
    return [(i, list(range(max(0, i - back), i + 1))) for i in range(length // block)]


def tile_masks(same, query_block, key_block, block):
    lowest = (query_block - key_block) * block - (block - 1)
    if lowest >= WINDOW:
        return None, same
    shape = (block, block)
    distance = (
        lax.broadcasted_iota(jnp.int32, shape, 1)
        - lax.broadcasted_iota(jnp.int32, shape, 0)
        + (query_block - key_block) * block
    )
    inside = same & (distance < WINDOW)
    if lowest < 0:
        inside = inside & (distance >= 0)
    return inside, same & (distance >= WINDOW)


def forward_kernel(heads, block, joined_ref, cos_ref, sin_ref, map_ref, row_ref, col_ref,
                   low_ref, att_ref, root_ref, keys, kfeat):
    length = cos_ref.shape[1]
    width = heads * HEAD_SIZE
    scale = HEAD_SIZE ** -0.5
    key_t = rotate_t(joined_ref[0, width:width + HEAD_SIZE], cos_ref[...], sin_ref[...]).astype(BF16)
    low_ref[0, width:width + HEAD_SIZE] = key_t
    value_t = joined_ref[0, width + HEAD_SIZE:].astype(BF16)
    low_ref[0, width + HEAD_SIZE:] = value_t
    up, down = softmaxes_t(nn(map_ref[0, width:], key_t))
    kfeat[...] = jnp.concatenate([up, down], axis=0).T.astype(BF16)
    keys[...] = key_t.astype(F32).T.astype(BF16)

    for i, tiles in tile_plan(length, block):
        cols = slice(i * block, (i + 1) * block)

        def one_head(h, carry, i=i, tiles=tiles, cols=cols):
            rows = pl.ds(pl.multiple_of(h * HEAD_SIZE, HEAD_SIZE), HEAD_SIZE)
            query = rotate_t(joined_ref[0, rows, cols], cos_ref[:, cols], sin_ref[:, cols]).astype(BF16)
            low_ref[0, rows, cols] = query
            up, down = softmaxes_t(nn(map_ref[0, rows], query))
            feat = jnp.concatenate([up, down], axis=0).astype(BF16)
            weights = []
            total = None
            for j in tiles:
                span = slice(j * block, (j + 1) * block)
                same = col_ref[span, :] == row_ref[:, cols]
                inside, far = tile_masks(same, i, j, block)
                linear = nn(kfeat[span, :], feat)
                w = jnp.where(far, linear, 0.0)
                if inside is not None:
                    w = jnp.where(inside, jnp.exp(nn(keys[span, :], query) * scale), w)
                part = jnp.sum(w, axis=0, keepdims=True)
                total = part if total is None else total + part
                weights.append(w)
            root = lax.rsqrt(total)
            root_ref[0, h, :, cols] = root
            att = None
            for j, w in zip(tiles, weights):
                p = (w * root * root).astype(BF16)
                piece = nn(low_ref[0, width + HEAD_SIZE:, j * block:(j + 1) * block], p)
                att = piece if att is None else att + piece
            att_ref[0, rows, cols] = att.astype(BF16)
            return carry

        lax.fori_loop(0, heads, one_head, 0)


def attention_forward(joined_t, cosines, sines, maps_t, seg_row, seg_col, heads, block=256):
    groups, width, length = joined_t.shape
    qw = heads * HEAD_SIZE
    whole = lambda shape: pl.BlockSpec(shape, lambda g: (0,) * len(shape))
    mine = lambda shape: pl.BlockSpec((1,) + shape, lambda g: (g,) + (0,) * len(shape))
    return pl.pallas_call(
        partial(forward_kernel, heads, block),
        grid=(groups,),
        out_shape=(
            jax.ShapeDtypeStruct((groups, width, length), BF16),
            jax.ShapeDtypeStruct((groups, qw, length), BF16),
            jax.ShapeDtypeStruct((groups, heads, 1, length), F32),
        ),
        in_specs=[mine((width, length)), whole(cosines.shape), whole(sines.shape),
                  mine(maps_t.shape[1:]), whole(seg_row.shape), whole(seg_col.shape)],
        out_specs=(mine((width, length)), mine((qw, length)), mine((heads, 1, length))),
        scratch_shapes=[pltpu.VMEM((length, HEAD_SIZE), BF16), pltpu.VMEM((length, 2 * HEAD_SIZE), BF16)],
        compiler_params=pltpu.CompilerParams(vmem_limit_bytes=48 * 2**20),
        cost_estimate=pl.CostEstimate(flops=22 * 10**9, bytes_accessed=10**7, transcendentals=10**6),
        name="attention_forward",
    )(joined_t, cosines, sines, maps_t, seg_row, seg_col)


def backward_kernel(heads, block, low_ref, cos_ref, sin_ref, map_ref, back_ref, row_ref, col_ref,
                    att_ref, root_ref, gatt_ref, grad_ref, gmap_ref,
                    keys, kfeat, kfeat_t, values, gkeys, gkfeat, gvalues):
    length = cos_ref.shape[1]
    width = heads * HEAD_SIZE
    scale = HEAD_SIZE ** -0.5
    key_t = low_ref[0, width:width + HEAD_SIZE]
    key_up, key_down = softmaxes_t(nn(map_ref[0, width:], key_t))
    both = jnp.concatenate([key_up, key_down], axis=0)
    kfeat_t[...] = both.astype(BF16)
    kfeat[...] = both.T.astype(BF16)
    keys[...] = key_t.astype(F32).T.astype(BF16)
    values[...] = low_ref[0, width + HEAD_SIZE:].astype(F32).T.astype(BF16)
    gkeys[...] = jnp.zeros_like(gkeys)
    gkfeat[...] = jnp.zeros_like(gkfeat)
    gvalues[...] = jnp.zeros_like(gvalues)
    gmap_ref[...] = jnp.zeros_like(gmap_ref)

    for i, tiles in tile_plan(length, block):
        cols = slice(i * block, (i + 1) * block)

        def one_head(h, carry, i=i, tiles=tiles, cols=cols):
            rows = pl.ds(pl.multiple_of(h * HEAD_SIZE, HEAD_SIZE), HEAD_SIZE)
            query = low_ref[0, rows, cols]
            gatt = gatt_ref[0, rows, cols]
            up, down = softmaxes_t(nn(map_ref[0, rows], query))
            feat = jnp.concatenate([up, down], axis=0).astype(BF16)
            root = root_ref[0, h, :, cols]
            inverse = root * root
            delta = jnp.sum(gatt.astype(F32) * att_ref[0, rows, cols].astype(F32), axis=0, keepdims=True)
            gquery = jnp.zeros((HEAD_SIZE, block), F32)
            gfeat = jnp.zeros((2 * HEAD_SIZE, block), F32)
            for j in tiles:
                span = slice(j * block, (j + 1) * block)
                same = col_ref[span, :] == row_ref[:, cols]
                inside, far = tile_masks(same, i, j, block)
                gprob = nn(values[span, :], gatt) - delta
                grad_far = jnp.where(far, gprob * root * root, 0.0).astype(BF16)
                p = jnp.where(far, nn(kfeat[span, :], feat) * root * root, 0.0)
                if inside is not None:
                    near = jnp.where(inside, jnp.exp(nn(keys[span, :], query) * scale) * root * root, 0.0)
                    p = jnp.where(inside, near, p)
                    grad_near = (near * gprob * scale).astype(BF16)
                    gquery = gquery + nn(low_ref[0, width:width + HEAD_SIZE, span], grad_near)
                    gkeys[span, :] += nt(grad_near, query)
                gvalues[span, :] += nt(p.astype(BF16), gatt)
                gfeat = gfeat + nn(kfeat_t[:, span], grad_far)
                gkfeat[span, :] += nt(grad_far, feat)
            glogits = softmaxes_back_t(up, down, gfeat)
            gquery = gquery + nn(back_ref[0, h], glogits)
            gmap_ref[0, h] += nt(query, glogits)
            grad_ref[0, rows, cols] = rotate_back_t(gquery, cos_ref[:, cols], sin_ref[:, cols]).astype(BF16)
            return carry

        lax.fori_loop(0, heads, one_head, 0)
    glogits = softmaxes_back_t(key_up, key_down, gkfeat[...].T)
    gkey_t = gkeys[...].T + nn(back_ref[0, heads], glogits)
    gmap_ref[0, heads] = nt(key_t, glogits)
    grad_ref[0, width:width + HEAD_SIZE] = rotate_back_t(gkey_t, cos_ref[...], sin_ref[...]).astype(BF16)
    grad_ref[0, width + HEAD_SIZE:] = gvalues[...].T.astype(BF16)


def softmaxes_back_t(up, down, grads):
    gup, gdown = grads[:HEAD_SIZE], grads[HEAD_SIZE:]
    return (
        up * (gup - jnp.sum(gup * up, axis=0, keepdims=True))
        - down * (gdown - jnp.sum(gdown * down, axis=0, keepdims=True))
    ).astype(BF16)


def attention_backward(low, cosines, sines, maps_t, maps, seg_row, seg_col, att, root, gatt, heads, block=256):
    groups, width, length = low.shape
    qw = heads * HEAD_SIZE
    whole = lambda shape: pl.BlockSpec(shape, lambda g: (0,) * len(shape))
    mine = lambda shape: pl.BlockSpec((1,) + shape, lambda g: (g,) + (0,) * len(shape))
    return pl.pallas_call(
        partial(backward_kernel, heads, block),
        grid=(groups,),
        out_shape=(
            jax.ShapeDtypeStruct((groups, width, length), BF16),
            jax.ShapeDtypeStruct((groups, heads + 1, HEAD_SIZE, HEAD_SIZE), F32),
        ),
        in_specs=[mine((width, length)), whole(cosines.shape), whole(sines.shape),
                  mine(maps_t.shape[1:]), mine(maps.shape[1:]), whole(seg_row.shape), whole(seg_col.shape),
                  mine((qw, length)), mine((heads, 1, length)), mine((qw, length))],
        out_specs=(mine((width, length)), mine((heads + 1, HEAD_SIZE, HEAD_SIZE))),
        scratch_shapes=[
            pltpu.VMEM((length, HEAD_SIZE), BF16), pltpu.VMEM((length, 2 * HEAD_SIZE), BF16),
            pltpu.VMEM((2 * HEAD_SIZE, length), BF16), pltpu.VMEM((length, HEAD_SIZE), BF16),
            pltpu.VMEM((length, HEAD_SIZE), F32), pltpu.VMEM((length, 2 * HEAD_SIZE), F32),
            pltpu.VMEM((length, HEAD_SIZE), F32)],
        compiler_params=pltpu.CompilerParams(vmem_limit_bytes=48 * 2**20),
        cost_estimate=pl.CostEstimate(flops=40 * 10**9, bytes_accessed=10**7, transcendentals=10**6),
        name="attention_backward",
    )(low, cosines, sines, maps_t, maps, seg_row, seg_col, att, root, gatt)


def rotary_tables_t(length, width):
    half = width // 2
    frequency = rope_base ** (-(jnp.arange(half, dtype=F32) * 2.0) / width)
    angles = frequency[:, None] * jnp.arange(length, dtype=F32)[None, :]
    return jnp.cos(angles), jnp.sin(angles)


def normalize(values, gain_row):
    inverse = lax.rsqrt(jnp.mean(values * values, axis=-1, keepdims=True) + epsilon)
    scaled = values * inverse
    return scaled, inverse, (scaled * gain_row).astype(BF16)


def feed_kernel(
    n, dp, tile, cut,
    normed_in, cot_in, gate_up_in, down_in,
    sum_out, mixed_out, came, first_send, first_keep, second_send, second_keep,
    gate_up, down, normed, cots, acts, grads, arriving, sending, mixed, turned,
    load_sems, weight_sems, out_sems, core_send, core_recv, fill_sems, gather_send, gather_recv, sum_send, sum_recv, mixed_sems,
):
    share, width = normed_in.shape
    hidden = down_in.shape[0]
    block = width // dp
    piece = share // cut
    per = hidden // tile
    me = lax.axis_index("tensor")
    mine = lax.axis_index("dp")
    core = lax.rem(mine, 2)
    mate = {"dp": mine + 1 - 2 * core}
    place = (me, n - 1 - me)
    ends = (me < n - 1, me > 0)
    partner = (me + 1, me - 1)

    def device(way):
        return {"tensor": partner[way]}

    def rows_of(j, size=share):
        return pl.ds(pl.multiple_of(j * share, 16), size)

    barrier = pltpu.get_barrier_semaphore()
    for way in range(2):

        @pl.when(ends[way])
        def _(way=way):
            pl.semaphore_signal(barrier, inc=1, device_id=device(way), device_id_type=pl.DeviceIdType.MESH)

    pl.semaphore_signal(barrier, inc=1, device_id=mate, device_id_type=pl.DeviceIdType.MESH)
    own_load = pltpu.make_async_copy(normed_in, normed.at[rows_of(me)], load_sems.at[0])
    cot_load = pltpu.make_async_copy(cot_in, cots, load_sems.at[1])
    own_load.start()

    def weight_loads(f):
        span = slice(f * tile, (f + 1) * tile)
        return (
            pltpu.make_async_copy(gate_up_in.at[0, :, span], gate_up.at[0:width, span], weight_sems.at[0, f]),
            pltpu.make_async_copy(gate_up_in.at[1, :, span], gate_up.at[width:2 * width, span], weight_sems.at[1, f]),
            pltpu.make_async_copy(down_in.at[span], down.at[span], weight_sems.at[2, f]),
        )

    weights = [weight_loads(f) for f in range(per)]
    for load in weights[0]:
        load.start()
    cot_load.start()
    for loads in weights[1:]:
        for load in loads:
            load.start()
    inner = (me > 0) & (me < n - 1)

    @pl.when(inner)
    def _():
        pl.semaphore_wait(barrier, 3)

    @pl.when(jnp.logical_not(inner))
    def _():
        pl.semaphore_wait(barrier, 2)

    def gather(way, j):
        return pltpu.make_async_remote_copy(
            src_ref=normed.at[rows_of(j)], dst_ref=normed.at[rows_of(j)],
            send_sem=gather_send.at[way, j], recv_sem=gather_recv.at[way, j],
            device_id=device(way), device_id_type=pl.DeviceIdType.MESH)

    def gather_arrival(way, j):
        return pltpu.make_async_copy(normed.at[rows_of(j)], normed.at[rows_of(j)], gather_recv.at[way, j])

    def pass_on(way, j, q):
        rows = pl.ds(pl.multiple_of(j * share + q * piece, 16), piece)
        last = j == partner[way]
        slot = jnp.where(last, n, j) if way else j
        goal = pl.ds(pl.multiple_of(slot * share + q * piece, 16), piece)
        return pltpu.make_async_remote_copy(
            src_ref=sending.at[rows], dst_ref=arriving.at[goal],
            send_sem=sum_send.at[way, j * cut + q], recv_sem=sum_recv.at[way, j * cut + q],
            device_id=device(way), device_id_type=pl.DeviceIdType.MESH)

    def sum_arrival(way, j, q, slot):
        rows = pl.ds(pl.multiple_of(slot * share + q * piece, 16), piece)
        return pltpu.make_async_copy(arriving.at[rows], arriving.at[rows], sum_recv.at[way, j * cut + q])

    own_load.wait()
    for way in range(2):

        @pl.when(ends[way])
        def _(way=way):
            gather(way, me).start()

    def first_half(rows, f):
        span = pl.ds(pl.multiple_of(f * tile, tile), tile)
        upper = pl.ds(pl.multiple_of(hidden + f * tile, tile), tile)
        gate = nn(normed[rows, :], gate_up[0:width, span])
        up = nn(normed[rows, :], gate_up[width:2 * width, span])
        grad_act = nt(cots[rows, :], down[span, :])
        sigma = 1.0 / (1.0 + jnp.exp(-gate))
        silu = gate * sigma
        acts[rows, span] = (silu * up).astype(BF16)
        grads[rows, span] = (grad_act * up * (sigma + silu * (1.0 - sigma))).astype(BF16)
        grads[rows, upper] = (grad_act * silu).astype(BF16)

    def second_half(rows):
        @pl.loop(0, width // tile)
        def _(d):
            span = pl.ds(pl.multiple_of(d * tile, tile), tile)
            lower = pl.ds(pl.multiple_of(width + d * tile, tile), tile)
            sending[rows, span] = (
                nt(grads[rows, 0:hidden], gate_up[span, :]) + nt(grads[rows, hidden:], gate_up[lower, :])
            ).astype(BF16)

    both = jnp.minimum(me, n - 1 - me)
    long_side = jnp.where(me < n - 1 - me, 1, -1)

    def chunk_at(k):
        near = (k + 1) // 2 * (-1 if k % 2 else 1)
        return me + jnp.where(k <= 2 * both, near, (k - both) * long_side)

    def chunk_rows(k):
        return rows_of(chunk_at(k) if k else me)

    def put_mixed(k):
        return pltpu.make_async_copy(mixed, mixed_out.at[chunk_rows(k)], mixed_sems)

    def mix(k):
        if k:
            put_mixed(k - 1).wait()

        @pl.loop(0, width // tile)
        def _(d):
            span = pl.ds(pl.multiple_of(d * tile, tile), tile)
            mixed[:, span] = nn(acts[chunk_rows(k), :], down[:, span]).astype(BF16)

        put_mixed(k).start()

    for f in range(per):
        for load in weights[f]:
            load.wait()
        if f == 0:
            cot_load.wait()
        first_half(rows_of(me), f)
    second_half(rows_of(me))

    for k in range(1, n):
        mix(k - 1)
        for way in range(2):
            j = me - k if way == 0 else me + k
            there = (me >= k) if way == 0 else (me + k <= n - 1)

            @pl.when(there)
            def _(way=way, j=j):
                gather_arrival(way, j).wait()

                @pl.when(ends[way])
                def _():
                    gather(way, j).start()

        rows = chunk_rows(k)

        @pl.loop(0, per)
        def _(f):
            first_half(rows, f)

        second_half(rows)
        for way in range(2):

            @pl.when(place[way] == 0)
            def _(way=way):
                j = me + k if way == 0 else me - k
                for q in range(cut):
                    pass_on(way, j, q).start()

    room = 3 * block
    half = dp // 4
    items = dp // 2 * 2 * per

    def staged(pair, j, start=0, size=room):
        first = pl.multiple_of((lax.rem(pair, 2) * 2 + j) * room + start, 16)
        return gate_up.at[pl.ds(first, size)]

    def put_across(pair, j):
        return pltpu.make_async_remote_copy(
            src_ref=staged(pair, j), dst_ref=came.at[2 * pair + j],
            send_sem=core_send.at[pair, j], recv_sem=core_recv.at[pair, j],
            device_id=mate, device_id_type=pl.DeviceIdType.MESH)

    def fill(pair, j):
        return pltpu.make_async_copy(came.at[2 * (pair - half) + j], staged(pair, j), fill_sems.at[j])

    def put_own(pair, j, act):
        q = 2 * (pair - half) + j
        quarter = dp // 4
        rows = room // 2
        place = lax.div(mine, 2)
        for part, (other, keep, slot, goes) in enumerate((
            (first_send, first_keep, lax.div(q, 2), lax.rem(q, 2) != lax.rem(place, 2)),
            (second_send, second_keep, lax.rem(q, quarter), lax.div(q, quarter) != lax.div(place, quarter)),
        )):
            for ref, chosen in ((other, goes), (keep, jnp.logical_not(goes))):

                @pl.when(chosen)
                def _(ref=ref, part=part, slot=slot):
                    copy = pltpu.make_async_copy(
                        staged(pair, j, part * rows, rows), ref.at[slot], out_sems.at[lax.rem(pair, 2), j, part])
                    if act == "start":
                        copy.start()
                    else:
                        copy.wait()

    def weight_item(i):
        pair, f = lax.div(i, 2 * per), lax.rem(i, 2 * per)
        slot = lax.rem(pair, 2)
        other = lax.div(pair, half)

        def turn(source):
            for j in range(2):
                column = 2 * (2 * lax.rem(pair, half) + j) + lax.rem(core + 1 + other, 2)
                span = pl.ds(pl.multiple_of(column * block, block), block)
                turned[pl.ds(j * block, block), :] = source[:, span].T

        def store(row, goal, product):
            for j in range(2):
                start = pl.multiple_of((slot * 2 + j) * room + row * block, 16)
                rows = pl.ds(start, block)
                part = product[j * block:(j + 1) * block]

                @pl.when(pair < half)
                def _(rows=rows, part=part):
                    gate_up[rows, goal] = part.astype(BF16)

                @pl.when(pair >= half)
                def _(rows=rows, part=part):
                    gate_up[rows, goal] = (gate_up[rows, goal].astype(F32) + part).astype(BF16)

        @pl.when(f == 0)
        def _():
            @pl.when((pair >= 2) & (pair < half))
            def _():
                for j in range(2):
                    put_across(pair - 2, j).wait_send()

            @pl.when(pair >= half)
            def _():
                for j in range(2):
                    fill(pair, j).wait()

            turn(normed)

        @pl.when(f == per)
        def _():
            turn(cots)
            following = pair + 1

            @pl.when((following >= half) & (following < 2 * half))
            def _():
                @pl.when(following - 2 < half)
                def _():
                    for j in range(2):
                        put_across(following - 2, j).wait_send()

                @pl.when(following - 2 >= half)
                def _():
                    for j in range(2):
                        put_own(following - 2, j, "wait")

                for j in range(2):
                    put_across(following - half, j).wait_recv()
                    fill(following, j).start()

        @pl.when(f < per)
        def _():
            goal = pl.ds(pl.multiple_of(f * tile, tile), tile)
            for row in range(2):
                span = pl.ds(pl.multiple_of(row * hidden + f * tile, tile), tile)
                store(row, goal, nn(turned[...], grads[:, span]))

        @pl.when(f >= per)
        def _():
            goal = pl.ds(pl.multiple_of((f - per) * tile, tile), tile)
            store(2, goal, nn(turned[...], acts[:, goal]))

        @pl.when(f == 2 * per - 1)
        def _():
            @pl.when(pair < half)
            def _():
                for j in range(2):
                    put_across(pair, j).start()

            @pl.when(pair >= half)
            def _():
                for j in range(2):
                    put_own(pair, j, "start")

    first_step, last_step = cut + 1, cut * (n - 1) + n - 2
    every = -(-items // (last_step - first_step))

    def serve(step):
        for way in range(2):
            count = step - place[way]
            j_place = lax.div(count, cut) + 1
            q = lax.rem(count, cut)
            j = j_place if way == 0 else n - 1 - j_place

            @pl.when((place[way] > 0) & (j_place > place[way]) & (j_place < n))
            def _(way=way, j=j, q=q):
                sum_arrival(way, j, q, j).wait()
                rows = pl.ds(pl.multiple_of(j * share + q * piece, 16), piece)
                sending[rows, :] = (sending[rows, :].astype(F32) + arriving[rows, :].astype(F32)).astype(BF16)
                pass_on(way, j, q).start()

    @pl.loop(first_step, last_step)
    def _(step):
        serve(step)
        for j in range(every):
            item = (step - first_step) * every + j

            @pl.when(item < items)
            def _(item=item):
                weight_item(item)


    mix(n - 1)

    for way in range(2):

        @pl.when(place[way] > 0)
        def _(way=way):
            for q in range(cut):
                slot = n if way else me
                sum_arrival(way, me, q, slot).wait()
            slot = pl.ds(n * share, share) if way else rows_of(me)

            @pl.loop(0, width // tile)
            def _(d):
                span = pl.ds(pl.multiple_of(d * tile, tile), tile)
                sending[rows_of(me), span] = (
                    sending[rows_of(me), span].astype(F32) + arriving[slot, span].astype(F32)
                ).astype(BF16)

    final = pltpu.make_async_copy(sending.at[rows_of(me)], sum_out, load_sems.at[0])
    final.start()
    for pair in (2 * half - 2, 2 * half - 1):
        for j in range(2):
            put_own(pair, j, "wait")
    put_mixed(n - 1).wait()
    final.wait()
    for way in range(2):

        @pl.when(ends[way])
        def _(way=way):
            @pl.loop(0, n)
            def _(j):
                sent = (j <= me) if way == 0 else (j >= me)

                @pl.when(sent)
                def _():
                    gather(way, j).wait_send()

                @pl.when(jnp.logical_not(sent))
                def _():
                    for q in range(cut):
                        pass_on(way, j, q).wait_send()


def feed_forward(normed, cotangent, gate_up, down, n, dp, tile=512, cut=4):
    share, width = normed.shape
    hidden = down.shape[0]
    tokens = n * share
    block = width // dp
    anywhere = pl.BlockSpec(memory_space=pl.ANY)
    return pl.pallas_call(
        partial(feed_kernel, n, dp, tile, cut),
        out_shape=(
            jax.ShapeDtypeStruct((share, width), BF16),
            jax.ShapeDtypeStruct((tokens, width), BF16),
            jax.ShapeDtypeStruct((dp // 2, 3 * block, hidden), BF16),
            jax.ShapeDtypeStruct((dp // 4, 3 * block // 2, hidden), BF16),
            jax.ShapeDtypeStruct((dp // 4, 3 * block // 2, hidden), BF16),
            jax.ShapeDtypeStruct((dp // 4, 3 * block // 2, hidden), BF16),
            jax.ShapeDtypeStruct((dp // 4, 3 * block // 2, hidden), BF16),
        ),
        in_specs=[anywhere] * 4,
        out_specs=(anywhere,) * 7,
        scratch_shapes=[
            pltpu.VMEM((2 * width, hidden), BF16),
            pltpu.VMEM((hidden, width), BF16),
            pltpu.VMEM((tokens, width), BF16),
            pltpu.VMEM((tokens, width), BF16),
            pltpu.VMEM((tokens, hidden), BF16),
            pltpu.VMEM((tokens, 2 * hidden), BF16),
            pltpu.VMEM((tokens + share, width), BF16),
            pltpu.VMEM((tokens, width), BF16),
            pltpu.VMEM((share, width), BF16),
            pltpu.VMEM((2 * block, tokens), BF16),
            pltpu.SemaphoreType.DMA((2,)),
            pltpu.SemaphoreType.DMA((3, hidden // tile)),
            pltpu.SemaphoreType.DMA((2, 2, 2)),
            pltpu.SemaphoreType.DMA((dp // 4, 2)),
            pltpu.SemaphoreType.DMA((dp // 4, 2)),
            pltpu.SemaphoreType.DMA((2,)),
            pltpu.SemaphoreType.DMA((2, n)),
            pltpu.SemaphoreType.DMA((2, n)),
            pltpu.SemaphoreType.DMA((2, n * cut)),
            pltpu.SemaphoreType.DMA((2, n * cut)),
            pltpu.SemaphoreType.DMA,
        ],
        compiler_params=pltpu.CompilerParams(
            collective_id=0, has_side_effects=True, vmem_limit_bytes=60 * 2**20),
        cost_estimate=pl.CostEstimate(
            flops=18 * tokens * width * hidden, bytes_accessed=2 * 24 * 2**20, transcendentals=tokens * hidden),
        name="feed_forward",
    )(normed, cotangent, gate_up, down)


def ring(size, shift=1):
    return [(i, (i + shift) % size) for i in range(size)]


def flip(size, bit):
    return [(i, i ^ (1 << bit)) for i in range(size)]


def pick(array, index, axis):
    return lax.dynamic_index_in_dim(array, index, axis, keepdims=False)


def chunk_of(array, index, rows, axis):
    return lax.dynamic_slice_in_dim(array, index * rows, rows, axis)


def ring_sum(parts):
    size = len(parts)
    running = parts[1].astype(BF16)
    for step in range(2, size + 1):
        arrived = lax.ppermute(running, "tensor", ring(size)).astype(F32)
        running = arrived + parts[step % size].astype(F32)
        if step < size:
            running = running.astype(BF16)
    return running


def bits_of(size):
    return size.bit_length() - 1


def halve(current, axis, order):
    size = lax.axis_size("dp")
    mine = lax.axis_index("dp")
    remaining = sorted(order, reverse=True)
    shape = current.shape
    current = current.reshape(shape[:axis] + (2,) * len(remaining) + shape[axis + 1:])
    for place, bit in enumerate(order):
        where = axis + remaining.index(bit)
        own = (mine >> bit) & 1
        arrived = lax.ppermute(pick(current, 1 - own, where), "dp", flip(size, bit))
        current = pick(current, own, where).astype(F32) + arrived.astype(F32)
        remaining.remove(bit)
        if place < len(order) - 1:
            current = current.astype(BF16)
    return current


def scatter_rest(first_send, first_keep, second_send, second_keep):
    size = lax.axis_size("dp")
    rest = list(range(1, bits_of(size)))
    halves = []
    for send, keep, order in ((first_send, first_keep, rest), (second_send, second_keep, rest[::-1])):
        arrived = lax.ppermute(send, "dp", flip(size, order[0]))
        current = keep.astype(F32) + arrived.astype(F32)
        halves.append(halve(current.astype(BF16), 0, order[1:]) if order[1:] else current[0])
    return jnp.concatenate(halves, axis=0)


def scatter_dp(other, own):
    size = lax.axis_size("dp")
    arrived = lax.ppermute(other.astype(BF16), "dp", flip(size, 0))
    current = own.astype(F32) + arrived.astype(F32)
    rest = list(range(1, bits_of(size)))
    half = current.shape[1] // 2
    parts = []
    for part, order in ((current[:, :half], rest), (current[:, half:], rest[::-1])):
        parts.append(halve(part.astype(BF16), 0, order))
    return jnp.concatenate(parts, axis=0)


def scatter_small(blocks, over_tensor):
    size = lax.axis_size("dp")
    for bit in reversed(range(bits_of(size))):
        own = (lax.axis_index("dp") >> bit) & 1
        blocks = blocks.reshape((2, blocks.shape[0] // 2) + blocks.shape[1:])
        blocks = pick(blocks, own, 0) + lax.ppermute(pick(blocks, 1 - own, 0), "dp", flip(size, bit))
    blocks = blocks[0]
    if over_tensor:
        size = lax.axis_size("tensor")
        for bit in reversed(range(bits_of(size))):
            own = (lax.axis_index("tensor") >> bit) & 1
            blocks = blocks.reshape((2, blocks.shape[0] // 2) + blocks.shape[1:])
            blocks = pick(blocks, own, 0) + lax.ppermute(
                pick(blocks, 1 - own, 0), "tensor", flip(size, bit)
            )
        blocks = blocks[0]
    return blocks


def gather_weight(shard):
    piece = chunk_of(shard, lax.axis_index("dp"), shard.shape[0] // lax.axis_size("dp"), 0)
    whole = lax.all_gather(piece, ("tensor", "dp"), axis=0, tiled=True)
    return whole.reshape((lax.axis_size("tensor"),) + shard.shape)


def exchange(parts, shift):
    n = lax.axis_size("tensor")
    me = lax.axis_index("tensor")
    came = [parts(me)]
    for s in range(1, n):
        came.append(lax.ppermute(parts((me + s) % n), "tensor", ring(n, s)))
    return came


def by_place(came):
    n = len(came)
    me = lax.axis_index("tensor")
    stacked = jnp.stack(came)
    return [pick(stacked, (me + n - j) % n, 0) for j in range(n)]


def local(
    tokens,
    cotangent,
    segments,
    norm_gains,
    w_qkv,
    qkv_down,
    query_key_value_up,
    feature_maps,
    w_out,
    o_down,
    o_up,
    w_gate_up,
    w_down,
):
    token_rows, model_width = tokens.shape
    groups = w_qkv.shape[1]
    heads = HEADS // KVH
    query_width = heads * HEAD_SIZE
    joined_width = w_qkv.shape[2]
    rank = o_up.shape[0]
    dp = lax.axis_size("dp")
    n = lax.axis_size("tensor")
    me = lax.axis_index("tensor")
    share = token_rows // n
    gains = norm_gains.astype(F32)
    cosines, sines = rotary_tables_t(token_rows, HEAD_SIZE)
    dot = partial(jnp.einsum, preferred_element_type=F32)

    up = query_key_value_up.astype(BF16)
    edges = ((0, query_width), (query_width, query_width + HEAD_SIZE), (query_width + HEAD_SIZE, joined_width))
    up_wide = jnp.stack(
        [jnp.pad(up[:, :, a:b], ((0, 0), (0, 0), (a, joined_width - b))) for a, b in edges]
    )
    w_joined = (
        jnp.transpose(w_qkv, (1, 2, 0)).astype(F32) + dot("jrkc,jrd->kcd", up_wide, qkv_down)
    ).astype(BF16).reshape(groups * joined_width, model_width)
    down_flat = o_down.reshape(rank, -1)
    w_branch = (w_out.astype(F32) + dot("rc,rd->cd", down_flat, o_up)).astype(BF16)
    down_all = lax.all_gather(down_flat, "tensor")
    all_branch = gather_weight(w_branch)

    _, _, normed_one = normalize(tokens.astype(F32), gains[0])
    lowrank = dot("td,jrd->tjr", normed_one, qkv_down)
    joined = dot("cd,td->ct", w_joined, normed_one).reshape(groups, joined_width, token_rows)
    maps_t = jnp.swapaxes(feature_maps, 1, 2)
    maps = jnp.stack(
        [feature_maps[:, :, i * HEAD_SIZE:(i + 1) * HEAD_SIZE] for i in range(heads + 1)], axis=1
    )
    seg_row = segments.reshape(1, token_rows)
    seg_col = segments.reshape(token_rows, 1)
    low, attended, root = attention_forward(joined, cosines, sines, maps_t, seg_row, seg_col, heads)
    attended_flat = attended.reshape(groups * query_width, token_rows)
    att_came = exchange(lambda j: chunk_of(attended_flat, j, share, 1), 1)
    att_share = jnp.stack(by_place(att_came))
    lowrank_out = dot("nct,nrc->tr", att_share, down_all)
    tokens_share = chunk_of(tokens, me, share, 0).astype(F32)
    hidden = tokens_share + dot("nct,ncd->td", att_share, all_branch)
    scaled_two, inverse_two, normed_two = normalize(hidden, gains[1])

    grad_normed_two, mixed_parts, _, *grads_feed = feed_forward(
        normed_two, cotangent, jnp.transpose(w_gate_up, (1, 0, 2)), w_down, n, dp
    )
    grad_normed_two = grad_normed_two.astype(F32)
    weighted = grad_normed_two * gains[1]
    grad_hidden = chunk_of(cotangent, me, share, 0).astype(F32) + inverse_two * (
        weighted - scaled_two * jnp.mean(weighted * scaled_two, axis=-1, keepdims=True)
    )
    gain_two = jnp.sum(grad_normed_two * scaled_two, axis=0)
    grad_branch = grad_hidden.astype(BF16)

    grad_att_share = dot("ncd,td->nct", all_branch, grad_branch).astype(BF16)
    back = by_place(exchange(lambda j: pick(grad_att_share, j, 0), 1))
    grad_attended = jnp.concatenate(back, axis=1).reshape(groups, query_width, token_rows)
    mixed = ring_sum([chunk_of(mixed_parts, (me + n - s) % n, share, 0) for s in range(n)])
    output = (hidden + mixed).astype(BF16)

    grad_joined, grad_maps = attention_backward(
        low, cosines, sines, maps_t, maps, seg_row, seg_col, attended, root, grad_attended, heads
    )
    flat_joined = grad_joined.reshape(groups * joined_width, token_rows)
    grad_normed_one = ring_sum(
        [dot("ct,cd->td", chunk_of(flat_joined, (me + n - s) % n, share, 1), w_joined) for s in range(n)]
    )
    scaled_one, inverse_one, _ = normalize(tokens_share, gains[0])
    weighted = grad_normed_one * gains[0]
    grad_input = (
        grad_hidden
        + inverse_one
        * (weighted - scaled_one * jnp.mean(weighted * scaled_one, axis=-1, keepdims=True))
    ).astype(BF16)
    gain_one = jnp.sum(grad_normed_one * scaled_one, axis=0)

    width = model_width // dp
    core = lax.axis_index("dp") & 1

    def of_core(array, which):
        return jnp.concatenate([chunk_of(array, 2 * q + which, width, 1) for q in range(dp // 2)], axis=1)

    def blocks_of(product):
        return product.astype(BF16).reshape(dp // 2, width, -1)

    out_feed = scatter_rest(*grads_feed).reshape(3, width, -1)
    out_gate_up = jnp.transpose(out_feed[:2], (1, 0, 2))
    out_down = out_feed[2].T
    flat_att = jnp.concatenate(att_came, axis=0)
    out_branch = scatter_dp(
        *[blocks_of(dot("tb,ct->bc", of_core(grad_branch, which), flat_att)) for which in (1 - core, core)]
    )
    out_branch = ring_sum([chunk_of(out_branch, s, groups * query_width, 1) for s in range(n)]).T
    out_qkv = scatter_dp(
        *[blocks_of(dot("tb,ct->bc", of_core(normed_one, which), flat_joined)) for which in (1 - core, core)]
    ).reshape(width, groups, joined_width)

    lowrank_low = lowrank.astype(BF16)
    grad_up = jnp.concatenate(
        [dot("tr,kct->rkc", lowrank_low[:, j], grad_joined[:, a:b]) for j, (a, b) in enumerate(edges)],
        axis=2,
    )
    grad_maps = jnp.transpose(grad_maps, (0, 2, 1, 3)).reshape(groups, HEAD_SIZE, -1)
    small = jnp.concatenate(
        [
            jnp.moveaxis(grad_up.reshape(rank, groups, dp, -1), 2, 0).reshape(dp, -1),
            jnp.moveaxis(grad_maps.reshape(groups, HEAD_SIZE, dp, -1), 2, 0).reshape(dp, -1),
        ],
        axis=1,
    )
    small = scatter_small(small, False)
    cut = rank * groups * (joined_width // dp)
    out_up = small[:cut].reshape(rank, groups, -1)
    out_maps = small[cut:].reshape(groups, HEAD_SIZE, -1)

    grad_lowrank = dot("kct,jrkc->jrt", grad_joined, up_wide).astype(BF16)
    grad_qkv_down = dot("jrt,td->jrd", grad_lowrank, normed_one)
    grad_lowrank_out = dot("td,rd->tr", grad_branch, o_up).astype(BF16)
    grad_o_up = dot("tr,td->rd", lowrank_out.astype(BF16), grad_branch)
    grad_o_down = dot("tr,nct->nrc", grad_lowrank_out, att_share)
    shared = jnp.concatenate(
        [gain_one[None], gain_two[None], grad_qkv_down.reshape(-1, model_width), grad_o_up], axis=0
    )
    lines = shared.shape[0]
    shared = jnp.transpose(shared.reshape(lines, dp, n, -1), (1, 2, 0, 3)).reshape(dp, n, -1)
    downs = grad_o_down.reshape(n, rank, groups, dp, -1)
    downs = jnp.transpose(downs, (3, 0, 1, 2, 4)).reshape(dp, n, -1)
    cut = shared.shape[2]
    packed = scatter_small(jnp.concatenate([shared, downs], axis=2), True)
    shared = packed[:cut].reshape(lines, -1)
    out_o_down = packed[cut:].reshape(rank, groups, -1)
    return (
        output,
        grad_input,
        shared[:2],
        out_qkv,
        shared[2:lines - rank].reshape(3, rank, -1),
        out_up,
        out_maps,
        out_branch,
        out_o_down,
        shared[lines - rank:],
        out_gate_up,
        out_down,
    )


def solution(mesh):
    in_specs = (
        P("dp", None),
        P("dp", None),
        P("dp", None),
        P(),
        P(None, "tensor", None),
        P(),
        P(None, "tensor", None),
        P("tensor", None, None),
        P("tensor", None),
        P(None, "tensor", None),
        P(),
        P(None, None, "tensor"),
        P("tensor", None),
    )
    out_specs = (
        P(("dp", "tensor"), None),
        P(("dp", "tensor"), None),
        P(None, ("dp", "tensor")),
        P("dp", "tensor", None),
        P(None, None, ("dp", "tensor")),
        P(None, "tensor", "dp"),
        P("tensor", None, "dp"),
        P("tensor", "dp"),
        P(None, "tensor", "dp"),
        P(None, ("dp", "tensor")),
        P("dp", None, "tensor"),
        P("tensor", "dp"),
    )
    return jax.shard_map(
        local, mesh=mesh, in_specs=in_specs, out_specs=out_specs, check_vma=False
    )
```

```python
from functools import partial
import jax, jax.numpy as jnp
from jax import lax
from jax.experimental import pallas as pl
from jax.experimental.pallas import tpu as pltpu
from jax.sharding import PartitionSpec as P

HEADS = 32
KVH = 8
HEAD_SIZE = 64
WINDOW = 64
LONGEST = 512
epsilon = 1e-05
rope_base = 500000.0
F32 = jnp.float32
BF16 = jnp.bfloat16


def nn(a, b):
    return lax.dot_general(a, b, (((1,), (0,)), ((), ())), preferred_element_type=F32)


def nt(a, b):
    return lax.dot_general(a, b, (((1,), (1,)), ((), ())), preferred_element_type=F32)


def rotate_t(part, cosines, sines):
    half = part.shape[0] // 2
    a, b = part[:half], part[half:]
    return jnp.concatenate([a * cosines - b * sines, b * cosines + a * sines], axis=0)


def rotate_back_t(part, cosines, sines):
    half = part.shape[0] // 2
    a, b = part[:half], part[half:]
    return jnp.concatenate([a * cosines + b * sines, b * cosines - a * sines], axis=0)


def softmaxes_t(logits):
    up = jnp.exp(logits - jnp.max(logits, axis=0, keepdims=True))
    down = jnp.exp(jnp.min(logits, axis=0, keepdims=True) - logits)
    up = up * (1.0 / jnp.sum(up, axis=0, keepdims=True))
    down = down * (1.0 / jnp.sum(down, axis=0, keepdims=True))
    return up, down


def tile_plan(length, block):
    back = LONGEST // block
    return [(i, list(range(max(0, i - back), i + 1))) for i in range(length // block)]


def tile_masks(same, query_block, key_block, block):
    lowest = (query_block - key_block) * block - (block - 1)
    if lowest >= WINDOW:
        return None, same
    shape = (block, block)
    distance = (
        lax.broadcasted_iota(jnp.int32, shape, 1)
        - lax.broadcasted_iota(jnp.int32, shape, 0)
        + (query_block - key_block) * block
    )
    inside = same & (distance < WINDOW)
    if lowest < 0:
        inside = inside & (distance >= 0)
    return inside, same & (distance >= WINDOW)


def forward_kernel(heads, block, joined_ref, cos_ref, sin_ref, map_ref, row_ref, col_ref,
                   low_ref, att_ref, root_ref, keys, kfeat):
    length = cos_ref.shape[1]
    width = heads * HEAD_SIZE
    scale = HEAD_SIZE ** -0.5
    key_t = rotate_t(joined_ref[0, width:width + HEAD_SIZE], cos_ref[...], sin_ref[...]).astype(BF16)
    low_ref[0, width:width + HEAD_SIZE] = key_t
    value_t = joined_ref[0, width + HEAD_SIZE:].astype(BF16)
    low_ref[0, width + HEAD_SIZE:] = value_t
    up, down = softmaxes_t(nn(map_ref[0, width:], key_t))
    kfeat[...] = jnp.concatenate([up, down], axis=0).T.astype(BF16)
    keys[...] = key_t.astype(F32).T.astype(BF16)

    for i, tiles in tile_plan(length, block):
        cols = slice(i * block, (i + 1) * block)

        def one_head(h, carry, i=i, tiles=tiles, cols=cols):
            rows = pl.ds(pl.multiple_of(h * HEAD_SIZE, HEAD_SIZE), HEAD_SIZE)
            query = rotate_t(joined_ref[0, rows, cols], cos_ref[:, cols], sin_ref[:, cols]).astype(BF16)
            low_ref[0, rows, cols] = query
            up, down = softmaxes_t(nn(map_ref[0, rows], query))
            feat = jnp.concatenate([up, down], axis=0).astype(BF16)
            weights = []
            total = None
            for j in tiles:
                span = slice(j * block, (j + 1) * block)
                same = col_ref[span, :] == row_ref[:, cols]
                inside, far = tile_masks(same, i, j, block)
                linear = nn(kfeat[span, :], feat)
                w = jnp.where(far, linear, 0.0)
                if inside is not None:
                    w = jnp.where(inside, jnp.exp(nn(keys[span, :], query) * scale), w)
                part = jnp.sum(w, axis=0, keepdims=True)
                total = part if total is None else total + part
                weights.append(w)
            root = lax.rsqrt(total)
            root_ref[0, h, :, cols] = root
            att = None
            for j, w in zip(tiles, weights):
                p = (w * root * root).astype(BF16)
                piece = nn(low_ref[0, width + HEAD_SIZE:, j * block:(j + 1) * block], p)
                att = piece if att is None else att + piece
            att_ref[0, rows, cols] = att.astype(BF16)
            return carry

        lax.fori_loop(0, heads, one_head, 0)


def attention_forward(joined_t, cosines, sines, maps_t, seg_row, seg_col, heads, block=256):
    groups, width, length = joined_t.shape
    qw = heads * HEAD_SIZE
    whole = lambda shape: pl.BlockSpec(shape, lambda g: (0,) * len(shape))
    mine = lambda shape: pl.BlockSpec((1,) + shape, lambda g: (g,) + (0,) * len(shape))
    return pl.pallas_call(
        partial(forward_kernel, heads, block),
        grid=(groups,),
        out_shape=(
            jax.ShapeDtypeStruct((groups, width, length), BF16),
            jax.ShapeDtypeStruct((groups, qw, length), BF16),
            jax.ShapeDtypeStruct((groups, heads, 1, length), F32),
        ),
        in_specs=[mine((width, length)), whole(cosines.shape), whole(sines.shape),
                  mine(maps_t.shape[1:]), whole(seg_row.shape), whole(seg_col.shape)],
        out_specs=(mine((width, length)), mine((qw, length)), mine((heads, 1, length))),
        scratch_shapes=[pltpu.VMEM((length, HEAD_SIZE), BF16), pltpu.VMEM((length, 2 * HEAD_SIZE), BF16)],
        compiler_params=pltpu.CompilerParams(vmem_limit_bytes=48 * 2**20),
        cost_estimate=pl.CostEstimate(flops=22 * 10**9, bytes_accessed=10**7, transcendentals=10**6),
        name="attention_forward",
    )(joined_t, cosines, sines, maps_t, seg_row, seg_col)


def backward_kernel(heads, block, low_ref, cos_ref, sin_ref, map_ref, back_ref, row_ref, col_ref,
                    att_ref, root_ref, gatt_ref, grad_ref, gmap_ref,
                    keys, kfeat, kfeat_t, values, gkeys, gkfeat, gvalues):
    length = cos_ref.shape[1]
    width = heads * HEAD_SIZE
    scale = HEAD_SIZE ** -0.5
    key_t = low_ref[0, width:width + HEAD_SIZE]
    key_up, key_down = softmaxes_t(nn(map_ref[0, width:], key_t))
    both = jnp.concatenate([key_up, key_down], axis=0)
    kfeat_t[...] = both.astype(BF16)
    kfeat[...] = both.T.astype(BF16)
    keys[...] = key_t.astype(F32).T.astype(BF16)
    values[...] = low_ref[0, width + HEAD_SIZE:].astype(F32).T.astype(BF16)
    gkeys[...] = jnp.zeros_like(gkeys)
    gkfeat[...] = jnp.zeros_like(gkfeat)
    gvalues[...] = jnp.zeros_like(gvalues)
    gmap_ref[...] = jnp.zeros_like(gmap_ref)

    for i, tiles in tile_plan(length, block):
        cols = slice(i * block, (i + 1) * block)

        def one_head(h, carry, i=i, tiles=tiles, cols=cols):
            rows = pl.ds(pl.multiple_of(h * HEAD_SIZE, HEAD_SIZE), HEAD_SIZE)
            query = low_ref[0, rows, cols]
            gatt = gatt_ref[0, rows, cols]
            up, down = softmaxes_t(nn(map_ref[0, rows], query))
            feat = jnp.concatenate([up, down], axis=0).astype(BF16)
            root = root_ref[0, h, :, cols]
            inverse = root * root
            delta = jnp.sum(gatt.astype(F32) * att_ref[0, rows, cols].astype(F32), axis=0, keepdims=True)
            gquery = jnp.zeros((HEAD_SIZE, block), F32)
            gfeat = jnp.zeros((2 * HEAD_SIZE, block), F32)
            for j in tiles:
                span = slice(j * block, (j + 1) * block)
                same = col_ref[span, :] == row_ref[:, cols]
                inside, far = tile_masks(same, i, j, block)
                gprob = nn(values[span, :], gatt) - delta
                grad_far = jnp.where(far, gprob * root * root, 0.0).astype(BF16)
                p = jnp.where(far, nn(kfeat[span, :], feat) * root * root, 0.0)
                if inside is not None:
                    near = jnp.where(inside, jnp.exp(nn(keys[span, :], query) * scale) * root * root, 0.0)
                    p = jnp.where(inside, near, p)
                    grad_near = (near * gprob * scale).astype(BF16)
                    gquery = gquery + nn(low_ref[0, width:width + HEAD_SIZE, span], grad_near)
                    gkeys[span, :] += nt(grad_near, query)
                gvalues[span, :] += nt(p.astype(BF16), gatt)
                gfeat = gfeat + nn(kfeat_t[:, span], grad_far)
                gkfeat[span, :] += nt(grad_far, feat)
            glogits = softmaxes_back_t(up, down, gfeat)
            gquery = gquery + nn(back_ref[0, h], glogits)
            gmap_ref[0, h] += nt(query, glogits)
            grad_ref[0, rows, cols] = rotate_back_t(gquery, cos_ref[:, cols], sin_ref[:, cols]).astype(BF16)
            return carry

        lax.fori_loop(0, heads, one_head, 0)
    glogits = softmaxes_back_t(key_up, key_down, gkfeat[...].T)
    gkey_t = gkeys[...].T + nn(back_ref[0, heads], glogits)
    gmap_ref[0, heads] = nt(key_t, glogits)
    grad_ref[0, width:width + HEAD_SIZE] = rotate_back_t(gkey_t, cos_ref[...], sin_ref[...]).astype(BF16)
    grad_ref[0, width + HEAD_SIZE:] = gvalues[...].T.astype(BF16)


def softmaxes_back_t(up, down, grads):
    gup, gdown = grads[:HEAD_SIZE], grads[HEAD_SIZE:]
    return (
        up * (gup - jnp.sum(gup * up, axis=0, keepdims=True))
        - down * (gdown - jnp.sum(gdown * down, axis=0, keepdims=True))
    ).astype(BF16)


def attention_backward(low, cosines, sines, maps_t, maps, seg_row, seg_col, att, root, gatt, heads, block=256):
    groups, width, length = low.shape
    qw = heads * HEAD_SIZE
    whole = lambda shape: pl.BlockSpec(shape, lambda g: (0,) * len(shape))
    mine = lambda shape: pl.BlockSpec((1,) + shape, lambda g: (g,) + (0,) * len(shape))
    return pl.pallas_call(
        partial(backward_kernel, heads, block),
        grid=(groups,),
        out_shape=(
            jax.ShapeDtypeStruct((groups, width, length), BF16),
            jax.ShapeDtypeStruct((groups, heads + 1, HEAD_SIZE, HEAD_SIZE), F32),
        ),
        in_specs=[mine((width, length)), whole(cosines.shape), whole(sines.shape),
                  mine(maps_t.shape[1:]), mine(maps.shape[1:]), whole(seg_row.shape), whole(seg_col.shape),
                  mine((qw, length)), mine((heads, 1, length)), mine((qw, length))],
        out_specs=(mine((width, length)), mine((heads + 1, HEAD_SIZE, HEAD_SIZE))),
        scratch_shapes=[
            pltpu.VMEM((length, HEAD_SIZE), BF16), pltpu.VMEM((length, 2 * HEAD_SIZE), BF16),
            pltpu.VMEM((2 * HEAD_SIZE, length), BF16), pltpu.VMEM((length, HEAD_SIZE), BF16),
            pltpu.VMEM((length, HEAD_SIZE), F32), pltpu.VMEM((length, 2 * HEAD_SIZE), F32),
            pltpu.VMEM((length, HEAD_SIZE), F32)],
        compiler_params=pltpu.CompilerParams(vmem_limit_bytes=48 * 2**20),
        cost_estimate=pl.CostEstimate(flops=40 * 10**9, bytes_accessed=10**7, transcendentals=10**6),
        name="attention_backward",
    )(low, cosines, sines, maps_t, maps, seg_row, seg_col, att, root, gatt)


def rotary_tables_t(length, width):
    half = width // 2
    frequency = rope_base ** (-(jnp.arange(half, dtype=F32) * 2.0) / width)
    angles = frequency[:, None] * jnp.arange(length, dtype=F32)[None, :]
    return jnp.cos(angles), jnp.sin(angles)


def normalize(values, gain_row):
    inverse = lax.rsqrt(jnp.mean(values * values, axis=-1, keepdims=True) + epsilon)
    scaled = values * inverse
    return scaled, inverse, (scaled * gain_row).astype(BF16)


def feed_kernel(
    n, dp, tile, cut,
    normed_in, cot_in, gate_up_in, down_in,
    sum_out, mixed_out, came, first_send, first_keep, second_send, second_keep,
    gate_up, down, normed, cots, acts, grads, arriving, sending, mixed, turned,
    load_sems, weight_sems, out_sems, core_send, core_recv, fill_sems, gather_send, gather_recv, sum_send, sum_recv, mixed_sems,
):
    share, width = normed_in.shape
    hidden = down_in.shape[0]
    block = width // dp
    piece = share // cut
    per = hidden // tile
    me = lax.axis_index("tensor")
    mine = lax.axis_index("dp")
    core = lax.rem(mine, 2)
    mate = {"dp": mine + 1 - 2 * core}
    place = (me, n - 1 - me)
    ends = (me < n - 1, me > 0)
    partner = (me + 1, me - 1)

    def device(way):
        return {"tensor": partner[way]}

    def rows_of(j, size=share):
        return pl.ds(pl.multiple_of(j * share, 16), size)

    barrier = pltpu.get_barrier_semaphore()
    for way in range(2):

        @pl.when(ends[way])
        def _(way=way):
            pl.semaphore_signal(barrier, inc=1, device_id=device(way), device_id_type=pl.DeviceIdType.MESH)

    pl.semaphore_signal(barrier, inc=1, device_id=mate, device_id_type=pl.DeviceIdType.MESH)
    own_load = pltpu.make_async_copy(normed_in, normed.at[rows_of(me)], load_sems.at[0])
    cot_load = pltpu.make_async_copy(cot_in, cots, load_sems.at[1])
    own_load.start()

    def weight_loads(f):
        span = slice(f * tile, (f + 1) * tile)
        return (
            pltpu.make_async_copy(gate_up_in.at[0, :, span], gate_up.at[0:width, span], weight_sems.at[0, f]),
            pltpu.make_async_copy(gate_up_in.at[1, :, span], gate_up.at[width:2 * width, span], weight_sems.at[1, f]),
            pltpu.make_async_copy(down_in.at[span], down.at[span], weight_sems.at[2, f]),
        )

    weights = [weight_loads(f) for f in range(per)]
    for load in weights[0]:
        load.start()
    cot_load.start()
    for loads in weights[1:]:
        for load in loads:
            load.start()
    inner = (me > 0) & (me < n - 1)

    @pl.when(inner)
    def _():
        pl.semaphore_wait(barrier, 3)

    @pl.when(jnp.logical_not(inner))
    def _():
        pl.semaphore_wait(barrier, 2)

    def gather(way, j):
        return pltpu.make_async_remote_copy(
            src_ref=normed.at[rows_of(j)], dst_ref=normed.at[rows_of(j)],
            send_sem=gather_send.at[way, j], recv_sem=gather_recv.at[way, j],
            device_id=device(way), device_id_type=pl.DeviceIdType.MESH)

    def gather_arrival(way, j):
        return pltpu.make_async_copy(normed.at[rows_of(j)], normed.at[rows_of(j)], gather_recv.at[way, j])

    def pass_on(way, j, q):
        rows = pl.ds(pl.multiple_of(j * share + q * piece, 16), piece)
        last = j == partner[way]
        slot = jnp.where(last, n, j) if way else j
        goal = pl.ds(pl.multiple_of(slot * share + q * piece, 16), piece)
        return pltpu.make_async_remote_copy(
            src_ref=sending.at[rows], dst_ref=arriving.at[goal],
            send_sem=sum_send.at[way, j * cut + q], recv_sem=sum_recv.at[way, j * cut + q],
            device_id=device(way), device_id_type=pl.DeviceIdType.MESH)

    def sum_arrival(way, j, q, slot):
        rows = pl.ds(pl.multiple_of(slot * share + q * piece, 16), piece)
        return pltpu.make_async_copy(arriving.at[rows], arriving.at[rows], sum_recv.at[way, j * cut + q])

    own_load.wait()
    for way in range(2):

        @pl.when(ends[way])
        def _(way=way):
            gather(way, me).start()

    def first_half(rows, f):
        span = pl.ds(pl.multiple_of(f * tile, tile), tile)
        upper = pl.ds(pl.multiple_of(hidden + f * tile, tile), tile)
        gate = nn(normed[rows, :], gate_up[0:width, span])
        up = nn(normed[rows, :], gate_up[width:2 * width, span])
        grad_act = nt(cots[rows, :], down[span, :])
        sigma = 1.0 / (1.0 + jnp.exp(-gate))
        silu = gate * sigma
        acts[rows, span] = (silu * up).astype(BF16)
        grads[rows, span] = (grad_act * up * (sigma + silu * (1.0 - sigma))).astype(BF16)
        grads[rows, upper] = (grad_act * silu).astype(BF16)

    def second_half(rows):
        @pl.loop(0, width // tile)
        def _(d):
            span = pl.ds(pl.multiple_of(d * tile, tile), tile)
            lower = pl.ds(pl.multiple_of(width + d * tile, tile), tile)
            sending[rows, span] = (
                nt(grads[rows, 0:hidden], gate_up[span, :]) + nt(grads[rows, hidden:], gate_up[lower, :])
            ).astype(BF16)

    both = jnp.minimum(me, n - 1 - me)
    long_side = jnp.where(me < n - 1 - me, 1, -1)

    def chunk_at(k):
        near = (k + 1) // 2 * (-1 if k % 2 else 1)
        return me + jnp.where(k <= 2 * both, near, (k - both) * long_side)

    def chunk_rows(k):
        return rows_of(chunk_at(k) if k else me)

    def put_mixed(k):
        return pltpu.make_async_copy(mixed, mixed_out.at[chunk_rows(k)], mixed_sems)

    def mix(k):
        if k:
            put_mixed(k - 1).wait()

        @pl.loop(0, width // tile)
        def _(d):
            span = pl.ds(pl.multiple_of(d * tile, tile), tile)
            mixed[:, span] = nn(acts[chunk_rows(k), :], down[:, span]).astype(BF16)

        put_mixed(k).start()

    for f in range(per):
        for load in weights[f]:
            load.wait()
        if f == 0:
            cot_load.wait()
        first_half(rows_of(me), f)
    second_half(rows_of(me))

    for k in range(1, n):
        mix(k - 1)
        for way in range(2):
            j = me - k if way == 0 else me + k
            there = (me >= k) if way == 0 else (me + k <= n - 1)

            @pl.when(there)
            def _(way=way, j=j):
                gather_arrival(way, j).wait()

                @pl.when(ends[way])
                def _():
                    gather(way, j).start()

        rows = chunk_rows(k)

        @pl.loop(0, per)
        def _(f):
            first_half(rows, f)

        second_half(rows)
        for way in range(2):

            @pl.when(place[way] == 0)
            def _(way=way):
                j = me + k if way == 0 else me - k
                for q in range(cut):
                    pass_on(way, j, q).start()

    room = 3 * block
    half = dp // 4
    items = dp // 2 * 2 * per

    def staged(pair, j, start=0, size=room):
        first = pl.multiple_of((lax.rem(pair, 2) * 2 + j) * room + start, 16)
        return gate_up.at[pl.ds(first, size)]

    def put_across(pair, j):
        return pltpu.make_async_remote_copy(
            src_ref=staged(pair, j), dst_ref=came.at[2 * pair + j],
            send_sem=core_send.at[pair, j], recv_sem=core_recv.at[pair, j],
            device_id=mate, device_id_type=pl.DeviceIdType.MESH)

    def fill(pair, j):
        return pltpu.make_async_copy(came.at[2 * (pair - half) + j], staged(pair, j), fill_sems.at[j])

    def put_own(pair, j, act):
        q = 2 * (pair - half) + j
        quarter = dp // 4
        rows = room // 2
        place = lax.div(mine, 2)
        for part, (other, keep, slot, goes) in enumerate((
            (first_send, first_keep, lax.div(q, 2), lax.rem(q, 2) != lax.rem(place, 2)),
            (second_send, second_keep, lax.rem(q, quarter), lax.div(q, quarter) != lax.div(place, quarter)),
        )):
            for ref, chosen in ((other, goes), (keep, jnp.logical_not(goes))):

                @pl.when(chosen)
                def _(ref=ref, part=part, slot=slot):
                    copy = pltpu.make_async_copy(
                        staged(pair, j, part * rows, rows), ref.at[slot], out_sems.at[lax.rem(pair, 2), j, part])
                    if act == "start":
                        copy.start()
                    else:
                        copy.wait()

    def weight_item(i):
        pair, f = lax.div(i, 2 * per), lax.rem(i, 2 * per)
        slot = lax.rem(pair, 2)
        other = lax.div(pair, half)

        def turn(source):
            for j in range(2):
                column = 2 * (2 * lax.rem(pair, half) + j) + lax.rem(core + 1 + other, 2)
                span = pl.ds(pl.multiple_of(column * block, block), block)
                turned[pl.ds(j * block, block), :] = source[:, span].T

        def store(row, goal, product):
            for j in range(2):
                start = pl.multiple_of((slot * 2 + j) * room + row * block, 16)
                rows = pl.ds(start, block)
                part = product[j * block:(j + 1) * block]

                @pl.when(pair < half)
                def _(rows=rows, part=part):
                    gate_up[rows, goal] = part.astype(BF16)

                @pl.when(pair >= half)
                def _(rows=rows, part=part):
                    gate_up[rows, goal] = (gate_up[rows, goal].astype(F32) + part).astype(BF16)

        @pl.when(f == 0)
        def _():
            @pl.when((pair >= 2) & (pair < half))
            def _():
                for j in range(2):
                    put_across(pair - 2, j).wait_send()

            @pl.when(pair >= half)
            def _():
                for j in range(2):
                    fill(pair, j).wait()

            turn(normed)

        @pl.when(f == per)
        def _():
            turn(cots)
            following = pair + 1

            @pl.when((following >= half) & (following < 2 * half))
            def _():
                @pl.when(following - 2 < half)
                def _():
                    for j in range(2):
                        put_across(following - 2, j).wait_send()

                @pl.when(following - 2 >= half)
                def _():
                    for j in range(2):
                        put_own(following - 2, j, "wait")

                for j in range(2):
                    put_across(following - half, j).wait_recv()
                    fill(following, j).start()

        @pl.when(f < per)
        def _():
            goal = pl.ds(pl.multiple_of(f * tile, tile), tile)
            for row in range(2):
                span = pl.ds(pl.multiple_of(row * hidden + f * tile, tile), tile)
                store(row, goal, nn(turned[...], grads[:, span]))

        @pl.when(f >= per)
        def _():
            goal = pl.ds(pl.multiple_of((f - per) * tile, tile), tile)
            store(2, goal, nn(turned[...], acts[:, goal]))

        @pl.when(f == 2 * per - 1)
        def _():
            @pl.when(pair < half)
            def _():
                for j in range(2):
                    put_across(pair, j).start()

            @pl.when(pair >= half)
            def _():
                for j in range(2):
                    put_own(pair, j, "start")

    first_step, last_step = cut + 1, cut * (n - 1) + n - 2
    every = -(-items // (last_step - first_step))

    def serve(step):
        for way in range(2):
            count = step - place[way]
            j_place = lax.div(count, cut) + 1
            q = lax.rem(count, cut)
            j = j_place if way == 0 else n - 1 - j_place

            @pl.when((place[way] > 0) & (j_place > place[way]) & (j_place < n))
            def _(way=way, j=j, q=q):
                sum_arrival(way, j, q, j).wait()
                rows = pl.ds(pl.multiple_of(j * share + q * piece, 16), piece)
                sending[rows, :] = (sending[rows, :].astype(F32) + arriving[rows, :].astype(F32)).astype(BF16)
                pass_on(way, j, q).start()

    @pl.loop(first_step, last_step)
    def _(step):
        serve(step)
        for j in range(every):
            item = (step - first_step) * every + j

            @pl.when(item < items)
            def _(item=item):
                weight_item(item)


    mix(n - 1)

    for way in range(2):

        @pl.when(place[way] > 0)
        def _(way=way):
            for q in range(cut):
                slot = n if way else me
                sum_arrival(way, me, q, slot).wait()
            slot = pl.ds(n * share, share) if way else rows_of(me)

            @pl.loop(0, width // tile)
            def _(d):
                span = pl.ds(pl.multiple_of(d * tile, tile), tile)
                sending[rows_of(me), span] = (
                    sending[rows_of(me), span].astype(F32) + arriving[slot, span].astype(F32)
                ).astype(BF16)

    final = pltpu.make_async_copy(sending.at[rows_of(me)], sum_out, load_sems.at[0])
    final.start()
    for pair in (2 * half - 2, 2 * half - 1):
        for j in range(2):
            put_own(pair, j, "wait")
    put_mixed(n - 1).wait()
    final.wait()
    for way in range(2):

        @pl.when(ends[way])
        def _(way=way):
            @pl.loop(0, n)
            def _(j):
                sent = (j <= me) if way == 0 else (j >= me)

                @pl.when(sent)
                def _():
                    gather(way, j).wait_send()

                @pl.when(jnp.logical_not(sent))
                def _():
                    for q in range(cut):
                        pass_on(way, j, q).wait_send()


def feed_forward(normed, cotangent, gate_up, down, n, dp, tile=512, cut=4):
    share, width = normed.shape
    hidden = down.shape[0]
    tokens = n * share
    block = width // dp
    anywhere = pl.BlockSpec(memory_space=pl.ANY)
    return pl.pallas_call(
        partial(feed_kernel, n, dp, tile, cut),
        out_shape=(
            jax.ShapeDtypeStruct((share, width), BF16),
            jax.ShapeDtypeStruct((tokens, width), BF16),
            jax.ShapeDtypeStruct((dp // 2, 3 * block, hidden), BF16),
            jax.ShapeDtypeStruct((dp // 4, 3 * block // 2, hidden), BF16),
            jax.ShapeDtypeStruct((dp // 4, 3 * block // 2, hidden), BF16),
            jax.ShapeDtypeStruct((dp // 4, 3 * block // 2, hidden), BF16),
            jax.ShapeDtypeStruct((dp // 4, 3 * block // 2, hidden), BF16),
        ),
        in_specs=[anywhere] * 4,
        out_specs=(anywhere,) * 7,
        scratch_shapes=[
            pltpu.VMEM((2 * width, hidden), BF16),
            pltpu.VMEM((hidden, width), BF16),
            pltpu.VMEM((tokens, width), BF16),
            pltpu.VMEM((tokens, width), BF16),
            pltpu.VMEM((tokens, hidden), BF16),
            pltpu.VMEM((tokens, 2 * hidden), BF16),
            pltpu.VMEM((tokens + share, width), BF16),
            pltpu.VMEM((tokens, width), BF16),
            pltpu.VMEM((share, width), BF16),
            pltpu.VMEM((2 * block, tokens), BF16),
            pltpu.SemaphoreType.DMA((2,)),
            pltpu.SemaphoreType.DMA((3, hidden // tile)),
            pltpu.SemaphoreType.DMA((2, 2, 2)),
            pltpu.SemaphoreType.DMA((dp // 4, 2)),
            pltpu.SemaphoreType.DMA((dp // 4, 2)),
            pltpu.SemaphoreType.DMA((2,)),
            pltpu.SemaphoreType.DMA((2, n)),
            pltpu.SemaphoreType.DMA((2, n)),
            pltpu.SemaphoreType.DMA((2, n * cut)),
            pltpu.SemaphoreType.DMA((2, n * cut)),
            pltpu.SemaphoreType.DMA,
        ],
        compiler_params=pltpu.CompilerParams(
            collective_id=0, has_side_effects=True, vmem_limit_bytes=60 * 2**20),
        cost_estimate=pl.CostEstimate(
            flops=18 * tokens * width * hidden, bytes_accessed=2 * 24 * 2**20, transcendentals=tokens * hidden),
        name="feed_forward",
    )(normed, cotangent, gate_up, down)


def tail_kernel(
    n, dp, tile, cut,
    joined_in, w_in, normed_in, att_in, att_mate_in, grad_in, grad_mate_in, fa_keep, fa_came, fb_keep, fb_came,
    sum_out, feed_a, feed_b, branch_out, qkv_a, qkv_b,
    joined, w, normed, att, att_mate, grad, grad_mate, arriving, sending,
    fa, fa2, fb, fb2, f_recvs, wm, w_recvs, w_done, w_last, qo, qm, qc, q_recvs,
    load_sems, out_sems, sum_send, sum_recv, f_sems, w_sems, q_sems, core_sems, last_send, last_recv,
):
    width = w.shape[1]
    joined_width, tokens = joined.shape
    share = tokens // n
    block = width // dp
    piece = share // cut
    columns = att.shape[0]
    me = lax.axis_index("tensor")
    mine = lax.axis_index("dp")
    core = lax.rem(mine, 2)
    bits = dp.bit_length() - 1
    mesh_id = pl.DeviceIdType.MESH
    place = (me, n - 1 - me)
    ends = (me < n - 1, me > 0)
    partner = (me + 1, me - 1)

    def own_bit(bit):
        return lax.rem(lax.div(mine, 1 << bit), 2)

    def mate(bit):
        return {"dp": mine + (1 << bit) * (1 - 2 * own_bit(bit))}

    barrier = pltpu.get_barrier_semaphore()
    for s in range(1, n):
        pl.semaphore_signal(barrier, inc=1, device_id={"tensor": lax.rem(me + s, n)}, device_id_type=mesh_id)
    for bit in range(bits):
        pl.semaphore_signal(barrier, inc=1, device_id=mate(bit), device_id_type=mesh_id)

    pairs = (
        (joined_in, joined), (w_in, w), (att_in, att), (att_mate_in, att_mate), (grad_in, grad),
        (grad_mate_in, grad_mate), (normed_in, normed), (fa_keep, fa), (fa_came, fa2), (fb_keep, fb), (fb_came, fb2),
    )
    loads = [pltpu.make_async_copy(a, b, load_sems.at[i]) for i, (a, b) in enumerate(pairs)]
    for load in loads:
        load.start()
    pl.semaphore_wait(barrier, n - 1 + bits)

    def rows_of(j):
        return pl.ds(pl.multiple_of(j * share, 16), share)

    def pass_on(way, j, q):
        rows = pl.ds(pl.multiple_of(j * share + q * piece, 16), piece)
        last = j == partner[way]
        slot = jnp.where(last, n, j) if way else j
        goal = pl.ds(pl.multiple_of(slot * share + q * piece, 16), piece)
        return pltpu.make_async_remote_copy(
            src_ref=sending.at[rows], dst_ref=arriving.at[goal],
            send_sem=sum_send.at[way, j * cut + q], recv_sem=sum_recv.at[way, j * cut + q],
            device_id={"tensor": partner[way]}, device_id_type=mesh_id)

    def sum_arrival(way, j, q, slot):
        rows = pl.ds(pl.multiple_of(slot * share + q * piece, 16), piece)
        return pltpu.make_async_copy(arriving.at[rows], arriving.at[rows], sum_recv.at[way, j * cut + q])

    loads[0].wait()
    loads[1].wait()
    for k in range(n):
        distance = n - 1 - k
        for way in range(2):
            j = me + distance if way == 0 else me - distance
            there = (j < n) if way == 0 else (j >= 0)
            if distance == 0 and way:
                continue

            @pl.when(there)
            def _(j=j, way=way, distance=distance):
                rows = rows_of(j)

                @pl.loop(0, width // tile)
                def _(d):
                    span = pl.ds(pl.multiple_of(d * tile, tile), tile)
                    sending[rows, span] = lax.dot_general(
                        joined[:, pl.ds(pl.multiple_of(j * share, 128), share)], w[:, span],
                        (((0,), (0,)), ((), ())), preferred_element_type=F32).astype(BF16)

                if distance:

                    @pl.when(place[way] == 0)
                    def _():
                        for q in range(cut):
                            pass_on(way, j, q).start()

    def halving(cur, parts, recvs, sems, stream, order):
        steps = []
        current = cur
        for step, bit in enumerate(order):
            count = 1 << (len(order) - step - 1)
            own = own_bit(bit)

            def index(slot, which, count=count):
                return 2 * slot + which if stream == 0 else which * count + slot

            room = recvs[stream][step]
            copies = [
                pltpu.make_async_remote_copy(
                    src_ref=current(index(slot, 1 - own)), dst_ref=room.at[slot],
                    send_sem=sems.at[0, stream, step, slot], recv_sem=sems.at[1, stream, step, slot],
                    device_id=mate(bit), device_id_type=mesh_id)
                for slot in range(count)
            ]

            def start(copies=copies):
                for copy in copies:
                    copy.start()

            def finish(copies=copies, current=current, room=room, count=count, own=own, index=index):
                for slot, copy in enumerate(copies):
                    copy.wait_recv()
                    kept = current(index(slot, own))
                    total = kept.shape[0]
                    rows = 128 if total % 128 == 0 else 64 if total % 64 == 0 else total

                    @pl.loop(0, total // rows)
                    def _(r):
                        span = pl.ds(pl.multiple_of(r * rows, 16), rows)
                        room[slot, span, :] = (kept[span, :].astype(F32) + room[slot, span, :].astype(F32)).astype(BF16)

            def settle(copies=copies):
                for copy in copies:
                    copy.wait_send()

            steps.append((start, finish, settle))
            current = lambda i, room=room: room.at[i]
        return steps

    rest = list(range(1, bits))
    half_rows = block // 2
    w_steps = [
        halving(lambda i, s=s: wm.at[i, pl.ds(s * half_rows, half_rows)], dp // 2, w_recvs, w_sems, s, order)
        for s, order in enumerate((rest, rest[::-1]))
    ]
    q_steps = [
        halving(lambda i, s=s: qm.at[i, pl.ds(s * half_rows, half_rows)], dp // 2, q_recvs, q_sems, s, order)
        for s, order in enumerate((rest, rest[::-1]))
    ]
    f_steps = [
        halving(lambda i, ref=ref: ref.at[i], dp // 4, f_recvs, f_sems, s, order[1:])
        for s, (ref, order) in enumerate(((fa, rest), (fb, rest[::-1])))
    ]

    for load in loads[2:6]:
        load.wait()

    @pl.loop(0, dp // 2)
    def _(q):
        span = pl.ds(pl.multiple_of(q * block, block), block)
        turned, turned_mate = grad[:, span].T, grad_mate[:, span].T
        for c in range(0, columns, tile):
            wm[q, :, c:c + tile] = (nt(turned, att[c:c + tile, :]) + nt(turned_mate, att_mate[c:c + tile, :])).astype(BF16)

    for s in range(2):
        w_steps[s][0][0]()

    loads[6].wait()

    def across(q):
        return pltpu.make_async_remote_copy(
            src_ref=qo.at[q], dst_ref=qc.at[q], send_sem=core_sems.at[0, q], recv_sem=core_sems.at[1, q],
            device_id=mate(0), device_id_type=mesh_id)

    def projection(q, which):
        column = 2 * q + which
        span = pl.ds(pl.multiple_of(column * block, block), block)
        return nt(normed[:, span].T, joined[...])

    @pl.loop(0, dp // 2)
    def _(q):
        qo[q] = projection(q, 1 - core).astype(BF16)
        across(q).start()

    @pl.loop(0, dp // 2)
    def _(q):
        product = projection(q, core)
        across(q).wait_recv()
        qm[q] = (product + qc[q].astype(F32)).astype(BF16)

    for s in range(2):
        q_steps[s][0][0]()

    for load in loads[7:]:
        load.wait()
    for one, other in ((fa, fa2), (fb, fb2)):
        for i in range(dp // 4):
            rows = 64 if one.shape[1] % 64 == 0 else one.shape[1]

            @pl.loop(0, one.shape[1] // rows)
            def _(r, one=one, other=other, i=i):
                span = pl.ds(pl.multiple_of(r * rows, 16), rows)
                one[i, span, :] = (one[i, span, :].astype(F32) + other[i, span, :].astype(F32)).astype(BF16)

    def serve(step):
        for way in range(2):
            count = step - place[way]
            reach = lax.div(count, cut)
            j_place = n - 1 - reach
            q = lax.rem(count, cut)
            j = j_place if way == 0 else n - 1 - j_place

            @pl.when((place[way] > 0) & (count >= 0) & (j_place > place[way]))
            def _(way=way, j=j, q=q):
                sum_arrival(way, j, q, j).wait()
                rows = pl.ds(pl.multiple_of(j * share + q * piece, 16), piece)
                sending[rows, :] = (sending[rows, :].astype(F32) + arriving[rows, :].astype(F32)).astype(BF16)
                pass_on(way, j, q).start()

    last_step = cut * (n - 2) + n - 1
    first = 1 + cut
    pl.loop(1, first)(serve)
    for step in range(len(rest)):
        for s in range(2):
            w_steps[s][step][1]()
            if step + 1 < len(rest):
                w_steps[s][step + 1][0]()
            q_steps[s][step][1]()
            if step + 1 < len(rest):
                q_steps[s][step + 1][0]()
        if step == 0:
            for s in range(2):
                f_steps[s][0][0]()
        begin = first + step * 2
        end = min(begin + 2, last_step) if step + 1 < len(rest) else last_step
        if step + 1 < len(rest):
            pl.loop(begin, end)(serve)

    own_columns = columns // n
    for s in range(2):
        w_done[pl.ds(s * half_rows, half_rows), :] = w_recvs[s][len(rest) - 1][0]

    def deliver(s):
        goal = lax.rem(me + s, n)
        return pltpu.make_async_remote_copy(
            src_ref=w_done.at[:, pl.ds(pl.multiple_of(goal * own_columns, 128), own_columns)],
            dst_ref=w_last.at[s - 1], send_sem=last_send.at[s - 1], recv_sem=last_recv.at[s - 1],
            device_id={"tensor": goal}, device_id_type=mesh_id)

    for s in range(1, n):
        deliver(s).start()
    q_outs = [
        pltpu.make_async_copy(q_recvs[s][len(rest) - 1].at[0], (qkv_a, qkv_b)[s], out_sems.at[s]) for s in range(2)
    ]
    for copy in q_outs:
        copy.start()
    pl.loop(first + 2 * (len(rest) - 1), last_step)(serve)

    for step in range(len(rest) - 1):
        for s in range(2):
            f_steps[s][step][1]()
            if step + 1 < len(rest) - 1:
                f_steps[s][step + 1][0]()
    f_outs = [
        pltpu.make_async_copy(f_recvs[s][len(rest) - 2].at[0], (feed_a, feed_b)[s], out_sems.at[2 + s]) for s in range(2)
    ]
    for copy in f_outs:
        copy.start()

    mine_columns = pl.ds(pl.multiple_of(me * own_columns, 128), own_columns)
    total = w_done[:, mine_columns].astype(F32)
    for s in range(1, n):
        deliver(s).wait_recv()
        total = total + w_last[s - 1].astype(F32)
    w_last[n - 1] = total.astype(BF16)
    branch = pltpu.make_async_copy(w_last.at[n - 1], branch_out, out_sems.at[4])
    branch.start()

    for way in range(2):

        @pl.when(place[way] > 0)
        def _(way=way):
            for q in range(cut):
                slot = n if way else me
                sum_arrival(way, me, q, slot).wait()
            slot = pl.ds(n * share, share) if way else rows_of(me)

            @pl.loop(0, width // tile)
            def _(d):
                span = pl.ds(pl.multiple_of(d * tile, tile), tile)
                sending[rows_of(me), span] = (
                    sending[rows_of(me), span].astype(F32) + arriving[slot, span].astype(F32)
                ).astype(BF16)

    final = pltpu.make_async_copy(sending.at[rows_of(me)], sum_out, out_sems.at[5])
    final.start()
    for copy in (*q_outs, *f_outs, branch, final):
        copy.wait()
    for steps in (*w_steps, *q_steps, *f_steps):
        for _, _, settle in steps:
            settle()
    for s in range(1, n):
        deliver(s).wait_send()

    @pl.loop(0, dp // 2)
    def _(q):
        across(q).wait_send()

    for way in range(2):

        @pl.when(ends[way])
        def _(way=way):
            @pl.loop(0, n)
            def _(j):
                sent = (j > me) if way == 0 else (j < me)

                @pl.when(sent)
                def _():
                    for q in range(cut):
                        pass_on(way, j, q).wait_send()


def tail(joined, w, normed, att, att_mate, grad, grad_mate, feed, n, dp, tile=512, cut=4):
    joined_width, tokens = joined.shape
    width = w.shape[1]
    share = tokens // n
    block = width // dp
    columns = att.shape[0]
    steps = dp.bit_length() - 2
    feed_rows, hidden = feed[0].shape[1:]
    anywhere = pl.BlockSpec(memory_space=pl.ANY)
    half = block // 2

    def rooms(rows, cols, count):
        return [[pltpu.VMEM((1 << (count - step - 1), rows, cols), BF16) for step in range(count)] for _ in range(2)]

    def like(array):
        return pltpu.VMEM(array.shape, BF16)

    return pl.pallas_call(
        partial(tail_kernel, n, dp, tile, cut),
        out_shape=(
            jax.ShapeDtypeStruct((share, width), BF16),
            jax.ShapeDtypeStruct((feed_rows, hidden), BF16),
            jax.ShapeDtypeStruct((feed_rows, hidden), BF16),
            jax.ShapeDtypeStruct((block, columns // n), BF16),
            jax.ShapeDtypeStruct((half, joined_width), BF16),
            jax.ShapeDtypeStruct((half, joined_width), BF16),
        ),
        in_specs=[anywhere] * 11,
        out_specs=(anywhere,) * 6,
        scratch_shapes=[
            like(joined), like(w), like(normed), like(att), like(att_mate), like(grad), like(grad_mate),
            pltpu.VMEM((tokens + share, width), BF16),
            pltpu.VMEM((tokens, width), BF16),
            like(feed[0]), like(feed[1]), like(feed[2]), like(feed[3]),
            rooms(feed_rows, hidden, steps - 1),
            pltpu.VMEM((dp // 2, block, columns), BF16),
            rooms(half, columns, steps),
            pltpu.VMEM((block, columns), BF16),
            pltpu.VMEM((n, block, columns // n), BF16),
            pltpu.VMEM((dp // 2, block, joined_width), BF16),
            pltpu.VMEM((dp // 2, block, joined_width), BF16),
            pltpu.VMEM((dp // 2, block, joined_width), BF16),
            rooms(half, joined_width, steps),
            pltpu.SemaphoreType.DMA((11,)),
            pltpu.SemaphoreType.DMA((6,)),
            pltpu.SemaphoreType.DMA((2, n * cut)),
            pltpu.SemaphoreType.DMA((2, n * cut)),
            pltpu.SemaphoreType.DMA((2, 2, steps, dp // 4)),
            pltpu.SemaphoreType.DMA((2, 2, steps, dp // 4)),
            pltpu.SemaphoreType.DMA((2, 2, steps, dp // 4)),
            pltpu.SemaphoreType.DMA((2, dp // 2)),
            pltpu.SemaphoreType.DMA((n - 1,)),
            pltpu.SemaphoreType.DMA((n - 1,)),
        ],
        compiler_params=pltpu.CompilerParams(
            collective_id=1, has_side_effects=True, vmem_limit_bytes=60 * 2**20),
        cost_estimate=pl.CostEstimate(flops=100 * 10**9, bytes_accessed=40 * 2**20, transcendentals=0),
        name="gradient_sums",
    )(joined, w, normed, att, att_mate, grad, grad_mate, *feed)


def ring(size, shift=1):
    return [(i, (i + shift) % size) for i in range(size)]


def flip(size, bit):
    return [(i, i ^ (1 << bit)) for i in range(size)]


def pick(array, index, axis):
    return lax.dynamic_index_in_dim(array, index, axis, keepdims=False)


def chunk_of(array, index, rows, axis):
    return lax.dynamic_slice_in_dim(array, index * rows, rows, axis)


def bits_of(size):
    return size.bit_length() - 1


def scatter_small(blocks, over_tensor):
    size = lax.axis_size("dp")
    for bit in reversed(range(bits_of(size))):
        own = (lax.axis_index("dp") >> bit) & 1
        blocks = blocks.reshape((2, blocks.shape[0] // 2) + blocks.shape[1:])
        blocks = pick(blocks, own, 0) + lax.ppermute(pick(blocks, 1 - own, 0), "dp", flip(size, bit))
    blocks = blocks[0]
    if over_tensor:
        size = lax.axis_size("tensor")
        for bit in reversed(range(bits_of(size))):
            own = (lax.axis_index("tensor") >> bit) & 1
            blocks = blocks.reshape((2, blocks.shape[0] // 2) + blocks.shape[1:])
            blocks = pick(blocks, own, 0) + lax.ppermute(
                pick(blocks, 1 - own, 0), "tensor", flip(size, bit)
            )
        blocks = blocks[0]
    return blocks


def gather_weight(shard):
    piece = chunk_of(shard, lax.axis_index("dp"), shard.shape[0] // lax.axis_size("dp"), 0)
    whole = lax.all_gather(piece, ("tensor", "dp"), axis=0, tiled=True)
    return whole.reshape((lax.axis_size("tensor"),) + shard.shape)


def exchange(parts, shift):
    n = lax.axis_size("tensor")
    me = lax.axis_index("tensor")
    came = [parts(me)]
    for s in range(1, n):
        came.append(lax.ppermute(parts((me + s) % n), "tensor", ring(n, s)))
    return came


def by_place(came):
    n = len(came)
    me = lax.axis_index("tensor")
    stacked = jnp.stack(came)
    return [pick(stacked, (me + n - j) % n, 0) for j in range(n)]


def local(
    tokens,
    cotangent,
    segments,
    norm_gains,
    w_qkv,
    qkv_down,
    query_key_value_up,
    feature_maps,
    w_out,
    o_down,
    o_up,
    w_gate_up,
    w_down,
):
    token_rows, model_width = tokens.shape
    groups = w_qkv.shape[1]
    heads = HEADS // KVH
    query_width = heads * HEAD_SIZE
    joined_width = w_qkv.shape[2]
    rank = o_up.shape[0]
    dp = lax.axis_size("dp")
    n = lax.axis_size("tensor")
    me = lax.axis_index("tensor")
    share = token_rows // n
    gains = norm_gains.astype(F32)
    cosines, sines = rotary_tables_t(token_rows, HEAD_SIZE)
    dot = partial(jnp.einsum, preferred_element_type=F32)

    up = query_key_value_up.astype(BF16)
    edges = ((0, query_width), (query_width, query_width + HEAD_SIZE), (query_width + HEAD_SIZE, joined_width))
    up_wide = jnp.stack(
        [jnp.pad(up[:, :, a:b], ((0, 0), (0, 0), (a, joined_width - b))) for a, b in edges]
    )
    w_joined = (
        jnp.transpose(w_qkv, (1, 2, 0)).astype(F32) + dot("jrkc,jrd->kcd", up_wide, qkv_down)
    ).astype(BF16).reshape(groups * joined_width, model_width)
    down_flat = o_down.reshape(rank, -1)
    w_branch = (w_out.astype(F32) + dot("rc,rd->cd", down_flat, o_up)).astype(BF16)
    down_all = lax.all_gather(down_flat, "tensor")
    all_branch = gather_weight(w_branch)

    _, _, normed_one = normalize(tokens.astype(F32), gains[0])
    lowrank = dot("td,jrd->tjr", normed_one, qkv_down)
    joined = dot("cd,td->ct", w_joined, normed_one).reshape(groups, joined_width, token_rows)
    maps_t = jnp.swapaxes(feature_maps, 1, 2)
    maps = jnp.stack(
        [feature_maps[:, :, i * HEAD_SIZE:(i + 1) * HEAD_SIZE] for i in range(heads + 1)], axis=1
    )
    seg_row = segments.reshape(1, token_rows)
    seg_col = segments.reshape(token_rows, 1)
    low, attended, root = attention_forward(joined, cosines, sines, maps_t, seg_row, seg_col, heads)
    attended_flat = attended.reshape(groups * query_width, token_rows)
    att_came = exchange(lambda j: chunk_of(attended_flat, j, share, 1), 1)
    att_share = jnp.stack(by_place(att_came))
    lowrank_out = dot("nct,nrc->tr", att_share, down_all)
    tokens_share = chunk_of(tokens, me, share, 0).astype(F32)
    hidden = tokens_share + dot("nct,ncd->td", att_share, all_branch)
    scaled_two, inverse_two, normed_two = normalize(hidden, gains[1])

    grad_normed_two, mixed_parts, _, *grads_feed = feed_forward(
        normed_two, cotangent, jnp.transpose(w_gate_up, (1, 0, 2)), w_down, n, dp
    )
    grad_normed_two = grad_normed_two.astype(F32)
    weighted = grad_normed_two * gains[1]
    grad_hidden = chunk_of(cotangent, me, share, 0).astype(F32) + inverse_two * (
        weighted - scaled_two * jnp.mean(weighted * scaled_two, axis=-1, keepdims=True)
    )
    gain_two = jnp.sum(grad_normed_two * scaled_two, axis=0)
    grad_branch = grad_hidden.astype(BF16)

    grad_att_share = dot("ncd,td->nct", all_branch, grad_branch).astype(BF16)
    back = by_place(exchange(lambda j: pick(grad_att_share, j, 0), 1))
    grad_attended = jnp.concatenate(back, axis=1).reshape(groups, query_width, token_rows)
    mixed = lax.psum_scatter(mixed_parts, "tensor", scatter_dimension=0, tiled=True).astype(F32)
    output = (hidden + mixed).astype(BF16)

    grad_joined, grad_maps = attention_backward(
        low, cosines, sines, maps_t, maps, seg_row, seg_col, attended, root, grad_attended, heads
    )
    flat_joined = grad_joined.reshape(groups * joined_width, token_rows)
    width = model_width // dp
    core = lax.axis_index("dp") & 1

    def of_core(array, which):
        return jnp.concatenate([chunk_of(array, 2 * q + which, width, 1) for q in range(dp // 2)], axis=1)

    flat_att = att_share.reshape(-1, share)
    att_mate = lax.ppermute(flat_att, "dp", flip(dp, 0))
    branch_own = of_core(grad_branch, core)
    branch_mate = lax.ppermute(of_core(grad_branch, 1 - core), "dp", flip(dp, 0))
    first_send, first_keep, second_send, second_keep = grads_feed
    rest = list(range(1, bits_of(dp)))
    grad_normed_one, feed_a, feed_b, out_branch, qkv_a, qkv_b = tail(
        flat_joined, w_joined, normed_one, flat_att, att_mate, branch_own, branch_mate,
        (
            first_keep, lax.ppermute(first_send, "dp", flip(dp, rest[0])),
            second_keep, lax.ppermute(second_send, "dp", flip(dp, rest[-1])),
        ),
        n, dp,
    )
    grad_normed_one = grad_normed_one.astype(F32)
    scaled_one, inverse_one, _ = normalize(tokens_share, gains[0])
    weighted = grad_normed_one * gains[0]
    grad_input = (
        grad_hidden
        + inverse_one
        * (weighted - scaled_one * jnp.mean(weighted * scaled_one, axis=-1, keepdims=True))
    ).astype(BF16)
    gain_one = jnp.sum(grad_normed_one * scaled_one, axis=0)

    out_feed = jnp.concatenate([feed_a, feed_b], axis=0).astype(F32).reshape(3, width, -1)
    out_gate_up = jnp.transpose(out_feed[:2], (1, 0, 2))
    out_down = out_feed[2].T
    out_branch = out_branch.T.astype(F32)
    out_qkv = jnp.concatenate([qkv_a, qkv_b], axis=0).astype(F32).reshape(width, groups, joined_width)

    lowrank_low = lowrank.astype(BF16)
    grad_up = jnp.concatenate(
        [dot("tr,kct->rkc", lowrank_low[:, j], grad_joined[:, a:b]) for j, (a, b) in enumerate(edges)],
        axis=2,
    )
    grad_maps = jnp.transpose(grad_maps, (0, 2, 1, 3)).reshape(groups, HEAD_SIZE, -1)
    small = jnp.concatenate(
        [
            jnp.moveaxis(grad_up.reshape(rank, groups, dp, -1), 2, 0).reshape(dp, -1),
            jnp.moveaxis(grad_maps.reshape(groups, HEAD_SIZE, dp, -1), 2, 0).reshape(dp, -1),
        ],
        axis=1,
    )
    small = scatter_small(small, False)
    cut = rank * groups * (joined_width // dp)
    out_up = small[:cut].reshape(rank, groups, -1)
    out_maps = small[cut:].reshape(groups, HEAD_SIZE, -1)

    grad_lowrank = dot("kct,jrkc->jrt", grad_joined, up_wide).astype(BF16)
    grad_qkv_down = dot("jrt,td->jrd", grad_lowrank, normed_one)
    grad_lowrank_out = dot("td,rd->tr", grad_branch, o_up).astype(BF16)
    grad_o_up = dot("tr,td->rd", lowrank_out.astype(BF16), grad_branch)
    grad_o_down = dot("tr,nct->nrc", grad_lowrank_out, att_share)
    shared = jnp.concatenate(
        [gain_one[None], gain_two[None], grad_qkv_down.reshape(-1, model_width), grad_o_up], axis=0
    )
    lines = shared.shape[0]
    shared = jnp.transpose(shared.reshape(lines, dp, n, -1), (1, 2, 0, 3)).reshape(dp, n, -1)
    downs = grad_o_down.reshape(n, rank, groups, dp, -1)
    downs = jnp.transpose(downs, (3, 0, 1, 2, 4)).reshape(dp, n, -1)
    cut = shared.shape[2]
    packed = scatter_small(jnp.concatenate([shared, downs], axis=2), True)
    shared = packed[:cut].reshape(lines, -1)
    out_o_down = packed[cut:].reshape(rank, groups, -1)
    return (
        output,
        grad_input,
        shared[:2],
        out_qkv,
        shared[2:lines - rank].reshape(3, rank, -1),
        out_up,
        out_maps,
        out_branch,
        out_o_down,
        shared[lines - rank:],
        out_gate_up,
        out_down,
    )


def solution(mesh):
    in_specs = (
        P("dp", None),
        P("dp", None),
        P("dp", None),
        P(),
        P(None, "tensor", None),
        P(),
        P(None, "tensor", None),
        P("tensor", None, None),
        P("tensor", None),
        P(None, "tensor", None),
        P(),
        P(None, None, "tensor"),
        P("tensor", None),
    )
    out_specs = (
        P(("dp", "tensor"), None),
        P(("dp", "tensor"), None),
        P(None, ("dp", "tensor")),
        P("dp", "tensor", None),
        P(None, None, ("dp", "tensor")),
        P(None, "tensor", "dp"),
        P("tensor", None, "dp"),
        P("tensor", "dp"),
        P(None, "tensor", "dp"),
        P(None, ("dp", "tensor")),
        P("dp", None, "tensor"),
        P("tensor", "dp"),
    )
    return jax.shard_map(
        local, mesh=mesh, in_specs=in_specs, out_specs=out_specs, check_vma=False
    )
```

```python
from functools import partial
import jax, jax.numpy as jnp
from jax import lax
from jax.experimental import pallas as pl
from jax.experimental.pallas import tpu as pltpu
from jax.sharding import PartitionSpec as P

HEADS = 32
KVH = 8
HEAD_SIZE = 64
WINDOW = 64
LONGEST = 512
epsilon = 1e-05
rope_base = 500000.0
F32 = jnp.float32
BF16 = jnp.bfloat16


def nn(a, b):
    return lax.dot_general(a, b, (((1,), (0,)), ((), ())), preferred_element_type=F32)


def nt(a, b):
    return lax.dot_general(a, b, (((1,), (1,)), ((), ())), preferred_element_type=F32)


def rotate_t(part, cosines, sines):
    half = part.shape[0] // 2
    a, b = part[:half], part[half:]
    return jnp.concatenate([a * cosines - b * sines, b * cosines + a * sines], axis=0)


def rotate_back_t(part, cosines, sines):
    half = part.shape[0] // 2
    a, b = part[:half], part[half:]
    return jnp.concatenate([a * cosines + b * sines, b * cosines - a * sines], axis=0)


def softmaxes_t(logits):
    up = jnp.exp(logits - jnp.max(logits, axis=0, keepdims=True))
    down = jnp.exp(jnp.min(logits, axis=0, keepdims=True) - logits)
    up = up * (1.0 / jnp.sum(up, axis=0, keepdims=True))
    down = down * (1.0 / jnp.sum(down, axis=0, keepdims=True))
    return up, down


def tile_plan(length, block):
    back = LONGEST // block
    return [(i, list(range(max(0, i - back), i + 1))) for i in range(length // block)]


def tile_masks(same, query_block, key_block, block):
    lowest = (query_block - key_block) * block - (block - 1)
    if lowest >= WINDOW:
        return None, same
    shape = (block, block)
    distance = (
        lax.broadcasted_iota(jnp.int32, shape, 1)
        - lax.broadcasted_iota(jnp.int32, shape, 0)
        + (query_block - key_block) * block
    )
    inside = same & (distance < WINDOW)
    if lowest < 0:
        inside = inside & (distance >= 0)
    return inside, same & (distance >= WINDOW)


def forward_kernel(heads, block, joined_ref, cos_ref, sin_ref, map_ref, row_ref, col_ref,
                   low_ref, att_ref, root_ref, keys, kfeat):
    length = cos_ref.shape[1]
    width = heads * HEAD_SIZE
    scale = HEAD_SIZE ** -0.5
    key_t = rotate_t(joined_ref[0, width:width + HEAD_SIZE], cos_ref[...], sin_ref[...]).astype(BF16)
    low_ref[0, width:width + HEAD_SIZE] = key_t
    value_t = joined_ref[0, width + HEAD_SIZE:].astype(BF16)
    low_ref[0, width + HEAD_SIZE:] = value_t
    up, down = softmaxes_t(nn(map_ref[0, width:], key_t))
    kfeat[...] = jnp.concatenate([up, down], axis=0).T.astype(BF16)
    keys[...] = key_t.astype(F32).T.astype(BF16)

    for i, tiles in tile_plan(length, block):
        cols = slice(i * block, (i + 1) * block)

        def one_head(h, carry, i=i, tiles=tiles, cols=cols):
            rows = pl.ds(pl.multiple_of(h * HEAD_SIZE, HEAD_SIZE), HEAD_SIZE)
            query = rotate_t(joined_ref[0, rows, cols], cos_ref[:, cols], sin_ref[:, cols]).astype(BF16)
            low_ref[0, rows, cols] = query
            up, down = softmaxes_t(nn(map_ref[0, rows], query))
            feat = jnp.concatenate([up, down], axis=0).astype(BF16)
            weights = []
            total = None
            for j in tiles:
                span = slice(j * block, (j + 1) * block)
                same = col_ref[span, :] == row_ref[:, cols]
                inside, far = tile_masks(same, i, j, block)
                linear = nn(kfeat[span, :], feat)
                w = jnp.where(far, linear, 0.0)
                if inside is not None:
                    w = jnp.where(inside, jnp.exp(nn(keys[span, :], query) * scale), w)
                part = jnp.sum(w, axis=0, keepdims=True)
                total = part if total is None else total + part
                weights.append(w)
            root = lax.rsqrt(total)
            root_ref[0, h, :, cols] = root
            att = None
            for j, w in zip(tiles, weights):
                p = (w * root * root).astype(BF16)
                piece = nn(low_ref[0, width + HEAD_SIZE:, j * block:(j + 1) * block], p)
                att = piece if att is None else att + piece
            att_ref[0, rows, cols] = att.astype(BF16)
            return carry

        lax.fori_loop(0, heads, one_head, 0)


def attention_forward(joined_t, cosines, sines, maps_t, seg_row, seg_col, heads, block=256):
    groups, width, length = joined_t.shape
    qw = heads * HEAD_SIZE
    whole = lambda shape: pl.BlockSpec(shape, lambda g: (0,) * len(shape))
    mine = lambda shape: pl.BlockSpec((1,) + shape, lambda g: (g,) + (0,) * len(shape))
    return pl.pallas_call(
        partial(forward_kernel, heads, block),
        grid=(groups,),
        out_shape=(
            jax.ShapeDtypeStruct((groups, width, length), BF16),
            jax.ShapeDtypeStruct((groups, qw, length), BF16),
            jax.ShapeDtypeStruct((groups, heads, 1, length), F32),
        ),
        in_specs=[mine((width, length)), whole(cosines.shape), whole(sines.shape),
                  mine(maps_t.shape[1:]), whole(seg_row.shape), whole(seg_col.shape)],
        out_specs=(mine((width, length)), mine((qw, length)), mine((heads, 1, length))),
        scratch_shapes=[pltpu.VMEM((length, HEAD_SIZE), BF16), pltpu.VMEM((length, 2 * HEAD_SIZE), BF16)],
        compiler_params=pltpu.CompilerParams(vmem_limit_bytes=48 * 2**20),
        cost_estimate=pl.CostEstimate(flops=22 * 10**9, bytes_accessed=10**7, transcendentals=10**6),
        name="attention_forward",
    )(joined_t, cosines, sines, maps_t, seg_row, seg_col)


def backward_kernel(heads, block, low_ref, cos_ref, sin_ref, map_ref, back_ref, row_ref, col_ref,
                    att_ref, root_ref, gatt_ref, grad_ref, gmap_ref,
                    keys, kfeat, kfeat_t, values, gkeys, gkfeat, gvalues):
    length = cos_ref.shape[1]
    width = heads * HEAD_SIZE
    scale = HEAD_SIZE ** -0.5
    key_t = low_ref[0, width:width + HEAD_SIZE]
    key_up, key_down = softmaxes_t(nn(map_ref[0, width:], key_t))
    both = jnp.concatenate([key_up, key_down], axis=0)
    kfeat_t[...] = both.astype(BF16)
    kfeat[...] = both.T.astype(BF16)
    keys[...] = key_t.astype(F32).T.astype(BF16)
    values[...] = low_ref[0, width + HEAD_SIZE:].astype(F32).T.astype(BF16)
    gkeys[...] = jnp.zeros_like(gkeys)
    gkfeat[...] = jnp.zeros_like(gkfeat)
    gvalues[...] = jnp.zeros_like(gvalues)
    gmap_ref[...] = jnp.zeros_like(gmap_ref)

    for i, tiles in tile_plan(length, block):
        cols = slice(i * block, (i + 1) * block)

        def one_head(h, carry, i=i, tiles=tiles, cols=cols):
            rows = pl.ds(pl.multiple_of(h * HEAD_SIZE, HEAD_SIZE), HEAD_SIZE)
            query = low_ref[0, rows, cols]
            gatt = gatt_ref[0, rows, cols]
            up, down = softmaxes_t(nn(map_ref[0, rows], query))
            feat = jnp.concatenate([up, down], axis=0).astype(BF16)
            root = root_ref[0, h, :, cols]
            inverse = root * root
            delta = jnp.sum(gatt.astype(F32) * att_ref[0, rows, cols].astype(F32), axis=0, keepdims=True)
            gquery = jnp.zeros((HEAD_SIZE, block), F32)
            gfeat = jnp.zeros((2 * HEAD_SIZE, block), F32)
            for j in tiles:
                span = slice(j * block, (j + 1) * block)
                same = col_ref[span, :] == row_ref[:, cols]
                inside, far = tile_masks(same, i, j, block)
                gprob = nn(values[span, :], gatt) - delta
                grad_far = jnp.where(far, gprob * root * root, 0.0).astype(BF16)
                p = jnp.where(far, nn(kfeat[span, :], feat) * root * root, 0.0)
                if inside is not None:
                    near = jnp.where(inside, jnp.exp(nn(keys[span, :], query) * scale) * root * root, 0.0)
                    p = jnp.where(inside, near, p)
                    grad_near = (near * gprob * scale).astype(BF16)
                    gquery = gquery + nn(low_ref[0, width:width + HEAD_SIZE, span], grad_near)
                    gkeys[span, :] += nt(grad_near, query)
                gvalues[span, :] += nt(p.astype(BF16), gatt)
                gfeat = gfeat + nn(kfeat_t[:, span], grad_far)
                gkfeat[span, :] += nt(grad_far, feat)
            glogits = softmaxes_back_t(up, down, gfeat)
            gquery = gquery + nn(back_ref[0, h], glogits)
            gmap_ref[0, h] += nt(query, glogits)
            grad_ref[0, rows, cols] = rotate_back_t(gquery, cos_ref[:, cols], sin_ref[:, cols]).astype(BF16)
            return carry

        lax.fori_loop(0, heads, one_head, 0)
    glogits = softmaxes_back_t(key_up, key_down, gkfeat[...].T)
    gkey_t = gkeys[...].T + nn(back_ref[0, heads], glogits)
    gmap_ref[0, heads] = nt(key_t, glogits)
    grad_ref[0, width:width + HEAD_SIZE] = rotate_back_t(gkey_t, cos_ref[...], sin_ref[...]).astype(BF16)
    grad_ref[0, width + HEAD_SIZE:] = gvalues[...].T.astype(BF16)


def softmaxes_back_t(up, down, grads):
    gup, gdown = grads[:HEAD_SIZE], grads[HEAD_SIZE:]
    return (
        up * (gup - jnp.sum(gup * up, axis=0, keepdims=True))
        - down * (gdown - jnp.sum(gdown * down, axis=0, keepdims=True))
    ).astype(BF16)


def attention_backward(low, cosines, sines, maps_t, maps, seg_row, seg_col, att, root, gatt, heads, block=256):
    groups, width, length = low.shape
    qw = heads * HEAD_SIZE
    whole = lambda shape: pl.BlockSpec(shape, lambda g: (0,) * len(shape))
    mine = lambda shape: pl.BlockSpec((1,) + shape, lambda g: (g,) + (0,) * len(shape))
    return pl.pallas_call(
        partial(backward_kernel, heads, block),
        grid=(groups,),
        out_shape=(
            jax.ShapeDtypeStruct((groups, width, length), BF16),
            jax.ShapeDtypeStruct((groups, heads + 1, HEAD_SIZE, HEAD_SIZE), F32),
        ),
        in_specs=[mine((width, length)), whole(cosines.shape), whole(sines.shape),
                  mine(maps_t.shape[1:]), mine(maps.shape[1:]), whole(seg_row.shape), whole(seg_col.shape),
                  mine((qw, length)), mine((heads, 1, length)), mine((qw, length))],
        out_specs=(mine((width, length)), mine((heads + 1, HEAD_SIZE, HEAD_SIZE))),
        scratch_shapes=[
            pltpu.VMEM((length, HEAD_SIZE), BF16), pltpu.VMEM((length, 2 * HEAD_SIZE), BF16),
            pltpu.VMEM((2 * HEAD_SIZE, length), BF16), pltpu.VMEM((length, HEAD_SIZE), BF16),
            pltpu.VMEM((length, HEAD_SIZE), F32), pltpu.VMEM((length, 2 * HEAD_SIZE), F32),
            pltpu.VMEM((length, HEAD_SIZE), F32)],
        compiler_params=pltpu.CompilerParams(vmem_limit_bytes=48 * 2**20),
        cost_estimate=pl.CostEstimate(flops=40 * 10**9, bytes_accessed=10**7, transcendentals=10**6),
        name="attention_backward",
    )(low, cosines, sines, maps_t, maps, seg_row, seg_col, att, root, gatt)


def rotary_tables_t(length, width):
    half = width // 2
    frequency = rope_base ** (-(jnp.arange(half, dtype=F32) * 2.0) / width)
    angles = frequency[:, None] * jnp.arange(length, dtype=F32)[None, :]
    return jnp.cos(angles), jnp.sin(angles)


def normalize(values, gain_row):
    inverse = lax.rsqrt(jnp.mean(values * values, axis=-1, keepdims=True) + epsilon)
    scaled = values * inverse
    return scaled, inverse, (scaled * gain_row).astype(BF16)


def feed_kernel(
    n, dp, tile, cut,
    normed_in, cot_in, gate_up_in, down_in,
    sum_out, mixed_out, came, first_send, first_keep, second_send, second_keep,
    gate_up, down, normed, cots, acts, grads, arriving, sending, mixed, turned,
    load_sems, weight_sems, out_sems, core_send, core_recv, fill_sems, gather_send, gather_recv, sum_send, sum_recv, mixed_sems,
):
    share, width = normed_in.shape
    hidden = down_in.shape[0]
    block = width // dp
    piece = share // cut
    per = hidden // tile
    me = lax.axis_index("tensor")
    mine = lax.axis_index("dp")
    core = lax.rem(mine, 2)
    mate = {"dp": mine + 1 - 2 * core}
    place = (me, n - 1 - me)
    ends = (me < n - 1, me > 0)
    partner = (me + 1, me - 1)

    def device(way):
        return {"tensor": partner[way]}

    def rows_of(j, size=share):
        return pl.ds(pl.multiple_of(j * share, 16), size)

    barrier = pltpu.get_barrier_semaphore()
    for way in range(2):

        @pl.when(ends[way])
        def _(way=way):
            pl.semaphore_signal(barrier, inc=1, device_id=device(way), device_id_type=pl.DeviceIdType.MESH)

    pl.semaphore_signal(barrier, inc=1, device_id=mate, device_id_type=pl.DeviceIdType.MESH)
    own_load = pltpu.make_async_copy(normed_in, normed.at[rows_of(me)], load_sems.at[0])
    cot_load = pltpu.make_async_copy(cot_in, cots, load_sems.at[1])
    own_load.start()

    def weight_loads(f):
        span = slice(f * tile, (f + 1) * tile)
        return (
            pltpu.make_async_copy(gate_up_in.at[0, :, span], gate_up.at[0:width, span], weight_sems.at[0, f]),
            pltpu.make_async_copy(gate_up_in.at[1, :, span], gate_up.at[width:2 * width, span], weight_sems.at[1, f]),
            pltpu.make_async_copy(down_in.at[span], down.at[span], weight_sems.at[2, f]),
        )

    weights = [weight_loads(f) for f in range(per)]
    for load in weights[0]:
        load.start()
    cot_load.start()
    for loads in weights[1:]:
        for load in loads:
            load.start()
    inner = (me > 0) & (me < n - 1)

    @pl.when(inner)
    def _():
        pl.semaphore_wait(barrier, 3)

    @pl.when(jnp.logical_not(inner))
    def _():
        pl.semaphore_wait(barrier, 2)

    def gather(way, j):
        return pltpu.make_async_remote_copy(
            src_ref=normed.at[rows_of(j)], dst_ref=normed.at[rows_of(j)],
            send_sem=gather_send.at[way, j], recv_sem=gather_recv.at[way, j],
            device_id=device(way), device_id_type=pl.DeviceIdType.MESH)

    def gather_arrival(way, j):
        return pltpu.make_async_copy(normed.at[rows_of(j)], normed.at[rows_of(j)], gather_recv.at[way, j])

    def pass_on(way, j, q):
        rows = pl.ds(pl.multiple_of(j * share + q * piece, 16), piece)
        last = j == partner[way]
        slot = jnp.where(last, n, j) if way else j
        goal = pl.ds(pl.multiple_of(slot * share + q * piece, 16), piece)
        return pltpu.make_async_remote_copy(
            src_ref=sending.at[rows], dst_ref=arriving.at[goal],
            send_sem=sum_send.at[way, j * cut + q], recv_sem=sum_recv.at[way, j * cut + q],
            device_id=device(way), device_id_type=pl.DeviceIdType.MESH)

    def sum_arrival(way, j, q, slot):
        rows = pl.ds(pl.multiple_of(slot * share + q * piece, 16), piece)
        return pltpu.make_async_copy(arriving.at[rows], arriving.at[rows], sum_recv.at[way, j * cut + q])

    own_load.wait()
    for way in range(2):

        @pl.when(ends[way])
        def _(way=way):
            gather(way, me).start()

    def first_half(rows, f):
        span = pl.ds(pl.multiple_of(f * tile, tile), tile)
        upper = pl.ds(pl.multiple_of(hidden + f * tile, tile), tile)
        gate = nn(normed[rows, :], gate_up[0:width, span])
        up = nn(normed[rows, :], gate_up[width:2 * width, span])
        grad_act = nt(cots[rows, :], down[span, :])
        sigma = 1.0 / (1.0 + jnp.exp(-gate))
        silu = gate * sigma
        acts[rows, span] = (silu * up).astype(BF16)
        grads[rows, span] = (grad_act * up * (sigma + silu * (1.0 - sigma))).astype(BF16)
        grads[rows, upper] = (grad_act * silu).astype(BF16)

    def second_half(rows):
        @pl.loop(0, width // tile)
        def _(d):
            span = pl.ds(pl.multiple_of(d * tile, tile), tile)
            lower = pl.ds(pl.multiple_of(width + d * tile, tile), tile)
            sending[rows, span] = (
                nt(grads[rows, 0:hidden], gate_up[span, :]) + nt(grads[rows, hidden:], gate_up[lower, :])
            ).astype(BF16)

    both = jnp.minimum(me, n - 1 - me)
    long_side = jnp.where(me < n - 1 - me, 1, -1)

    def chunk_at(k):
        near = (k + 1) // 2 * (-1 if k % 2 else 1)
        return me + jnp.where(k <= 2 * both, near, (k - both) * long_side)

    def chunk_rows(k):
        return rows_of(chunk_at(k) if k else me)

    def put_mixed(k):
        return pltpu.make_async_copy(mixed, mixed_out.at[chunk_rows(k)], mixed_sems)

    def mix(k):
        if k:
            put_mixed(k - 1).wait()

        @pl.loop(0, width // tile)
        def _(d):
            span = pl.ds(pl.multiple_of(d * tile, tile), tile)
            mixed[:, span] = nn(acts[chunk_rows(k), :], down[:, span]).astype(BF16)

        put_mixed(k).start()

    for f in range(per):
        for load in weights[f]:
            load.wait()
        if f == 0:
            cot_load.wait()
        first_half(rows_of(me), f)
    second_half(rows_of(me))

    for k in range(1, n):
        mix(k - 1)
        for way in range(2):
            j = me - k if way == 0 else me + k
            there = (me >= k) if way == 0 else (me + k <= n - 1)

            @pl.when(there)
            def _(way=way, j=j):
                gather_arrival(way, j).wait()

                @pl.when(ends[way])
                def _():
                    gather(way, j).start()

        rows = chunk_rows(k)

        @pl.loop(0, per)
        def _(f):
            first_half(rows, f)

        second_half(rows)
        for way in range(2):

            @pl.when(place[way] == 0)
            def _(way=way):
                j = me + k if way == 0 else me - k
                for q in range(cut):
                    pass_on(way, j, q).start()

    room = 3 * block
    half = dp // 4
    items = dp // 2 * 2 * per

    def staged(pair, j, start=0, size=room):
        first = pl.multiple_of((lax.rem(pair, 2) * 2 + j) * room + start, 16)
        return gate_up.at[pl.ds(first, size)]

    def put_across(pair, j):
        return pltpu.make_async_remote_copy(
            src_ref=staged(pair, j), dst_ref=came.at[2 * pair + j],
            send_sem=core_send.at[pair, j], recv_sem=core_recv.at[pair, j],
            device_id=mate, device_id_type=pl.DeviceIdType.MESH)

    def fill(pair, j):
        return pltpu.make_async_copy(came.at[2 * (pair - half) + j], staged(pair, j), fill_sems.at[j])

    def put_own(pair, j, act):
        q = 2 * (pair - half) + j
        quarter = dp // 4
        rows = room // 2
        place = lax.div(mine, 2)
        for part, (other, keep, slot, goes) in enumerate((
            (first_send, first_keep, lax.div(q, 2), lax.rem(q, 2) != lax.rem(place, 2)),
            (second_send, second_keep, lax.rem(q, quarter), lax.div(q, quarter) != lax.div(place, quarter)),
        )):
            for ref, chosen in ((other, goes), (keep, jnp.logical_not(goes))):

                @pl.when(chosen)
                def _(ref=ref, part=part, slot=slot):
                    copy = pltpu.make_async_copy(
                        staged(pair, j, part * rows, rows), ref.at[slot], out_sems.at[lax.rem(pair, 2), j, part])
                    if act == "start":
                        copy.start()
                    else:
                        copy.wait()

    def weight_item(i):
        pair, f = lax.div(i, 2 * per), lax.rem(i, 2 * per)
        slot = lax.rem(pair, 2)
        other = lax.div(pair, half)

        def turn(source):
            for j in range(2):
                column = 2 * (2 * lax.rem(pair, half) + j) + lax.rem(core + 1 + other, 2)
                span = pl.ds(pl.multiple_of(column * block, block), block)
                turned[pl.ds(j * block, block), :] = source[:, span].T

        def store(row, goal, product):
            for j in range(2):
                start = pl.multiple_of((slot * 2 + j) * room + row * block, 16)
                rows = pl.ds(start, block)
                part = product[j * block:(j + 1) * block]

                @pl.when(pair < half)
                def _(rows=rows, part=part):
                    gate_up[rows, goal] = part.astype(BF16)

                @pl.when(pair >= half)
                def _(rows=rows, part=part):
                    gate_up[rows, goal] = (gate_up[rows, goal].astype(F32) + part).astype(BF16)

        @pl.when(f == 0)
        def _():
            @pl.when((pair >= 2) & (pair < half))
            def _():
                for j in range(2):
                    put_across(pair - 2, j).wait_send()

            @pl.when(pair >= half)
            def _():
                for j in range(2):
                    fill(pair, j).wait()

            turn(normed)

        @pl.when(f == per)
        def _():
            turn(cots)
            following = pair + 1

            @pl.when((following >= half) & (following < 2 * half))
            def _():
                @pl.when(following - 2 < half)
                def _():
                    for j in range(2):
                        put_across(following - 2, j).wait_send()

                @pl.when(following - 2 >= half)
                def _():
                    for j in range(2):
                        put_own(following - 2, j, "wait")

                for j in range(2):
                    put_across(following - half, j).wait_recv()
                    fill(following, j).start()

        @pl.when(f < per)
        def _():
            goal = pl.ds(pl.multiple_of(f * tile, tile), tile)
            for row in range(2):
                span = pl.ds(pl.multiple_of(row * hidden + f * tile, tile), tile)
                store(row, goal, nn(turned[...], grads[:, span]))

        @pl.when(f >= per)
        def _():
            goal = pl.ds(pl.multiple_of((f - per) * tile, tile), tile)
            store(2, goal, nn(turned[...], acts[:, goal]))

        @pl.when(f == 2 * per - 1)
        def _():
            @pl.when(pair < half)
            def _():
                for j in range(2):
                    put_across(pair, j).start()

            @pl.when(pair >= half)
            def _():
                for j in range(2):
                    put_own(pair, j, "start")

    first_step, last_step = cut + 1, cut * (n - 1) + n - 2
    every = -(-items // (last_step - first_step))

    def serve(step):
        for way in range(2):
            count = step - place[way]
            j_place = lax.div(count, cut) + 1
            q = lax.rem(count, cut)
            j = j_place if way == 0 else n - 1 - j_place

            @pl.when((place[way] > 0) & (j_place > place[way]) & (j_place < n))
            def _(way=way, j=j, q=q):
                sum_arrival(way, j, q, j).wait()
                rows = pl.ds(pl.multiple_of(j * share + q * piece, 16), piece)
                sending[rows, :] = (sending[rows, :].astype(F32) + arriving[rows, :].astype(F32)).astype(BF16)
                pass_on(way, j, q).start()

    @pl.loop(first_step, last_step)
    def _(step):
        serve(step)
        for j in range(every):
            item = (step - first_step) * every + j

            @pl.when(item < items)
            def _(item=item):
                weight_item(item)


    mix(n - 1)

    for way in range(2):

        @pl.when(place[way] > 0)
        def _(way=way):
            for q in range(cut):
                slot = n if way else me
                sum_arrival(way, me, q, slot).wait()
            slot = pl.ds(n * share, share) if way else rows_of(me)

            @pl.loop(0, width // tile)
            def _(d):
                span = pl.ds(pl.multiple_of(d * tile, tile), tile)
                sending[rows_of(me), span] = (
                    sending[rows_of(me), span].astype(F32) + arriving[slot, span].astype(F32)
                ).astype(BF16)

    final = pltpu.make_async_copy(sending.at[rows_of(me)], sum_out, load_sems.at[0])
    final.start()
    for pair in (2 * half - 2, 2 * half - 1):
        for j in range(2):
            put_own(pair, j, "wait")
    put_mixed(n - 1).wait()
    final.wait()
    for way in range(2):

        @pl.when(ends[way])
        def _(way=way):
            @pl.loop(0, n)
            def _(j):
                sent = (j <= me) if way == 0 else (j >= me)

                @pl.when(sent)
                def _():
                    gather(way, j).wait_send()

                @pl.when(jnp.logical_not(sent))
                def _():
                    for q in range(cut):
                        pass_on(way, j, q).wait_send()


def feed_forward(normed, cotangent, gate_up, down, n, dp, tile=512, cut=4):
    share, width = normed.shape
    hidden = down.shape[0]
    tokens = n * share
    block = width // dp
    anywhere = pl.BlockSpec(memory_space=pl.ANY)
    return pl.pallas_call(
        partial(feed_kernel, n, dp, tile, cut),
        out_shape=(
            jax.ShapeDtypeStruct((share, width), BF16),
            jax.ShapeDtypeStruct((tokens, width), BF16),
            jax.ShapeDtypeStruct((dp // 2, 3 * block, hidden), BF16),
            jax.ShapeDtypeStruct((dp // 4, 3 * block // 2, hidden), BF16),
            jax.ShapeDtypeStruct((dp // 4, 3 * block // 2, hidden), BF16),
            jax.ShapeDtypeStruct((dp // 4, 3 * block // 2, hidden), BF16),
            jax.ShapeDtypeStruct((dp // 4, 3 * block // 2, hidden), BF16),
        ),
        in_specs=[anywhere] * 4,
        out_specs=(anywhere,) * 7,
        scratch_shapes=[
            pltpu.VMEM((2 * width, hidden), BF16),
            pltpu.VMEM((hidden, width), BF16),
            pltpu.VMEM((tokens, width), BF16),
            pltpu.VMEM((tokens, width), BF16),
            pltpu.VMEM((tokens, hidden), BF16),
            pltpu.VMEM((tokens, 2 * hidden), BF16),
            pltpu.VMEM((tokens + share, width), BF16),
            pltpu.VMEM((tokens, width), BF16),
            pltpu.VMEM((share, width), BF16),
            pltpu.VMEM((2 * block, tokens), BF16),
            pltpu.SemaphoreType.DMA((2,)),
            pltpu.SemaphoreType.DMA((3, hidden // tile)),
            pltpu.SemaphoreType.DMA((2, 2, 2)),
            pltpu.SemaphoreType.DMA((dp // 4, 2)),
            pltpu.SemaphoreType.DMA((dp // 4, 2)),
            pltpu.SemaphoreType.DMA((2,)),
            pltpu.SemaphoreType.DMA((2, n)),
            pltpu.SemaphoreType.DMA((2, n)),
            pltpu.SemaphoreType.DMA((2, n * cut)),
            pltpu.SemaphoreType.DMA((2, n * cut)),
            pltpu.SemaphoreType.DMA,
        ],
        compiler_params=pltpu.CompilerParams(
            collective_id=0, has_side_effects=True, vmem_limit_bytes=60 * 2**20),
        cost_estimate=pl.CostEstimate(
            flops=18 * tokens * width * hidden, bytes_accessed=2 * 24 * 2**20, transcendentals=tokens * hidden),
        name="feed_forward",
    )(normed, cotangent, gate_up, down)


def tail_kernel(
    n, dp, tile, cut,
    joined_in, w_in, normed_in, att_in, att_mate_in, grad_in, grad_mate_in, fa_keep, fa_came, fb_keep, fb_came, small_in,
    sum_out, feed_a, feed_b, branch_out, qkv_a, qkv_b, small_out, own_out,
    joined, w, normed, att, att_mate, grad, grad_mate, arriving, sending,
    fa, fa2, fb, fb2, small, small_recvs, small_came, small_total, f_recvs, wm, w_recvs, w_done, w_last, qo, qm, qc, q_recvs,
    load_sems, out_sems, sum_send, sum_recv, f_sems, w_sems, q_sems, core_sems, last_send, last_recv, small_sems, few_send, few_recv,
):
    width = w.shape[1]
    joined_width, tokens = joined.shape
    share = tokens // n
    block = width // dp
    piece = share // cut
    columns = att.shape[0]
    me = lax.axis_index("tensor")
    mine = lax.axis_index("dp")
    core = lax.rem(mine, 2)
    bits = dp.bit_length() - 1
    mesh_id = pl.DeviceIdType.MESH
    place = (me, n - 1 - me)
    ends = (me < n - 1, me > 0)
    partner = (me + 1, me - 1)

    def own_bit(bit):
        return lax.rem(lax.div(mine, 1 << bit), 2)

    def mate(bit):
        return {"dp": mine + (1 << bit) * (1 - 2 * own_bit(bit))}

    barrier = pltpu.get_barrier_semaphore()
    for s in range(1, n):
        pl.semaphore_signal(barrier, inc=1, device_id={"tensor": lax.rem(me + s, n)}, device_id_type=mesh_id)
    for bit in range(bits):
        pl.semaphore_signal(barrier, inc=1, device_id=mate(bit), device_id_type=mesh_id)

    pairs = (
        (small_in, small), (joined_in, joined), (w_in, w), (att_in, att), (att_mate_in, att_mate), (grad_in, grad),
        (grad_mate_in, grad_mate), (normed_in, normed), (fa_keep, fa), (fa_came, fa2), (fb_keep, fb), (fb_came, fb2),
    )
    loads = [pltpu.make_async_copy(a, b, load_sems.at[i]) for i, (a, b) in enumerate(pairs)]
    for load in loads:
        load.start()
    pl.semaphore_wait(barrier, n - 1 + bits)

    def rows_of(j):
        return pl.ds(pl.multiple_of(j * share, 16), share)

    def pass_on(way, j, q):
        rows = pl.ds(pl.multiple_of(j * share + q * piece, 16), piece)
        last = j == partner[way]
        slot = jnp.where(last, n, j) if way else j
        goal = pl.ds(pl.multiple_of(slot * share + q * piece, 16), piece)
        return pltpu.make_async_remote_copy(
            src_ref=sending.at[rows], dst_ref=arriving.at[goal],
            send_sem=sum_send.at[way, j * cut + q], recv_sem=sum_recv.at[way, j * cut + q],
            device_id={"tensor": partner[way]}, device_id_type=mesh_id)

    def sum_arrival(way, j, q, slot):
        rows = pl.ds(pl.multiple_of(slot * share + q * piece, 16), piece)
        return pltpu.make_async_copy(arriving.at[rows], arriving.at[rows], sum_recv.at[way, j * cut + q])

    def halving(cur, recvs, sems, stream, order):
        steps = []
        current = cur
        for step, bit in enumerate(order):
            count = 1 << (len(order) - step - 1)
            own = own_bit(bit)

            def index(slot, which, count=count):
                return 2 * slot + which if stream == 0 else which * count + slot

            room = recvs[stream][step]
            copies = [
                pltpu.make_async_remote_copy(
                    src_ref=current(index(slot, 1 - own)), dst_ref=room.at[slot],
                    send_sem=sems.at[0, stream, step, slot], recv_sem=sems.at[1, stream, step, slot],
                    device_id=mate(bit), device_id_type=mesh_id)
                for slot in range(count)
            ]

            def start(copies=copies):
                for copy in copies:
                    copy.start()

            def finish(copies=copies, current=current, room=room, count=count, own=own, index=index):
                for slot, copy in enumerate(copies):
                    copy.wait_recv()
                    kept = current(index(slot, own))
                    total = kept.shape[0]
                    rows = 128 if total % 128 == 0 else 64 if total % 64 == 0 else total

                    @pl.loop(0, total // rows)
                    def _(r):
                        span = pl.ds(pl.multiple_of(r * rows, 16), rows)
                        room[slot, span, :] = (kept[span, :].astype(F32) + room[slot, span, :].astype(F32)).astype(room.dtype)

            def settle(copies=copies):
                for copy in copies:
                    copy.wait_send()

            steps.append((start, finish, settle))
            current = lambda i, room=room: room.at[i]
        return steps

    loads[0].wait()
    small_steps = halving(lambda i: small.at[i], [None, small_recvs], small_sems, 1, list(range(bits))[::-1])
    small_steps[0][0]()
    loads[1].wait()
    loads[2].wait()
    for k in range(n):
        distance = n - 1 - k
        for way in range(2):
            j = me + distance if way == 0 else me - distance
            there = (j < n) if way == 0 else (j >= 0)
            if distance == 0 and way:
                continue

            @pl.when(there)
            def _(j=j, way=way, distance=distance):
                rows = rows_of(j)

                @pl.loop(0, width // tile)
                def _(d):
                    span = pl.ds(pl.multiple_of(d * tile, tile), tile)
                    sending[rows, span] = lax.dot_general(
                        joined[:, pl.ds(pl.multiple_of(j * share, 128), share)], w[:, span],
                        (((0,), (0,)), ((), ())), preferred_element_type=F32).astype(BF16)

                if distance:

                    @pl.when(place[way] == 0)
                    def _():
                        for q in range(cut):
                            pass_on(way, j, q).start()

    rest = list(range(1, bits))
    half_rows = block // 2
    w_steps = [
        halving(lambda i, s=s: wm.at[i, pl.ds(s * half_rows, half_rows)], w_recvs, w_sems, s, order)
        for s, order in enumerate((rest, rest[::-1]))
    ]
    q_steps = [
        halving(lambda i, s=s: qm.at[i, pl.ds(s * half_rows, half_rows)], q_recvs, q_sems, s, order)
        for s, order in enumerate((rest, rest[::-1]))
    ]
    f_steps = [
        halving(lambda i, ref=ref: ref.at[i], f_recvs, f_sems, s, order[1:])
        for s, (ref, order) in enumerate(((fa, rest), (fb, rest[::-1])))
    ]

    def next_small(step):
        small_steps[step][1]()
        if step + 1 < bits:
            small_steps[step + 1][0]()

    next_small(0)
    for load in loads[3:7]:
        load.wait()

    @pl.loop(0, dp // 2)
    def _(q):
        span = pl.ds(pl.multiple_of(q * block, block), block)
        turned, turned_mate = grad[:, span].T, grad_mate[:, span].T
        for c in range(0, columns, tile):
            wm[q, :, c:c + tile] = (nt(turned, att[c:c + tile, :]) + nt(turned_mate, att_mate[c:c + tile, :])).astype(BF16)

    for s in range(2):
        w_steps[s][0][0]()

    loads[7].wait()

    def across(q):
        return pltpu.make_async_remote_copy(
            src_ref=qo.at[q], dst_ref=qc.at[q], send_sem=core_sems.at[0, q], recv_sem=core_sems.at[1, q],
            device_id=mate(0), device_id_type=mesh_id)

    def projection(q, which):
        column = 2 * q + which
        span = pl.ds(pl.multiple_of(column * block, block), block)
        return nt(normed[:, span].T, joined[...])

    @pl.loop(0, dp // 2)
    def _(q):
        qo[q] = projection(q, 1 - core).astype(BF16)
        across(q).start()

    @pl.loop(0, dp // 2)
    def _(q):
        product = projection(q, core)
        across(q).wait_recv()
        qm[q] = (product + qc[q].astype(F32)).astype(BF16)

    for s in range(2):
        q_steps[s][0][0]()

    for step in range(1, bits):
        next_small(step)
    for load in loads[8:]:
        load.wait()
    for one, other in ((fa, fa2), (fb, fb2)):
        for i in range(dp // 4):
            rows = 64 if one.shape[1] % 64 == 0 else one.shape[1]

            @pl.loop(0, one.shape[1] // rows)
            def _(r, one=one, other=other, i=i):
                span = pl.ds(pl.multiple_of(r * rows, 16), rows)
                one[i, span, :] = (one[i, span, :].astype(F32) + other[i, span, :].astype(F32)).astype(BF16)

    def serve(step):
        for way in range(2):
            count = step - place[way]
            reach = lax.div(count, cut)
            j_place = n - 1 - reach
            q = lax.rem(count, cut)
            j = j_place if way == 0 else n - 1 - j_place

            @pl.when((place[way] > 0) & (count >= 0) & (j_place > place[way]))
            def _(way=way, j=j, q=q):
                sum_arrival(way, j, q, j).wait()
                rows = pl.ds(pl.multiple_of(j * share + q * piece, 16), piece)
                sending[rows, :] = (sending[rows, :].astype(F32) + arriving[rows, :].astype(F32)).astype(BF16)
                pass_on(way, j, q).start()

    few = small_total.shape[0]

    def deliver_small(s):
        goal = lax.rem(me + s, n)
        return pltpu.make_async_remote_copy(
            src_ref=small_recvs[bits - 1].at[0, pl.ds(pl.multiple_of(goal * few, 8), few)],
            dst_ref=small_came.at[s - 1], send_sem=few_send.at[s - 1], recv_sem=few_recv.at[s - 1],
            device_id={"tensor": goal}, device_id_type=mesh_id)

    for s in range(1, n):
        deliver_small(s).start()
    own_copy = pltpu.make_async_copy(
        small_recvs[bits - 1].at[0, pl.ds(n * few, own_out.shape[0])], own_out, out_sems.at[6])
    own_copy.start()
    last_step = cut * (n - 2) + n - 1
    first = 1 + cut
    pl.loop(1, first)(serve)
    for step in range(len(rest)):
        for s in range(2):
            w_steps[s][step][1]()
            if step + 1 < len(rest):
                w_steps[s][step + 1][0]()
            q_steps[s][step][1]()
            if step + 1 < len(rest):
                q_steps[s][step + 1][0]()
        if step == 0:
            for s in range(2):
                f_steps[s][0][0]()
        begin = first + step * 2
        end = min(begin + 2, last_step) if step + 1 < len(rest) else last_step
        if step + 1 < len(rest):
            pl.loop(begin, end)(serve)

    own_columns = columns // n
    for s in range(2):
        w_done[pl.ds(s * half_rows, half_rows), :] = w_recvs[s][len(rest) - 1][0]

    def deliver(s):
        goal = lax.rem(me + s, n)
        return pltpu.make_async_remote_copy(
            src_ref=w_done.at[:, pl.ds(pl.multiple_of(goal * own_columns, 128), own_columns)],
            dst_ref=w_last.at[s - 1], send_sem=last_send.at[s - 1], recv_sem=last_recv.at[s - 1],
            device_id={"tensor": goal}, device_id_type=mesh_id)

    for s in range(1, n):
        deliver(s).start()
    q_outs = [
        pltpu.make_async_copy(q_recvs[s][len(rest) - 1].at[0], (qkv_a, qkv_b)[s], out_sems.at[s]) for s in range(2)
    ]
    for copy in q_outs:
        copy.start()
    pl.loop(first + 2 * (len(rest) - 1), last_step)(serve)

    for step in range(len(rest) - 1):
        for s in range(2):
            f_steps[s][step][1]()
            if step + 1 < len(rest) - 1:
                f_steps[s][step + 1][0]()
    f_outs = [
        pltpu.make_async_copy(f_recvs[s][len(rest) - 2].at[0], (feed_a, feed_b)[s], out_sems.at[2 + s]) for s in range(2)
    ]
    for copy in f_outs:
        copy.start()

    mine_columns = pl.ds(pl.multiple_of(me * own_columns, 128), own_columns)
    total = w_done[:, mine_columns].astype(F32)
    for s in range(1, n):
        deliver(s).wait_recv()
        total = total + w_last[s - 1].astype(F32)
    w_last[n - 1] = total.astype(BF16)
    branch = pltpu.make_async_copy(w_last.at[n - 1], branch_out, out_sems.at[4])
    branch.start()

    total = small_recvs[bits - 1][0, pl.ds(pl.multiple_of(me * few, 8), few), :]
    for s in range(1, n):
        deliver_small(s).wait_recv()
        total = total + small_came[s - 1]
    small_total[...] = total
    few_copy = pltpu.make_async_copy(small_total, small_out, out_sems.at[7])
    few_copy.start()

    for way in range(2):

        @pl.when(place[way] > 0)
        def _(way=way):
            for q in range(cut):
                slot = n if way else me
                sum_arrival(way, me, q, slot).wait()
            slot = pl.ds(n * share, share) if way else rows_of(me)

            @pl.loop(0, width // tile)
            def _(d):
                span = pl.ds(pl.multiple_of(d * tile, tile), tile)
                sending[rows_of(me), span] = (
                    sending[rows_of(me), span].astype(F32) + arriving[slot, span].astype(F32)
                ).astype(BF16)

    final = pltpu.make_async_copy(sending.at[rows_of(me)], sum_out, out_sems.at[5])
    final.start()
    for copy in (*q_outs, *f_outs, branch, final, own_copy, few_copy):
        copy.wait()
    for steps in (*w_steps, *q_steps, *f_steps, small_steps):
        for _, _, settle in steps:
            settle()
    for s in range(1, n):
        deliver(s).wait_send()
        deliver_small(s).wait_send()

    @pl.loop(0, dp // 2)
    def _(q):
        across(q).wait_send()

    for way in range(2):

        @pl.when(ends[way])
        def _(way=way):
            @pl.loop(0, n)
            def _(j):
                sent = (j > me) if way == 0 else (j < me)

                @pl.when(sent)
                def _():
                    for q in range(cut):
                        pass_on(way, j, q).wait_send()


def tail(joined, w, normed, att, att_mate, grad, grad_mate, feed, small, few, n, dp, tile=512, cut=4):
    joined_width, tokens = joined.shape
    width = w.shape[1]
    share = tokens // n
    block = width // dp
    columns = att.shape[0]
    steps = dp.bit_length() - 2
    feed_rows, hidden = feed[0].shape[1:]
    anywhere = pl.BlockSpec(memory_space=pl.ANY)
    half = block // 2

    def rooms(rows, cols, count):
        return [[pltpu.VMEM((1 << (count - step - 1), rows, cols), BF16) for step in range(count)] for _ in range(2)]

    def like(array):
        return pltpu.VMEM(array.shape, BF16)

    return pl.pallas_call(
        partial(tail_kernel, n, dp, tile, cut),
        out_shape=(
            jax.ShapeDtypeStruct((share, width), BF16),
            jax.ShapeDtypeStruct((feed_rows, hidden), BF16),
            jax.ShapeDtypeStruct((feed_rows, hidden), BF16),
            jax.ShapeDtypeStruct((block, columns // n), BF16),
            jax.ShapeDtypeStruct((half, joined_width), BF16),
            jax.ShapeDtypeStruct((half, joined_width), BF16),
            jax.ShapeDtypeStruct((few, small.shape[2]), F32),
            jax.ShapeDtypeStruct((small.shape[1] - n * few, small.shape[2]), F32),
        ),
        in_specs=[anywhere] * 12,
        out_specs=(anywhere,) * 8,
        scratch_shapes=[
            like(joined), like(w), like(normed), like(att), like(att_mate), like(grad), like(grad_mate),
            pltpu.VMEM((tokens + share, width), BF16),
            pltpu.VMEM((tokens, width), BF16),
            like(feed[0]), like(feed[1]), like(feed[2]), like(feed[3]),
            pltpu.VMEM(small.shape, F32),
            [pltpu.VMEM((1 << (steps - step),) + small.shape[1:], F32) for step in range(steps + 1)],
            pltpu.VMEM((n - 1, few, small.shape[2]), F32),
            pltpu.VMEM((few, small.shape[2]), F32),
            rooms(feed_rows, hidden, steps - 1),
            pltpu.VMEM((dp // 2, block, columns), BF16),
            rooms(half, columns, steps),
            pltpu.VMEM((block, columns), BF16),
            pltpu.VMEM((n, block, columns // n), BF16),
            pltpu.VMEM((dp // 2, block, joined_width), BF16),
            pltpu.VMEM((dp // 2, block, joined_width), BF16),
            pltpu.VMEM((dp // 2, block, joined_width), BF16),
            rooms(half, joined_width, steps),
            pltpu.SemaphoreType.DMA((12,)),
            pltpu.SemaphoreType.DMA((8,)),
            pltpu.SemaphoreType.DMA((2, n * cut)),
            pltpu.SemaphoreType.DMA((2, n * cut)),
            pltpu.SemaphoreType.DMA((2, 2, steps, dp // 4)),
            pltpu.SemaphoreType.DMA((2, 2, steps, dp // 4)),
            pltpu.SemaphoreType.DMA((2, 2, steps, dp // 4)),
            pltpu.SemaphoreType.DMA((2, dp // 2)),
            pltpu.SemaphoreType.DMA((n - 1,)),
            pltpu.SemaphoreType.DMA((n - 1,)),
            pltpu.SemaphoreType.DMA((2, 2, steps + 1, dp // 2)),
            pltpu.SemaphoreType.DMA((n - 1,)),
            pltpu.SemaphoreType.DMA((n - 1,)),
        ],
        compiler_params=pltpu.CompilerParams(
            collective_id=1, has_side_effects=True, vmem_limit_bytes=60 * 2**20),
        cost_estimate=pl.CostEstimate(flops=10**6, bytes_accessed=10**5, transcendentals=0),
        name="gradient_sums",
    )(joined, w, normed, att, att_mate, grad, grad_mate, *feed, small)


def ring(size, shift=1):
    return [(i, (i + shift) % size) for i in range(size)]


def flip(size, bit):
    return [(i, i ^ (1 << bit)) for i in range(size)]


def pick(array, index, axis):
    return lax.dynamic_index_in_dim(array, index, axis, keepdims=False)


def chunk_of(array, index, rows, axis):
    return lax.dynamic_slice_in_dim(array, index * rows, rows, axis)


def bits_of(size):
    return size.bit_length() - 1


def gather_weight(shard):
    piece = chunk_of(shard, lax.axis_index("dp"), shard.shape[0] // lax.axis_size("dp"), 0)
    whole = lax.all_gather(piece, ("tensor", "dp"), axis=0, tiled=True)
    return whole.reshape((lax.axis_size("tensor"),) + shard.shape)


def exchange(parts, shift):
    n = lax.axis_size("tensor")
    me = lax.axis_index("tensor")
    came = [parts(me)]
    for s in range(1, n):
        came.append(lax.ppermute(parts((me + s) % n), "tensor", ring(n, s)))
    return came


def by_place(came):
    n = len(came)
    me = lax.axis_index("tensor")
    stacked = jnp.stack(came)
    return [pick(stacked, (me + n - j) % n, 0) for j in range(n)]


def local(
    tokens,
    cotangent,
    segments,
    norm_gains,
    w_qkv,
    qkv_down,
    query_key_value_up,
    feature_maps,
    w_out,
    o_down,
    o_up,
    w_gate_up,
    w_down,
):
    token_rows, model_width = tokens.shape
    groups = w_qkv.shape[1]
    heads = HEADS // KVH
    query_width = heads * HEAD_SIZE
    joined_width = w_qkv.shape[2]
    rank = o_up.shape[0]
    dp = lax.axis_size("dp")
    n = lax.axis_size("tensor")
    me = lax.axis_index("tensor")
    share = token_rows // n
    gains = norm_gains.astype(F32)
    cosines, sines = rotary_tables_t(token_rows, HEAD_SIZE)
    dot = partial(jnp.einsum, preferred_element_type=F32)

    up = query_key_value_up.astype(BF16)
    edges = ((0, query_width), (query_width, query_width + HEAD_SIZE), (query_width + HEAD_SIZE, joined_width))
    up_wide = jnp.stack(
        [jnp.pad(up[:, :, a:b], ((0, 0), (0, 0), (a, joined_width - b))) for a, b in edges]
    )
    w_joined = (
        jnp.transpose(w_qkv, (1, 2, 0)).astype(F32) + dot("jrkc,jrd->kcd", up_wide, qkv_down)
    ).astype(BF16).reshape(groups * joined_width, model_width)
    down_flat = o_down.reshape(rank, -1)
    w_branch = (w_out.astype(F32) + dot("rc,rd->cd", down_flat, o_up)).astype(BF16)
    down_all = lax.all_gather(down_flat, "tensor")
    all_branch = gather_weight(w_branch)

    _, _, normed_one = normalize(tokens.astype(F32), gains[0])
    lowrank = dot("td,jrd->tjr", normed_one, qkv_down)
    joined = dot("cd,td->ct", w_joined, normed_one).reshape(groups, joined_width, token_rows)
    maps_t = jnp.swapaxes(feature_maps, 1, 2)
    maps = jnp.stack(
        [feature_maps[:, :, i * HEAD_SIZE:(i + 1) * HEAD_SIZE] for i in range(heads + 1)], axis=1
    )
    seg_row = segments.reshape(1, token_rows)
    seg_col = segments.reshape(token_rows, 1)
    low, attended, root = attention_forward(joined, cosines, sines, maps_t, seg_row, seg_col, heads)
    attended_flat = attended.reshape(groups * query_width, token_rows)
    att_came = exchange(lambda j: chunk_of(attended_flat, j, share, 1), 1)
    att_share = jnp.stack(by_place(att_came))
    lowrank_out = dot("nct,nrc->tr", att_share, down_all)
    tokens_share = chunk_of(tokens, me, share, 0).astype(F32)
    hidden = tokens_share + dot("nct,ncd->td", att_share, all_branch)
    scaled_two, inverse_two, normed_two = normalize(hidden, gains[1])

    grad_normed_two, mixed_parts, _, *grads_feed = feed_forward(
        normed_two, cotangent, jnp.transpose(w_gate_up, (1, 0, 2)), w_down, n, dp
    )
    grad_normed_two = grad_normed_two.astype(F32)
    weighted = grad_normed_two * gains[1]
    grad_hidden = chunk_of(cotangent, me, share, 0).astype(F32) + inverse_two * (
        weighted - scaled_two * jnp.mean(weighted * scaled_two, axis=-1, keepdims=True)
    )
    gain_two = jnp.sum(grad_normed_two * scaled_two, axis=0)
    grad_branch = grad_hidden.astype(BF16)

    grad_att_share = dot("ncd,td->nct", all_branch, grad_branch).astype(BF16)
    back = by_place(exchange(lambda j: pick(grad_att_share, j, 0), 1))
    grad_attended = jnp.concatenate(back, axis=1).reshape(groups, query_width, token_rows)
    mixed_parts, grad_attended = lax.optimization_barrier((mixed_parts, grad_attended))
    mixed_came = exchange(lambda j: chunk_of(mixed_parts, j, share, 0), 1)

    grad_joined, grad_maps = attention_backward(
        low, cosines, sines, maps_t, maps, seg_row, seg_col, attended, root, grad_attended, heads
    )
    flat_joined = grad_joined.reshape(groups * joined_width, token_rows)
    near = [part for s, part in enumerate(mixed_came) if s != n // 2]
    flat_joined, near = lax.optimization_barrier((flat_joined, near))
    mixed = sum(part.astype(F32) for part in (*near, mixed_came[n // 2]))
    lowrank_low = lowrank.astype(BF16)
    grad_up = jnp.concatenate(
        [dot("tr,kct->rkc", lowrank_low[:, j], grad_joined[:, a:b]) for j, (a, b) in enumerate(edges)],
        axis=2,
    )
    grad_maps = jnp.transpose(grad_maps, (0, 2, 1, 3)).reshape(groups, HEAD_SIZE, -1)
    small = jnp.concatenate(
        [
            jnp.moveaxis(grad_up.reshape(rank, groups, dp, -1), 2, 0).reshape(dp, -1),
            jnp.moveaxis(grad_maps.reshape(groups, HEAD_SIZE, dp, -1), 2, 0).reshape(dp, -1),
        ],
        axis=1,
    )
    grad_lowrank = dot("kct,jrkc->jrt", grad_joined, up_wide).astype(BF16)
    grad_qkv_down = dot("jrt,td->jrd", grad_lowrank, normed_one)
    grad_lowrank_out = dot("td,rd->tr", grad_branch, o_up).astype(BF16)
    grad_o_up = dot("tr,td->rd", lowrank_out.astype(BF16), grad_branch)
    grad_o_down = dot("tr,nct->nrc", grad_lowrank_out, att_share)
    gain_one = jnp.sum(dot("ct,cd->td", flat_joined, w_joined) * normed_one.astype(F32), axis=0)
    shared = jnp.concatenate(
        [gain_one[None] / gains[:1], gain_two[None], grad_qkv_down.reshape(-1, model_width), grad_o_up], axis=0
    )
    lines = shared.shape[0]
    shared = jnp.transpose(shared.reshape(lines, dp, n, -1), (1, 2, 0, 3)).reshape(dp, n, -1)
    downs = grad_o_down.reshape(n, rank, groups, dp, -1)
    downs = jnp.transpose(downs, (3, 0, 1, 2, 4)).reshape(dp, n, -1)
    packed = jnp.concatenate([shared, downs], axis=2)
    few = -(-packed.shape[2] // 1024) * 8
    packed = jnp.pad(packed, ((0, 0), (0, 0), (0, few * 128 - packed.shape[2]))).reshape(dp, n * few, 128)
    tall = -(-small.shape[1] // 1024) * 8
    small = jnp.pad(small, ((0, 0), (0, tall * 128 - small.shape[1]))).reshape(dp, tall, 128)
    packed = jnp.concatenate([packed, small], axis=1)
    width = model_width // dp
    core = lax.axis_index("dp") & 1

    def of_core(array, which):
        return jnp.concatenate([chunk_of(array, 2 * q + which, width, 1) for q in range(dp // 2)], axis=1)

    flat_att = att_share.reshape(-1, share)
    att_mate = lax.ppermute(flat_att, "dp", flip(dp, 0))
    branch_own = of_core(grad_branch, core)
    branch_mate = lax.ppermute(of_core(grad_branch, 1 - core), "dp", flip(dp, 0))
    first_send, first_keep, second_send, second_keep = grads_feed
    rest = list(range(1, bits_of(dp)))
    grad_normed_one, feed_a, feed_b, out_branch, qkv_a, qkv_b, few_small, own_small = tail(
        flat_joined, w_joined, normed_one, flat_att, att_mate, branch_own, branch_mate,
        (
            first_keep, lax.ppermute(first_send, "dp", flip(dp, rest[0])),
            second_keep, lax.ppermute(second_send, "dp", flip(dp, rest[-1])),
        ),
        packed, few, n, dp,
    )
    own_small = own_small.reshape(-1)
    cut = rank * groups * (joined_width // dp)
    out_up = own_small[:cut].reshape(rank, groups, -1)
    out_maps = own_small[cut:cut + groups * HEAD_SIZE * (feature_maps.shape[2] // dp)].reshape(groups, HEAD_SIZE, -1)
    few_small = few_small.reshape(-1)
    cut = lines * (model_width // (dp * n))
    shared = few_small[:cut].reshape(lines, -1)
    out_o_down = few_small[cut:cut + rank * groups * (query_width // dp)].reshape(rank, groups, -1)
    grad_normed_one = grad_normed_one.astype(F32)
    output = (hidden + mixed).astype(BF16)
    scaled_one, inverse_one, _ = normalize(tokens_share, gains[0])
    weighted = grad_normed_one * gains[0]
    grad_input = (
        grad_hidden
        + inverse_one
        * (weighted - scaled_one * jnp.mean(weighted * scaled_one, axis=-1, keepdims=True))
    ).astype(BF16)
    out_feed = jnp.concatenate([feed_a, feed_b], axis=0).astype(F32).reshape(3, width, -1)
    out_gate_up = jnp.transpose(out_feed[:2], (1, 0, 2))
    out_down = out_feed[2].T
    out_branch = out_branch.T.astype(F32)
    out_qkv = jnp.concatenate([qkv_a, qkv_b], axis=0).astype(F32).reshape(width, groups, joined_width)

    return (
        output,
        grad_input,
        shared[:2],
        out_qkv,
        shared[2:lines - rank].reshape(3, rank, -1),
        out_up,
        out_maps,
        out_branch,
        out_o_down,
        shared[lines - rank:],
        out_gate_up,
        out_down,
    )


def solution(mesh):
    in_specs = (
        P("dp", None),
        P("dp", None),
        P("dp", None),
        P(),
        P(None, "tensor", None),
        P(),
        P(None, "tensor", None),
        P("tensor", None, None),
        P("tensor", None),
        P(None, "tensor", None),
        P(),
        P(None, None, "tensor"),
        P("tensor", None),
    )
    out_specs = (
        P(("dp", "tensor"), None),
        P(("dp", "tensor"), None),
        P(None, ("dp", "tensor")),
        P("dp", "tensor", None),
        P(None, None, ("dp", "tensor")),
        P(None, "tensor", "dp"),
        P("tensor", None, "dp"),
        P("tensor", "dp"),
        P(None, "tensor", "dp"),
        P(None, ("dp", "tensor")),
        P("dp", None, "tensor"),
        P("tensor", "dp"),
    )
    return jax.shard_map(
        local, mesh=mesh, in_specs=in_specs, out_specs=out_specs, check_vma=False
    )
```

```python
from functools import partial
import jax, jax.numpy as jnp
from jax import lax
from jax.experimental import pallas as pl
from jax.experimental.pallas import tpu as pltpu
from jax.sharding import PartitionSpec as P

HEADS = 32
KVH = 8
HEAD_SIZE = 64
WINDOW = 64
LONGEST = 512
epsilon = 1e-05
rope_base = 500000.0
F32 = jnp.float32
BF16 = jnp.bfloat16


def nn(a, b):
    return lax.dot_general(a, b, (((1,), (0,)), ((), ())), preferred_element_type=F32)


def nt(a, b):
    return lax.dot_general(a, b, (((1,), (1,)), ((), ())), preferred_element_type=F32)


def rotate_t(part, cosines, sines):
    half = part.shape[0] // 2
    a, b = part[:half], part[half:]
    return jnp.concatenate([a * cosines - b * sines, b * cosines + a * sines], axis=0)


def rotate_back_t(part, cosines, sines):
    half = part.shape[0] // 2
    a, b = part[:half], part[half:]
    return jnp.concatenate([a * cosines + b * sines, b * cosines - a * sines], axis=0)


def softmaxes_t(logits):
    up = jnp.exp(logits - jnp.max(logits, axis=0, keepdims=True))
    down = jnp.exp(jnp.min(logits, axis=0, keepdims=True) - logits)
    up = up * (1.0 / jnp.sum(up, axis=0, keepdims=True))
    down = down * (1.0 / jnp.sum(down, axis=0, keepdims=True))
    return up, down


def tile_plan(length, block):
    back = LONGEST // block
    return [(i, list(range(max(0, i - back), i + 1))) for i in range(length // block)]


def tile_masks(same, query_block, key_block, block):
    lowest = (query_block - key_block) * block - (block - 1)
    if lowest >= WINDOW:
        return None, same
    shape = (block, block)
    distance = (
        lax.broadcasted_iota(jnp.int32, shape, 1)
        - lax.broadcasted_iota(jnp.int32, shape, 0)
        + (query_block - key_block) * block
    )
    inside = same & (distance < WINDOW)
    if lowest < 0:
        inside = inside & (distance >= 0)
    return inside, same & (distance >= WINDOW)


def forward_kernel(heads, block, joined_ref, cos_ref, sin_ref, map_ref, row_ref, col_ref,
                   low_ref, att_ref, root_ref, keys, kfeat):
    length = cos_ref.shape[1]
    width = heads * HEAD_SIZE
    scale = HEAD_SIZE ** -0.5
    key_t = rotate_t(joined_ref[0, width:width + HEAD_SIZE], cos_ref[...], sin_ref[...]).astype(BF16)
    low_ref[0, width:width + HEAD_SIZE] = key_t
    value_t = joined_ref[0, width + HEAD_SIZE:].astype(BF16)
    low_ref[0, width + HEAD_SIZE:] = value_t
    up, down = softmaxes_t(nn(map_ref[0, width:], key_t))
    kfeat[...] = jnp.concatenate([up, down], axis=0).T.astype(BF16)
    keys[...] = key_t.astype(F32).T.astype(BF16)

    for i, tiles in tile_plan(length, block):
        cols = slice(i * block, (i + 1) * block)

        def one_head(h, carry, i=i, tiles=tiles, cols=cols):
            rows = pl.ds(pl.multiple_of(h * HEAD_SIZE, HEAD_SIZE), HEAD_SIZE)
            query = rotate_t(joined_ref[0, rows, cols], cos_ref[:, cols], sin_ref[:, cols]).astype(BF16)
            low_ref[0, rows, cols] = query
            up, down = softmaxes_t(nn(map_ref[0, rows], query))
            feat = jnp.concatenate([up, down], axis=0).astype(BF16)
            weights = []
            total = None
            for j in tiles:
                span = slice(j * block, (j + 1) * block)
                same = col_ref[span, :] == row_ref[:, cols]
                inside, far = tile_masks(same, i, j, block)
                linear = nn(kfeat[span, :], feat)
                w = jnp.where(far, linear, 0.0)
                if inside is not None:
                    w = jnp.where(inside, jnp.exp(nn(keys[span, :], query) * scale), w)
                part = jnp.sum(w, axis=0, keepdims=True)
                total = part if total is None else total + part
                weights.append(w)
            root = lax.rsqrt(total)
            root_ref[0, h, :, cols] = root
            att = None
            for j, w in zip(tiles, weights):
                p = (w * root * root).astype(BF16)
                piece = nn(low_ref[0, width + HEAD_SIZE:, j * block:(j + 1) * block], p)
                att = piece if att is None else att + piece
            att_ref[0, rows, cols] = att.astype(BF16)
            return carry

        lax.fori_loop(0, heads, one_head, 0, unroll=True)


def attention_forward(joined_t, cosines, sines, maps_t, seg_row, seg_col, heads, block=256):
    groups, width, length = joined_t.shape
    qw = heads * HEAD_SIZE
    whole = lambda shape: pl.BlockSpec(shape, lambda g: (0,) * len(shape))
    mine = lambda shape: pl.BlockSpec((1,) + shape, lambda g: (g,) + (0,) * len(shape))
    return pl.pallas_call(
        partial(forward_kernel, heads, block),
        grid=(groups,),
        out_shape=(
            jax.ShapeDtypeStruct((groups, width, length), BF16),
            jax.ShapeDtypeStruct((groups, qw, length), BF16),
            jax.ShapeDtypeStruct((groups, heads, 1, length), F32),
        ),
        in_specs=[mine((width, length)), whole(cosines.shape), whole(sines.shape),
                  mine(maps_t.shape[1:]), whole(seg_row.shape), whole(seg_col.shape)],
        out_specs=(mine((width, length)), mine((qw, length)), mine((heads, 1, length))),
        scratch_shapes=[pltpu.VMEM((length, HEAD_SIZE), BF16), pltpu.VMEM((length, 2 * HEAD_SIZE), BF16)],
        compiler_params=pltpu.CompilerParams(vmem_limit_bytes=48 * 2**20),
        cost_estimate=pl.CostEstimate(flops=22 * 10**9, bytes_accessed=10**7, transcendentals=10**6),
        name="attention_forward",
    )(joined_t, cosines, sines, maps_t, seg_row, seg_col)


def backward_kernel(heads, block, low_ref, cos_ref, sin_ref, map_ref, back_ref, row_ref, col_ref,
                    att_ref, root_ref, gatt_ref, grad_ref, gmap_ref,
                    keys, kfeat, kfeat_t, values, gkeys, gkfeat, gvalues):
    length = cos_ref.shape[1]
    width = heads * HEAD_SIZE
    scale = HEAD_SIZE ** -0.5
    key_t = low_ref[0, width:width + HEAD_SIZE]
    key_up, key_down = softmaxes_t(nn(map_ref[0, width:], key_t))
    both = jnp.concatenate([key_up, key_down], axis=0)
    kfeat_t[...] = both.astype(BF16)
    kfeat[...] = both.T.astype(BF16)
    keys[...] = key_t.astype(F32).T.astype(BF16)
    values[...] = low_ref[0, width + HEAD_SIZE:].astype(F32).T.astype(BF16)
    gkeys[...] = jnp.zeros_like(gkeys)
    gkfeat[...] = jnp.zeros_like(gkfeat)
    gvalues[...] = jnp.zeros_like(gvalues)
    gmap_ref[...] = jnp.zeros_like(gmap_ref)

    for i, tiles in tile_plan(length, block):
        cols = slice(i * block, (i + 1) * block)

        def one_head(h, carry, i=i, tiles=tiles, cols=cols):
            rows = pl.ds(pl.multiple_of(h * HEAD_SIZE, HEAD_SIZE), HEAD_SIZE)
            query = low_ref[0, rows, cols]
            gatt = gatt_ref[0, rows, cols]
            up, down = softmaxes_t(nn(map_ref[0, rows], query))
            feat = jnp.concatenate([up, down], axis=0).astype(BF16)
            root = root_ref[0, h, :, cols]
            inverse = root * root
            delta = jnp.sum(gatt.astype(F32) * att_ref[0, rows, cols].astype(F32), axis=0, keepdims=True)
            gquery = jnp.zeros((HEAD_SIZE, block), F32)
            gfeat = jnp.zeros((2 * HEAD_SIZE, block), F32)
            for j in tiles:
                span = slice(j * block, (j + 1) * block)
                same = col_ref[span, :] == row_ref[:, cols]
                inside, far = tile_masks(same, i, j, block)
                gprob = nn(values[span, :], gatt) - delta
                grad_far = jnp.where(far, gprob * root * root, 0.0).astype(BF16)
                p = jnp.where(far, nn(kfeat[span, :], feat) * root * root, 0.0)
                if inside is not None:
                    near = jnp.where(inside, jnp.exp(nn(keys[span, :], query) * scale) * root * root, 0.0)
                    p = jnp.where(inside, near, p)
                    grad_near = (near * gprob * scale).astype(BF16)
                    gquery = gquery + nn(low_ref[0, width:width + HEAD_SIZE, span], grad_near)
                    gkeys[span, :] += nt(grad_near, query)
                gvalues[span, :] += nt(p.astype(BF16), gatt)
                gfeat = gfeat + nn(kfeat_t[:, span], grad_far)
                gkfeat[span, :] += nt(grad_far, feat)
            glogits = softmaxes_back_t(up, down, gfeat)
            gquery = gquery + nn(back_ref[0, h], glogits)
            gmap_ref[0, h] += nt(query, glogits)
            grad_ref[0, rows, cols] = rotate_back_t(gquery, cos_ref[:, cols], sin_ref[:, cols]).astype(BF16)
            return carry

        lax.fori_loop(0, heads, one_head, 0, unroll=True)
    glogits = softmaxes_back_t(key_up, key_down, gkfeat[...].T)
    gkey_t = gkeys[...].T + nn(back_ref[0, heads], glogits)
    gmap_ref[0, heads] = nt(key_t, glogits)
    grad_ref[0, width:width + HEAD_SIZE] = rotate_back_t(gkey_t, cos_ref[...], sin_ref[...]).astype(BF16)
    grad_ref[0, width + HEAD_SIZE:] = gvalues[...].T.astype(BF16)


def softmaxes_back_t(up, down, grads):
    gup, gdown = grads[:HEAD_SIZE], grads[HEAD_SIZE:]
    return (
        up * (gup - jnp.sum(gup * up, axis=0, keepdims=True))
        - down * (gdown - jnp.sum(gdown * down, axis=0, keepdims=True))
    ).astype(BF16)


def attention_backward(low, cosines, sines, maps_t, maps, seg_row, seg_col, att, root, gatt, heads, block=256):
    groups, width, length = low.shape
    qw = heads * HEAD_SIZE
    whole = lambda shape: pl.BlockSpec(shape, lambda g: (0,) * len(shape))
    mine = lambda shape: pl.BlockSpec((1,) + shape, lambda g: (g,) + (0,) * len(shape))
    return pl.pallas_call(
        partial(backward_kernel, heads, block),
        grid=(groups,),
        out_shape=(
            jax.ShapeDtypeStruct((groups, width, length), BF16),
            jax.ShapeDtypeStruct((groups, heads + 1, HEAD_SIZE, HEAD_SIZE), F32),
        ),
        in_specs=[mine((width, length)), whole(cosines.shape), whole(sines.shape),
                  mine(maps_t.shape[1:]), mine(maps.shape[1:]), whole(seg_row.shape), whole(seg_col.shape),
                  mine((qw, length)), mine((heads, 1, length)), mine((qw, length))],
        out_specs=(mine((width, length)), mine((heads + 1, HEAD_SIZE, HEAD_SIZE))),
        scratch_shapes=[
            pltpu.VMEM((length, HEAD_SIZE), BF16), pltpu.VMEM((length, 2 * HEAD_SIZE), BF16),
            pltpu.VMEM((2 * HEAD_SIZE, length), BF16), pltpu.VMEM((length, HEAD_SIZE), BF16),
            pltpu.VMEM((length, HEAD_SIZE), F32), pltpu.VMEM((length, 2 * HEAD_SIZE), F32),
            pltpu.VMEM((length, HEAD_SIZE), F32)],
        compiler_params=pltpu.CompilerParams(vmem_limit_bytes=48 * 2**20),
        cost_estimate=pl.CostEstimate(flops=40 * 10**9, bytes_accessed=10**7, transcendentals=10**6),
        name="attention_backward",
    )(low, cosines, sines, maps_t, maps, seg_row, seg_col, att, root, gatt)


def rotary_tables_t(length, width):
    half = width // 2
    frequency = rope_base ** (-(jnp.arange(half, dtype=F32) * 2.0) / width)
    angles = frequency[:, None] * jnp.arange(length, dtype=F32)[None, :]
    return jnp.cos(angles), jnp.sin(angles)


def normalize(values, gain_row):
    inverse = lax.rsqrt(jnp.mean(values * values, axis=-1, keepdims=True) + epsilon)
    scaled = values * inverse
    return scaled, inverse, (scaled * gain_row).astype(BF16)


def feed_kernel(
    n, dp, tile, cut,
    normed_in, cot_in, gate_up_in, down_in,
    sum_out, mixed_out, came, first_send, first_keep, second_send, second_keep,
    gate_up, down, normed, cots, acts, grads, arriving, sending, mixed, turned,
    load_sems, weight_sems, out_sems, core_send, core_recv, fill_sems, gather_send, gather_recv, sum_send, sum_recv, mixed_sems,
):
    share, width = normed_in.shape
    hidden = down_in.shape[0]
    block = width // dp
    piece = share // cut
    per = hidden // tile
    me = lax.axis_index("tensor")
    mine = lax.axis_index("dp")
    core = lax.rem(mine, 2)
    mate = {"dp": mine + 1 - 2 * core}
    place = (me, n - 1 - me)
    ends = (me < n - 1, me > 0)
    partner = (me + 1, me - 1)

    def device(way):
        return {"tensor": partner[way]}

    def rows_of(j, size=share):
        return pl.ds(pl.multiple_of(j * share, 16), size)

    barrier = pltpu.get_barrier_semaphore()
    for way in range(2):

        @pl.when(ends[way])
        def _(way=way):
            pl.semaphore_signal(barrier, inc=1, device_id=device(way), device_id_type=pl.DeviceIdType.MESH)

    pl.semaphore_signal(barrier, inc=1, device_id=mate, device_id_type=pl.DeviceIdType.MESH)
    own_load = pltpu.make_async_copy(normed_in, normed.at[rows_of(me)], load_sems.at[0])
    cot_load = pltpu.make_async_copy(cot_in, cots, load_sems.at[1])
    own_load.start()

    def weight_loads(f):
        span = slice(f * tile, (f + 1) * tile)
        return (
            pltpu.make_async_copy(gate_up_in.at[0, :, span], gate_up.at[0:width, span], weight_sems.at[0, f]),
            pltpu.make_async_copy(gate_up_in.at[1, :, span], gate_up.at[width:2 * width, span], weight_sems.at[1, f]),
            pltpu.make_async_copy(down_in.at[span], down.at[span], weight_sems.at[2, f]),
        )

    weights = [weight_loads(f) for f in range(per)]
    for load in weights[0]:
        load.start()
    cot_load.start()
    for loads in weights[1:]:
        for load in loads:
            load.start()
    inner = (me > 0) & (me < n - 1)

    @pl.when(inner)
    def _():
        pl.semaphore_wait(barrier, 3)

    @pl.when(jnp.logical_not(inner))
    def _():
        pl.semaphore_wait(barrier, 2)

    def gather(way, j):
        return pltpu.make_async_remote_copy(
            src_ref=normed.at[rows_of(j)], dst_ref=normed.at[rows_of(j)],
            send_sem=gather_send.at[way, j], recv_sem=gather_recv.at[way, j],
            device_id=device(way), device_id_type=pl.DeviceIdType.MESH)

    def gather_arrival(way, j):
        return pltpu.make_async_copy(normed.at[rows_of(j)], normed.at[rows_of(j)], gather_recv.at[way, j])

    def pass_on(way, j, q):
        rows = pl.ds(pl.multiple_of(j * share + q * piece, 16), piece)
        last = j == partner[way]
        slot = jnp.where(last, n, j) if way else j
        goal = pl.ds(pl.multiple_of(slot * share + q * piece, 16), piece)
        return pltpu.make_async_remote_copy(
            src_ref=sending.at[rows], dst_ref=arriving.at[goal],
            send_sem=sum_send.at[way, j * cut + q], recv_sem=sum_recv.at[way, j * cut + q],
            device_id=device(way), device_id_type=pl.DeviceIdType.MESH)

    def sum_arrival(way, j, q, slot):
        rows = pl.ds(pl.multiple_of(slot * share + q * piece, 16), piece)
        return pltpu.make_async_copy(arriving.at[rows], arriving.at[rows], sum_recv.at[way, j * cut + q])

    own_load.wait()
    for way in range(2):

        @pl.when(ends[way])
        def _(way=way):
            gather(way, me).start()

    def first_half(rows, f):
        span = pl.ds(pl.multiple_of(f * tile, tile), tile)
        upper = pl.ds(pl.multiple_of(hidden + f * tile, tile), tile)
        gate = nn(normed[rows, :], gate_up[0:width, span])
        up = nn(normed[rows, :], gate_up[width:2 * width, span])
        grad_act = nt(cots[rows, :], down[span, :])
        sigma = 1.0 / (1.0 + jnp.exp(-gate))
        silu = gate * sigma
        acts[rows, span] = (silu * up).astype(BF16)
        grads[rows, span] = (grad_act * up * (sigma + silu * (1.0 - sigma))).astype(BF16)
        grads[rows, upper] = (grad_act * silu).astype(BF16)

    def second_half(rows):
        @pl.loop(0, width // tile)
        def _(d):
            span = pl.ds(pl.multiple_of(d * tile, tile), tile)
            lower = pl.ds(pl.multiple_of(width + d * tile, tile), tile)
            sending[rows, span] = (
                nt(grads[rows, 0:hidden], gate_up[span, :]) + nt(grads[rows, hidden:], gate_up[lower, :])
            ).astype(BF16)

    both = jnp.minimum(me, n - 1 - me)
    long_side = jnp.where(me < n - 1 - me, 1, -1)

    def chunk_at(k):
        near = (k + 1) // 2 * (-1 if k % 2 else 1)
        return me + jnp.where(k <= 2 * both, near, (k - both) * long_side)

    def chunk_rows(k):
        return rows_of(chunk_at(k) if k else me)

    def put_mixed(k):
        return pltpu.make_async_copy(mixed, mixed_out.at[chunk_rows(k)], mixed_sems)

    def mix(k):
        if k:
            put_mixed(k - 1).wait()

        @pl.loop(0, width // tile)
        def _(d):
            span = pl.ds(pl.multiple_of(d * tile, tile), tile)
            mixed[:, span] = nn(acts[chunk_rows(k), :], down[:, span]).astype(BF16)

        put_mixed(k).start()

    for f in range(per):
        for load in weights[f]:
            load.wait()
        if f == 0:
            cot_load.wait()
        first_half(rows_of(me), f)
    second_half(rows_of(me))

    for k in range(1, n):
        mix(k - 1)
        for way in range(2):
            j = me - k if way == 0 else me + k
            there = (me >= k) if way == 0 else (me + k <= n - 1)

            @pl.when(there)
            def _(way=way, j=j):
                gather_arrival(way, j).wait()

                @pl.when(ends[way])
                def _():
                    gather(way, j).start()

        rows = chunk_rows(k)

        @pl.loop(0, per)
        def _(f):
            first_half(rows, f)

        second_half(rows)
        for way in range(2):

            @pl.when(place[way] == 0)
            def _(way=way):
                j = me + k if way == 0 else me - k
                for q in range(cut):
                    pass_on(way, j, q).start()

    room = 3 * block
    half = dp // 4
    items = dp // 2 * 2 * per

    def staged(pair, j, start=0, size=room):
        first = pl.multiple_of((lax.rem(pair, 2) * 2 + j) * room + start, 16)
        return gate_up.at[pl.ds(first, size)]

    def put_across(pair, j):
        return pltpu.make_async_remote_copy(
            src_ref=staged(pair, j), dst_ref=came.at[2 * pair + j],
            send_sem=core_send.at[pair, j], recv_sem=core_recv.at[pair, j],
            device_id=mate, device_id_type=pl.DeviceIdType.MESH)

    def fill(pair, j):
        return pltpu.make_async_copy(came.at[2 * (pair - half) + j], staged(pair, j), fill_sems.at[j])

    def put_own(pair, j, act):
        q = 2 * (pair - half) + j
        quarter = dp // 4
        rows = room // 2
        place = lax.div(mine, 2)
        for part, (other, keep, slot, goes) in enumerate((
            (first_send, first_keep, lax.div(q, 2), lax.rem(q, 2) != lax.rem(place, 2)),
            (second_send, second_keep, lax.rem(q, quarter), lax.div(q, quarter) != lax.div(place, quarter)),
        )):
            for ref, chosen in ((other, goes), (keep, jnp.logical_not(goes))):

                @pl.when(chosen)
                def _(ref=ref, part=part, slot=slot):
                    copy = pltpu.make_async_copy(
                        staged(pair, j, part * rows, rows), ref.at[slot], out_sems.at[lax.rem(pair, 2), j, part])
                    if act == "start":
                        copy.start()
                    else:
                        copy.wait()

    def weight_item(i):
        pair, f = lax.div(i, 2 * per), lax.rem(i, 2 * per)
        slot = lax.rem(pair, 2)
        other = lax.div(pair, half)

        def turn(source):
            for j in range(2):
                column = 2 * (2 * lax.rem(pair, half) + j) + lax.rem(core + 1 + other, 2)
                span = pl.ds(pl.multiple_of(column * block, block), block)
                turned[pl.ds(j * block, block), :] = source[:, span].T

        def store(row, goal, product):
            for j in range(2):
                start = pl.multiple_of((slot * 2 + j) * room + row * block, 16)
                rows = pl.ds(start, block)
                part = product[j * block:(j + 1) * block]

                @pl.when(pair < half)
                def _(rows=rows, part=part):
                    gate_up[rows, goal] = part.astype(BF16)

                @pl.when(pair >= half)
                def _(rows=rows, part=part):
                    gate_up[rows, goal] = (gate_up[rows, goal].astype(F32) + part).astype(BF16)

        @pl.when(f == 0)
        def _():
            @pl.when((pair >= 2) & (pair < half))
            def _():
                for j in range(2):
                    put_across(pair - 2, j).wait_send()

            @pl.when(pair >= half)
            def _():
                for j in range(2):
                    fill(pair, j).wait()

            turn(normed)

        @pl.when(f == per)
        def _():
            turn(cots)
            following = pair + 1

            @pl.when((following >= half) & (following < 2 * half))
            def _():
                @pl.when(following - 2 < half)
                def _():
                    for j in range(2):
                        put_across(following - 2, j).wait_send()

                @pl.when(following - 2 >= half)
                def _():
                    for j in range(2):
                        put_own(following - 2, j, "wait")

                for j in range(2):
                    put_across(following - half, j).wait_recv()
                    fill(following, j).start()

        @pl.when(f < per)
        def _():
            goal = pl.ds(pl.multiple_of(f * tile, tile), tile)
            for row in range(2):
                span = pl.ds(pl.multiple_of(row * hidden + f * tile, tile), tile)
                store(row, goal, nn(turned[...], grads[:, span]))

        @pl.when(f >= per)
        def _():
            goal = pl.ds(pl.multiple_of((f - per) * tile, tile), tile)
            store(2, goal, nn(turned[...], acts[:, goal]))

        @pl.when(f == 2 * per - 1)
        def _():
            @pl.when(pair < half)
            def _():
                for j in range(2):
                    put_across(pair, j).start()

            @pl.when(pair >= half)
            def _():
                for j in range(2):
                    put_own(pair, j, "start")

    first_step, last_step = cut + 1, cut * (n - 1) + n - 2
    every = -(-items // (last_step - first_step))

    def serve(step):
        for way in range(2):
            count = step - place[way]
            j_place = lax.div(count, cut) + 1
            q = lax.rem(count, cut)
            j = j_place if way == 0 else n - 1 - j_place

            @pl.when((place[way] > 0) & (j_place > place[way]) & (j_place < n))
            def _(way=way, j=j, q=q):
                sum_arrival(way, j, q, j).wait()
                rows = pl.ds(pl.multiple_of(j * share + q * piece, 16), piece)
                sending[rows, :] = (sending[rows, :].astype(F32) + arriving[rows, :].astype(F32)).astype(BF16)
                pass_on(way, j, q).start()

    @pl.loop(first_step, last_step)
    def _(step):
        serve(step)
        for j in range(every):
            item = (step - first_step) * every + j

            @pl.when(item < items)
            def _(item=item):
                weight_item(item)


    mix(n - 1)

    for way in range(2):

        @pl.when(place[way] > 0)
        def _(way=way):
            for q in range(cut):
                slot = n if way else me
                sum_arrival(way, me, q, slot).wait()
            slot = pl.ds(n * share, share) if way else rows_of(me)

            @pl.loop(0, width // tile)
            def _(d):
                span = pl.ds(pl.multiple_of(d * tile, tile), tile)
                sending[rows_of(me), span] = (
                    sending[rows_of(me), span].astype(F32) + arriving[slot, span].astype(F32)
                ).astype(BF16)

    final = pltpu.make_async_copy(sending.at[rows_of(me)], sum_out, load_sems.at[0])
    final.start()
    for pair in (2 * half - 2, 2 * half - 1):
        for j in range(2):
            put_own(pair, j, "wait")
    put_mixed(n - 1).wait()
    final.wait()
    for way in range(2):

        @pl.when(ends[way])
        def _(way=way):
            @pl.loop(0, n)
            def _(j):
                sent = (j <= me) if way == 0 else (j >= me)

                @pl.when(sent)
                def _():
                    gather(way, j).wait_send()

                @pl.when(jnp.logical_not(sent))
                def _():
                    for q in range(cut):
                        pass_on(way, j, q).wait_send()


def feed_forward(normed, cotangent, gate_up, down, n, dp, tile=512, cut=4):
    share, width = normed.shape
    hidden = down.shape[0]
    tokens = n * share
    block = width // dp
    anywhere = pl.BlockSpec(memory_space=pl.ANY)
    return pl.pallas_call(
        partial(feed_kernel, n, dp, tile, cut),
        out_shape=(
            jax.ShapeDtypeStruct((share, width), BF16),
            jax.ShapeDtypeStruct((tokens, width), BF16),
            jax.ShapeDtypeStruct((dp // 2, 3 * block, hidden), BF16),
            jax.ShapeDtypeStruct((dp // 4, 3 * block // 2, hidden), BF16),
            jax.ShapeDtypeStruct((dp // 4, 3 * block // 2, hidden), BF16),
            jax.ShapeDtypeStruct((dp // 4, 3 * block // 2, hidden), BF16),
            jax.ShapeDtypeStruct((dp // 4, 3 * block // 2, hidden), BF16),
        ),
        in_specs=[anywhere] * 4,
        out_specs=(anywhere,) * 7,
        scratch_shapes=[
            pltpu.VMEM((2 * width, hidden), BF16),
            pltpu.VMEM((hidden, width), BF16),
            pltpu.VMEM((tokens, width), BF16),
            pltpu.VMEM((tokens, width), BF16),
            pltpu.VMEM((tokens, hidden), BF16),
            pltpu.VMEM((tokens, 2 * hidden), BF16),
            pltpu.VMEM((tokens + share, width), BF16),
            pltpu.VMEM((tokens, width), BF16),
            pltpu.VMEM((share, width), BF16),
            pltpu.VMEM((2 * block, tokens), BF16),
            pltpu.SemaphoreType.DMA((2,)),
            pltpu.SemaphoreType.DMA((3, hidden // tile)),
            pltpu.SemaphoreType.DMA((2, 2, 2)),
            pltpu.SemaphoreType.DMA((dp // 4, 2)),
            pltpu.SemaphoreType.DMA((dp // 4, 2)),
            pltpu.SemaphoreType.DMA((2,)),
            pltpu.SemaphoreType.DMA((2, n)),
            pltpu.SemaphoreType.DMA((2, n)),
            pltpu.SemaphoreType.DMA((2, n * cut)),
            pltpu.SemaphoreType.DMA((2, n * cut)),
            pltpu.SemaphoreType.DMA,
        ],
        compiler_params=pltpu.CompilerParams(
            collective_id=0, has_side_effects=True, vmem_limit_bytes=60 * 2**20),
        cost_estimate=pl.CostEstimate(
            flops=18 * tokens * width * hidden, bytes_accessed=2 * 24 * 2**20, transcendentals=tokens * hidden),
        name="feed_forward",
    )(normed, cotangent, gate_up, down)


def tail_kernel(
    n, dp, tile, cut,
    joined_in, w_in, normed_in, att_in, att_mate_in, grad_in, grad_mate_in, fa_keep, fa_came, fb_keep, fb_came, small_in,
    sum_out, feed_a, feed_b, branch_out, qkv_a, qkv_b, small_out, own_out,
    joined, w, normed, att, att_mate, grad, grad_mate, arriving, sending,
    fa, fa2, fb, fb2, small, small_recvs, small_came, small_total, f_recvs, wm, w_recvs, w_done, w_last, qo, qm, qc, q_recvs,
    load_sems, out_sems, sum_send, sum_recv, f_sems, w_sems, q_sems, core_sems, last_send, last_recv, small_sems, few_send, few_recv,
):
    width = w.shape[1]
    joined_width, tokens = joined.shape
    share = tokens // n
    block = width // dp
    piece = share // cut
    columns = att.shape[0]
    me = lax.axis_index("tensor")
    mine = lax.axis_index("dp")
    core = lax.rem(mine, 2)
    bits = dp.bit_length() - 1
    mesh_id = pl.DeviceIdType.MESH
    place = (me, n - 1 - me)
    ends = (me < n - 1, me > 0)
    partner = (me + 1, me - 1)

    def own_bit(bit):
        return lax.rem(lax.div(mine, 1 << bit), 2)

    def mate(bit):
        return {"dp": mine + (1 << bit) * (1 - 2 * own_bit(bit))}

    barrier = pltpu.get_barrier_semaphore()
    for s in range(1, n):
        pl.semaphore_signal(barrier, inc=1, device_id={"tensor": lax.rem(me + s, n)}, device_id_type=mesh_id)
    for bit in range(bits):
        pl.semaphore_signal(barrier, inc=1, device_id=mate(bit), device_id_type=mesh_id)

    pairs = (
        (small_in, small), (joined_in, joined), (w_in, w), (att_in, att), (att_mate_in, att_mate), (grad_in, grad),
        (grad_mate_in, grad_mate), (normed_in, normed), (fa_keep, fa), (fa_came, fa2), (fb_keep, fb), (fb_came, fb2),
    )
    loads = [pltpu.make_async_copy(a, b, load_sems.at[i]) for i, (a, b) in enumerate(pairs)]
    for load in loads:
        load.start()
    pl.semaphore_wait(barrier, n - 1 + bits)

    def rows_of(j):
        return pl.ds(pl.multiple_of(j * share, 16), share)

    def pass_on(way, j, q):
        rows = pl.ds(pl.multiple_of(j * share + q * piece, 16), piece)
        last = j == partner[way]
        slot = jnp.where(last, n, j) if way else j
        goal = pl.ds(pl.multiple_of(slot * share + q * piece, 16), piece)
        return pltpu.make_async_remote_copy(
            src_ref=sending.at[rows], dst_ref=arriving.at[goal],
            send_sem=sum_send.at[way, j * cut + q], recv_sem=sum_recv.at[way, j * cut + q],
            device_id={"tensor": partner[way]}, device_id_type=mesh_id)

    def sum_arrival(way, j, q, slot):
        rows = pl.ds(pl.multiple_of(slot * share + q * piece, 16), piece)
        return pltpu.make_async_copy(arriving.at[rows], arriving.at[rows], sum_recv.at[way, j * cut + q])

    def halving(cur, recvs, sems, stream, order):
        steps = []
        current = cur
        for step, bit in enumerate(order):
            count = 1 << (len(order) - step - 1)
            own = own_bit(bit)

            def index(slot, which, count=count):
                return 2 * slot + which if stream == 0 else which * count + slot

            room = recvs[stream][step]
            copies = [
                pltpu.make_async_remote_copy(
                    src_ref=current(index(slot, 1 - own)), dst_ref=room.at[slot],
                    send_sem=sems.at[0, stream, step, slot], recv_sem=sems.at[1, stream, step, slot],
                    device_id=mate(bit), device_id_type=mesh_id)
                for slot in range(count)
            ]

            def start(copies=copies):
                for copy in copies:
                    copy.start()

            def finish(copies=copies, current=current, room=room, count=count, own=own, index=index):
                for slot, copy in enumerate(copies):
                    copy.wait_recv()
                    kept = current(index(slot, own))
                    total = kept.shape[0]
                    rows = 128 if total % 128 == 0 else 64 if total % 64 == 0 else total

                    @pl.loop(0, total // rows)
                    def _(r):
                        span = pl.ds(pl.multiple_of(r * rows, 16), rows)
                        room[slot, span, :] = (kept[span, :].astype(F32) + room[slot, span, :].astype(F32)).astype(room.dtype)

            def settle(copies=copies):
                for copy in copies:
                    copy.wait_send()

            steps.append((start, finish, settle))
            current = lambda i, room=room: room.at[i]
        return steps

    loads[0].wait()
    small_steps = halving(lambda i: small.at[i], [None, small_recvs], small_sems, 1, list(range(bits))[::-1])
    small_steps[0][0]()
    loads[1].wait()
    loads[2].wait()
    for k in range(n):
        distance = n - 1 - k
        for way in range(2):
            j = me + distance if way == 0 else me - distance
            there = (j < n) if way == 0 else (j >= 0)
            if distance == 0 and way:
                continue

            @pl.when(there)
            def _(j=j, way=way, distance=distance):
                rows = rows_of(j)

                @pl.loop(0, width // tile)
                def _(d):
                    span = pl.ds(pl.multiple_of(d * tile, tile), tile)
                    sending[rows, span] = lax.dot_general(
                        joined[:, pl.ds(pl.multiple_of(j * share, 128), share)], w[:, span],
                        (((0,), (0,)), ((), ())), preferred_element_type=F32).astype(BF16)

                if distance:

                    @pl.when(place[way] == 0)
                    def _():
                        for q in range(cut):
                            pass_on(way, j, q).start()

    rest = list(range(1, bits))
    half_rows = block // 2
    w_steps = [
        halving(lambda i, s=s: wm.at[i, pl.ds(s * half_rows, half_rows)], w_recvs, w_sems, s, order)
        for s, order in enumerate((rest, rest[::-1]))
    ]
    q_steps = [
        halving(lambda i, s=s: qm.at[i, pl.ds(s * half_rows, half_rows)], q_recvs, q_sems, s, order)
        for s, order in enumerate((rest, rest[::-1]))
    ]
    f_steps = [
        halving(lambda i, ref=ref: ref.at[i], f_recvs, f_sems, s, order[1:])
        for s, (ref, order) in enumerate(((fa, rest), (fb, rest[::-1])))
    ]

    def next_small(step):
        small_steps[step][1]()
        if step + 1 < bits:
            small_steps[step + 1][0]()

    next_small(0)
    for load in loads[3:7]:
        load.wait()

    @pl.loop(0, dp // 2)
    def _(q):
        span = pl.ds(pl.multiple_of(q * block, block), block)
        turned, turned_mate = grad[:, span].T, grad_mate[:, span].T
        for c in range(0, columns, tile):
            wm[q, :, c:c + tile] = (nt(turned, att[c:c + tile, :]) + nt(turned_mate, att_mate[c:c + tile, :])).astype(BF16)

    for s in range(2):
        w_steps[s][0][0]()

    loads[7].wait()

    def across(q):
        return pltpu.make_async_remote_copy(
            src_ref=qo.at[q], dst_ref=qc.at[q], send_sem=core_sems.at[0, q], recv_sem=core_sems.at[1, q],
            device_id=mate(0), device_id_type=mesh_id)

    def projection(q, which):
        column = 2 * q + which
        span = pl.ds(pl.multiple_of(column * block, block), block)
        return nt(normed[:, span].T, joined[...])

    @pl.loop(0, dp // 2)
    def _(q):
        qo[q] = projection(q, 1 - core).astype(BF16)
        across(q).start()

    @pl.loop(0, dp // 2)
    def _(q):
        product = projection(q, core)
        across(q).wait_recv()
        qm[q] = (product + qc[q].astype(F32)).astype(BF16)

    for s in range(2):
        q_steps[s][0][0]()

    for step in range(1, bits):
        next_small(step)
    for load in loads[8:]:
        load.wait()
    for one, other in ((fa, fa2), (fb, fb2)):
        for i in range(dp // 4):
            rows = 64 if one.shape[1] % 64 == 0 else one.shape[1]

            @pl.loop(0, one.shape[1] // rows)
            def _(r, one=one, other=other, i=i):
                span = pl.ds(pl.multiple_of(r * rows, 16), rows)
                one[i, span, :] = (one[i, span, :].astype(F32) + other[i, span, :].astype(F32)).astype(BF16)

    def serve(step):
        for way in range(2):
            count = step - place[way]
            reach = lax.div(count, cut)
            j_place = n - 1 - reach
            q = lax.rem(count, cut)
            j = j_place if way == 0 else n - 1 - j_place

            @pl.when((place[way] > 0) & (count >= 0) & (j_place > place[way]))
            def _(way=way, j=j, q=q):
                sum_arrival(way, j, q, j).wait()
                rows = pl.ds(pl.multiple_of(j * share + q * piece, 16), piece)
                sending[rows, :] = (sending[rows, :].astype(F32) + arriving[rows, :].astype(F32)).astype(BF16)
                pass_on(way, j, q).start()

    few = small_total.shape[0]

    def deliver_small(s):
        goal = lax.rem(me + s, n)
        return pltpu.make_async_remote_copy(
            src_ref=small_recvs[bits - 1].at[0, pl.ds(pl.multiple_of(goal * few, 8), few)],
            dst_ref=small_came.at[s - 1], send_sem=few_send.at[s - 1], recv_sem=few_recv.at[s - 1],
            device_id={"tensor": goal}, device_id_type=mesh_id)

    for s in range(1, n):
        deliver_small(s).start()
    own_copy = pltpu.make_async_copy(
        small_recvs[bits - 1].at[0, pl.ds(n * few, own_out.shape[0])], own_out, out_sems.at[6])
    own_copy.start()
    last_step = cut * (n - 2) + n - 1
    first = 1 + cut
    pl.loop(1, first)(serve)
    for step in range(len(rest)):
        for s in range(2):
            w_steps[s][step][1]()
            if step + 1 < len(rest):
                w_steps[s][step + 1][0]()
            q_steps[s][step][1]()
            if step + 1 < len(rest):
                q_steps[s][step + 1][0]()
        if step == 0:
            for s in range(2):
                f_steps[s][0][0]()
        begin = first + step * 2
        end = min(begin + 2, last_step) if step + 1 < len(rest) else last_step
        if step + 1 < len(rest):
            pl.loop(begin, end)(serve)

    own_columns = columns // n
    for s in range(2):
        w_done[pl.ds(s * half_rows, half_rows), :] = w_recvs[s][len(rest) - 1][0]

    def deliver(s):
        goal = lax.rem(me + s, n)
        return pltpu.make_async_remote_copy(
            src_ref=w_done.at[:, pl.ds(pl.multiple_of(goal * own_columns, 128), own_columns)],
            dst_ref=w_last.at[s - 1], send_sem=last_send.at[s - 1], recv_sem=last_recv.at[s - 1],
            device_id={"tensor": goal}, device_id_type=mesh_id)

    for s in range(1, n):
        deliver(s).start()
    q_outs = [
        pltpu.make_async_copy(q_recvs[s][len(rest) - 1].at[0], (qkv_a, qkv_b)[s], out_sems.at[s]) for s in range(2)
    ]
    for copy in q_outs:
        copy.start()
    pl.loop(first + 2 * (len(rest) - 1), last_step)(serve)

    for step in range(len(rest) - 1):
        for s in range(2):
            f_steps[s][step][1]()
            if step + 1 < len(rest) - 1:
                f_steps[s][step + 1][0]()
    f_outs = [
        pltpu.make_async_copy(f_recvs[s][len(rest) - 2].at[0], (feed_a, feed_b)[s], out_sems.at[2 + s]) for s in range(2)
    ]
    for copy in f_outs:
        copy.start()

    mine_columns = pl.ds(pl.multiple_of(me * own_columns, 128), own_columns)
    total = w_done[:, mine_columns].astype(F32)
    for s in range(1, n):
        deliver(s).wait_recv()
        total = total + w_last[s - 1].astype(F32)
    w_last[n - 1] = total.astype(BF16)
    branch = pltpu.make_async_copy(w_last.at[n - 1], branch_out, out_sems.at[4])
    branch.start()

    total = small_recvs[bits - 1][0, pl.ds(pl.multiple_of(me * few, 8), few), :]
    for s in range(1, n):
        deliver_small(s).wait_recv()
        total = total + small_came[s - 1]
    small_total[...] = total
    few_copy = pltpu.make_async_copy(small_total, small_out, out_sems.at[7])
    few_copy.start()

    for way in range(2):

        @pl.when(place[way] > 0)
        def _(way=way):
            for q in range(cut):
                slot = n if way else me
                sum_arrival(way, me, q, slot).wait()
            slot = pl.ds(n * share, share) if way else rows_of(me)

            @pl.loop(0, width // tile)
            def _(d):
                span = pl.ds(pl.multiple_of(d * tile, tile), tile)
                sending[rows_of(me), span] = (
                    sending[rows_of(me), span].astype(F32) + arriving[slot, span].astype(F32)
                ).astype(BF16)

    final = pltpu.make_async_copy(sending.at[rows_of(me)], sum_out, out_sems.at[5])
    final.start()
    for copy in (*q_outs, *f_outs, branch, final, own_copy, few_copy):
        copy.wait()
    for steps in (*w_steps, *q_steps, *f_steps, small_steps):
        for _, _, settle in steps:
            settle()
    for s in range(1, n):
        deliver(s).wait_send()
        deliver_small(s).wait_send()

    @pl.loop(0, dp // 2)
    def _(q):
        across(q).wait_send()

    for way in range(2):

        @pl.when(ends[way])
        def _(way=way):
            @pl.loop(0, n)
            def _(j):
                sent = (j > me) if way == 0 else (j < me)

                @pl.when(sent)
                def _():
                    for q in range(cut):
                        pass_on(way, j, q).wait_send()


def tail(joined, w, normed, att, att_mate, grad, grad_mate, feed, small, few, n, dp, tile=512, cut=4):
    joined_width, tokens = joined.shape
    width = w.shape[1]
    share = tokens // n
    block = width // dp
    columns = att.shape[0]
    steps = dp.bit_length() - 2
    feed_rows, hidden = feed[0].shape[1:]
    anywhere = pl.BlockSpec(memory_space=pl.ANY)
    half = block // 2

    def rooms(rows, cols, count):
        return [[pltpu.VMEM((1 << (count - step - 1), rows, cols), BF16) for step in range(count)] for _ in range(2)]

    def like(array):
        return pltpu.VMEM(array.shape, BF16)

    return pl.pallas_call(
        partial(tail_kernel, n, dp, tile, cut),
        out_shape=(
            jax.ShapeDtypeStruct((share, width), BF16),
            jax.ShapeDtypeStruct((feed_rows, hidden), BF16),
            jax.ShapeDtypeStruct((feed_rows, hidden), BF16),
            jax.ShapeDtypeStruct((block, columns // n), BF16),
            jax.ShapeDtypeStruct((half, joined_width), BF16),
            jax.ShapeDtypeStruct((half, joined_width), BF16),
            jax.ShapeDtypeStruct((few, small.shape[2]), F32),
            jax.ShapeDtypeStruct((small.shape[1] - n * few, small.shape[2]), F32),
        ),
        in_specs=[anywhere] * 12,
        out_specs=(anywhere,) * 8,
        scratch_shapes=[
            like(joined), like(w), like(normed), like(att), like(att_mate), like(grad), like(grad_mate),
            pltpu.VMEM((tokens + share, width), BF16),
            pltpu.VMEM((tokens, width), BF16),
            like(feed[0]), like(feed[1]), like(feed[2]), like(feed[3]),
            pltpu.VMEM(small.shape, F32),
            [pltpu.VMEM((1 << (steps - step),) + small.shape[1:], F32) for step in range(steps + 1)],
            pltpu.VMEM((n - 1, few, small.shape[2]), F32),
            pltpu.VMEM((few, small.shape[2]), F32),
            rooms(feed_rows, hidden, steps - 1),
            pltpu.VMEM((dp // 2, block, columns), BF16),
            rooms(half, columns, steps),
            pltpu.VMEM((block, columns), BF16),
            pltpu.VMEM((n, block, columns // n), BF16),
            pltpu.VMEM((dp // 2, block, joined_width), BF16),
            pltpu.VMEM((dp // 2, block, joined_width), BF16),
            pltpu.VMEM((dp // 2, block, joined_width), BF16),
            rooms(half, joined_width, steps),
            pltpu.SemaphoreType.DMA((12,)),
            pltpu.SemaphoreType.DMA((8,)),
            pltpu.SemaphoreType.DMA((2, n * cut)),
            pltpu.SemaphoreType.DMA((2, n * cut)),
            pltpu.SemaphoreType.DMA((2, 2, steps, dp // 4)),
            pltpu.SemaphoreType.DMA((2, 2, steps, dp // 4)),
            pltpu.SemaphoreType.DMA((2, 2, steps, dp // 4)),
            pltpu.SemaphoreType.DMA((2, dp // 2)),
            pltpu.SemaphoreType.DMA((n - 1,)),
            pltpu.SemaphoreType.DMA((n - 1,)),
            pltpu.SemaphoreType.DMA((2, 2, steps + 1, dp // 2)),
            pltpu.SemaphoreType.DMA((n - 1,)),
            pltpu.SemaphoreType.DMA((n - 1,)),
        ],
        compiler_params=pltpu.CompilerParams(
            collective_id=1, has_side_effects=True, vmem_limit_bytes=60 * 2**20),
        cost_estimate=pl.CostEstimate(flops=10**6, bytes_accessed=10**5, transcendentals=0),
        name="gradient_sums",
    )(joined, w, normed, att, att_mate, grad, grad_mate, *feed, small)


def ring(size, shift=1):
    return [(i, (i + shift) % size) for i in range(size)]


def flip(size, bit):
    return [(i, i ^ (1 << bit)) for i in range(size)]


def pick(array, index, axis):
    return lax.dynamic_index_in_dim(array, index, axis, keepdims=False)


def chunk_of(array, index, rows, axis):
    return lax.dynamic_slice_in_dim(array, index * rows, rows, axis)


def bits_of(size):
    return size.bit_length() - 1


def gather_weight(shard):
    piece = chunk_of(shard, lax.axis_index("dp"), shard.shape[0] // lax.axis_size("dp"), 0)
    whole = lax.all_gather(piece, ("tensor", "dp"), axis=0, tiled=True)
    return whole.reshape((lax.axis_size("tensor"),) + shard.shape)


def exchange(parts, shift):
    n = lax.axis_size("tensor")
    me = lax.axis_index("tensor")
    came = [parts(me)]
    for s in range(1, n):
        came.append(lax.ppermute(parts((me + s) % n), "tensor", ring(n, s)))
    return came


def by_place(came):
    n = len(came)
    me = lax.axis_index("tensor")
    stacked = jnp.stack(came)
    return [pick(stacked, (me + n - j) % n, 0) for j in range(n)]


def local(
    tokens,
    cotangent,
    segments,
    norm_gains,
    w_qkv,
    qkv_down,
    query_key_value_up,
    feature_maps,
    w_out,
    o_down,
    o_up,
    w_gate_up,
    w_down,
):
    token_rows, model_width = tokens.shape
    groups = w_qkv.shape[1]
    heads = HEADS // KVH
    query_width = heads * HEAD_SIZE
    joined_width = w_qkv.shape[2]
    rank = o_up.shape[0]
    dp = lax.axis_size("dp")
    n = lax.axis_size("tensor")
    me = lax.axis_index("tensor")
    share = token_rows // n
    gains = norm_gains.astype(F32)
    cosines, sines = rotary_tables_t(token_rows, HEAD_SIZE)
    dot = partial(jnp.einsum, preferred_element_type=F32)

    up = query_key_value_up.astype(BF16)
    edges = ((0, query_width), (query_width, query_width + HEAD_SIZE), (query_width + HEAD_SIZE, joined_width))
    up_wide = jnp.stack(
        [jnp.pad(up[:, :, a:b], ((0, 0), (0, 0), (a, joined_width - b))) for a, b in edges]
    )
    w_joined = (
        jnp.transpose(w_qkv, (1, 2, 0)).astype(F32) + dot("jrkc,jrd->kcd", up_wide, qkv_down)
    ).astype(BF16).reshape(groups * joined_width, model_width)
    down_flat = o_down.reshape(rank, -1)
    w_branch = (w_out.astype(F32) + dot("rc,rd->cd", down_flat, o_up)).astype(BF16)
    down_all = lax.all_gather(down_flat, "tensor")
    all_branch = gather_weight(w_branch)

    _, _, normed_one = normalize(tokens.astype(F32), gains[0])
    lowrank = dot("td,jrd->tjr", normed_one, qkv_down)
    joined = dot("cd,td->ct", w_joined, normed_one).reshape(groups, joined_width, token_rows)
    maps_t = jnp.swapaxes(feature_maps, 1, 2)
    maps = jnp.stack(
        [feature_maps[:, :, i * HEAD_SIZE:(i + 1) * HEAD_SIZE] for i in range(heads + 1)], axis=1
    )
    seg_row = segments.reshape(1, token_rows)
    seg_col = segments.reshape(token_rows, 1)
    low, attended, root = attention_forward(joined, cosines, sines, maps_t, seg_row, seg_col, heads)
    attended_flat = attended.reshape(groups * query_width, token_rows)
    att_came = exchange(lambda j: chunk_of(attended_flat, j, share, 1), 1)
    att_share = jnp.stack(by_place(att_came))
    lowrank_out = dot("nct,nrc->tr", att_share, down_all)
    tokens_share = chunk_of(tokens, me, share, 0).astype(F32)
    hidden = tokens_share + dot("nct,ncd->td", att_share, all_branch)
    scaled_two, inverse_two, normed_two = normalize(hidden, gains[1])

    grad_normed_two, mixed_parts, _, *grads_feed = feed_forward(
        normed_two, cotangent, jnp.transpose(w_gate_up, (1, 0, 2)), w_down, n, dp
    )
    grad_normed_two = grad_normed_two.astype(F32)
    weighted = grad_normed_two * gains[1]
    grad_hidden = chunk_of(cotangent, me, share, 0).astype(F32) + inverse_two * (
        weighted - scaled_two * jnp.mean(weighted * scaled_two, axis=-1, keepdims=True)
    )
    gain_two = jnp.sum(grad_normed_two * scaled_two, axis=0)
    grad_branch = grad_hidden.astype(BF16)

    grad_att_share = dot("ncd,td->nct", all_branch, grad_branch).astype(BF16)
    back = by_place(exchange(lambda j: pick(grad_att_share, j, 0), 1))
    grad_attended = jnp.concatenate(back, axis=1).reshape(groups, query_width, token_rows)
    mixed_parts, grad_attended = lax.optimization_barrier((mixed_parts, grad_attended))
    mixed_came = exchange(lambda j: chunk_of(mixed_parts, j, share, 0), 1)

    grad_joined, grad_maps = attention_backward(
        low, cosines, sines, maps_t, maps, seg_row, seg_col, attended, root, grad_attended, heads
    )
    flat_joined = grad_joined.reshape(groups * joined_width, token_rows)
    near = [part for s, part in enumerate(mixed_came) if s != n // 2]
    flat_joined, near = lax.optimization_barrier((flat_joined, near))
    mixed = sum(part.astype(F32) for part in (*near, mixed_came[n // 2]))
    lowrank_low = lowrank.astype(BF16)
    grad_up = jnp.concatenate(
        [dot("tr,kct->rkc", lowrank_low[:, j], grad_joined[:, a:b]) for j, (a, b) in enumerate(edges)],
        axis=2,
    )
    grad_maps = jnp.transpose(grad_maps, (0, 2, 1, 3)).reshape(groups, HEAD_SIZE, -1)
    small = jnp.concatenate(
        [
            jnp.moveaxis(grad_up.reshape(rank, groups, dp, -1), 2, 0).reshape(dp, -1),
            jnp.moveaxis(grad_maps.reshape(groups, HEAD_SIZE, dp, -1), 2, 0).reshape(dp, -1),
        ],
        axis=1,
    )
    grad_lowrank = dot("kct,jrkc->jrt", grad_joined, up_wide).astype(BF16)
    grad_qkv_down = dot("jrt,td->jrd", grad_lowrank, normed_one)
    grad_lowrank_out = dot("td,rd->tr", grad_branch, o_up).astype(BF16)
    grad_o_up = dot("tr,td->rd", lowrank_out.astype(BF16), grad_branch)
    grad_o_down = dot("tr,nct->nrc", grad_lowrank_out, att_share)
    gain_one = jnp.sum(dot("ct,cd->td", flat_joined, w_joined) * normed_one.astype(F32), axis=0)
    shared = jnp.concatenate(
        [gain_one[None] / gains[:1], gain_two[None], grad_qkv_down.reshape(-1, model_width), grad_o_up], axis=0
    )
    lines = shared.shape[0]
    shared = jnp.transpose(shared.reshape(lines, dp, n, -1), (1, 2, 0, 3)).reshape(dp, n, -1)
    downs = grad_o_down.reshape(n, rank, groups, dp, -1)
    downs = jnp.transpose(downs, (3, 0, 1, 2, 4)).reshape(dp, n, -1)
    packed = jnp.concatenate([shared, downs], axis=2)
    few = -(-packed.shape[2] // 1024) * 8
    packed = jnp.pad(packed, ((0, 0), (0, 0), (0, few * 128 - packed.shape[2]))).reshape(dp, n * few, 128)
    tall = -(-small.shape[1] // 1024) * 8
    small = jnp.pad(small, ((0, 0), (0, tall * 128 - small.shape[1]))).reshape(dp, tall, 128)
    packed = jnp.concatenate([packed, small], axis=1)
    width = model_width // dp
    core = lax.axis_index("dp") & 1

    def of_core(array, which):
        return jnp.concatenate([chunk_of(array, 2 * q + which, width, 1) for q in range(dp // 2)], axis=1)

    flat_att = att_share.reshape(-1, share)
    att_mate = lax.ppermute(flat_att, "dp", flip(dp, 0))
    branch_own = of_core(grad_branch, core)
    branch_mate = lax.ppermute(of_core(grad_branch, 1 - core), "dp", flip(dp, 0))
    first_send, first_keep, second_send, second_keep = grads_feed
    rest = list(range(1, bits_of(dp)))
    grad_normed_one, feed_a, feed_b, out_branch, qkv_a, qkv_b, few_small, own_small = tail(
        flat_joined, w_joined, normed_one, flat_att, att_mate, branch_own, branch_mate,
        (
            first_keep, lax.ppermute(first_send, "dp", flip(dp, rest[0])),
            second_keep, lax.ppermute(second_send, "dp", flip(dp, rest[-1])),
        ),
        packed, few, n, dp,
    )
    own_small = own_small.reshape(-1)
    cut = rank * groups * (joined_width // dp)
    out_up = own_small[:cut].reshape(rank, groups, -1)
    out_maps = own_small[cut:cut + groups * HEAD_SIZE * (feature_maps.shape[2] // dp)].reshape(groups, HEAD_SIZE, -1)
    few_small = few_small.reshape(-1)
    cut = lines * (model_width // (dp * n))
    shared = few_small[:cut].reshape(lines, -1)
    out_o_down = few_small[cut:cut + rank * groups * (query_width // dp)].reshape(rank, groups, -1)
    grad_normed_one = grad_normed_one.astype(F32)
    output = (hidden + mixed).astype(BF16)
    scaled_one, inverse_one, _ = normalize(tokens_share, gains[0])
    weighted = grad_normed_one * gains[0]
    grad_input = (
        grad_hidden
        + inverse_one
        * (weighted - scaled_one * jnp.mean(weighted * scaled_one, axis=-1, keepdims=True))
    ).astype(BF16)
    over = feed_a.shape[0] - width
    out_up_rows = jnp.concatenate([feed_a[width:], feed_b[:width - over]], axis=0)
    out_gate_up = jnp.stack([feed_a[:width], out_up_rows], axis=1).astype(F32)
    out_down = feed_b[width - over:].T.astype(F32)
    out_branch = out_branch.T.astype(F32)
    out_qkv = jnp.concatenate([qkv_a, qkv_b], axis=0).astype(F32).reshape(width, groups, joined_width)

    return (
        output,
        grad_input,
        shared[:2],
        out_qkv,
        shared[2:lines - rank].reshape(3, rank, -1),
        out_up,
        out_maps,
        out_branch,
        out_o_down,
        shared[lines - rank:],
        out_gate_up,
        out_down,
    )


def solution(mesh):
    in_specs = (
        P("dp", None),
        P("dp", None),
        P("dp", None),
        P(),
        P(None, "tensor", None),
        P(),
        P(None, "tensor", None),
        P("tensor", None, None),
        P("tensor", None),
        P(None, "tensor", None),
        P(),
        P(None, None, "tensor"),
        P("tensor", None),
    )
    out_specs = (
        P(("dp", "tensor"), None),
        P(("dp", "tensor"), None),
        P(None, ("dp", "tensor")),
        P("dp", "tensor", None),
        P(None, None, ("dp", "tensor")),
        P(None, "tensor", "dp"),
        P("tensor", None, "dp"),
        P("tensor", "dp"),
        P(None, "tensor", "dp"),
        P(None, ("dp", "tensor")),
        P("dp", None, "tensor"),
        P("tensor", "dp"),
    )
    return jax.shard_map(
        local, mesh=mesh, in_specs=in_specs, out_specs=out_specs, check_vma=False
    )
```
